32 devices in a mesh: dp: 2 (over x), seq: 4 (over y, core), mp: 4 (over z).
Axes of the slice: x: 2, y: 2, z: 4, core: 2. Of those that a mesh axis runs over, the one named last changes fastest.
Arguments:
- spectrogram: bfloat16 [2, 4096, 80], P('dp', 'seq'), may hold values from -6 to 6
- first_kernel: bfloat16 [3, 80, 768], P(None, None, 'mp'), may hold values from -0.375 to 0.375
- first_bias: float32 [768], P('mp'), may hold values from -3 to 3
- second_kernel: bfloat16 [3, 768, 768], P(None, 'mp'), may hold values from -0.125 to 0.125
- second_bias: float32 [768], replicated, may hold values from -3 to 3
- attend_gain: float32 [768], replicated, may hold values from 0.25 to 1.75
- attend_shift: float32 [768], replicated, may hold values from -2 to 2
- project_weight: bfloat16 [768, 3, 768], P(None, None, 'mp'), may hold values from -0.21875 to 0.21875
- project_bias: float32 [2, 768], P(None, 'mp'), may hold values from -2 to 2
- output_weight: bfloat16 [768, 768], P('mp'), may hold values from -1.75 to 1.75
- output_bias: float32 [768], replicated, may hold values from -2 to 2
- mixer_gain: float32 [768], replicated, may hold values from 0.25 to 1.75
- mixer_shift: float32 [768], replicated, may hold values from -2 to 2
- expand_weight: bfloat16 [768, 3072], P(None, 'mp'), may hold values from -0.21875 to 0.21875
- expand_bias: float32 [3072], P('mp'), may hold values from -2 to 2
- reduce_weight: bfloat16 [3072, 768], P('mp'), may hold values from -0.109375 to 0.109375
- reduce_bias: float32 [768], replicated, may hold values from -2 to 2
- cotangent: float32 [2, 2048, 768], P('dp', 'seq'), may hold values from -6 to 6
Outputs:
- encoded: float32 [2, 2048, 768], P('dp', 'seq')
- spectrogram_gradient: float32 [2, 4096, 80], P('dp', 'seq')
- first_kernel_gradient: float32 [3, 80, 768], P(None, None, 'mp')
- first_bias_gradient: float32 [768], P('mp')
- second_kernel_gradient: float32 [3, 768, 768], P(None, 'mp')
- second_bias_gradient: float32 [768], replicated
- attend_gain_gradient: float32 [768], replicated
- attend_shift_gradient: float32 [768], replicated
- project_weight_gradient: float32 [768, 3, 768], P(None, None, 'mp')
- project_bias_gradient: float32 [2, 768], P(None, 'mp')
- output_weight_gradient: float32 [768, 768], P('mp')
- output_bias_gradient: float32 [768], replicated
- mixer_gain_gradient: float32 [768], replicated
- mixer_shift_gradient: float32 [768], replicated
- expand_weight_gradient: float32 [768, 3072], P(None, 'mp')
- expand_bias_gradient: float32 [3072], P('mp')
- reduce_weight_gradient: float32 [3072, 768], P('mp')
- reduce_bias_gradient: float32 [768], replicated
The draws below stay inside these ranges and needn't reach their ends.
All inputs are finite; a program needn't handle non-finite values.
Results may differ from the reference program's by a relative error of at most 0.015.
Values may be sent and summed in bfloat16 or wider, within the bound.
No kernel may reach another device: no remote copies, remote signals or barrier semaphores. Data moves between devices by JAX's collectives and lax.ppermute only.
A program may use at most 128 MiB of HBM per device.

```python
import math
import jax
import jax.numpy as jnp
from jax import lax

D = 768
HEADS = 12
HEAD_DIM = 64
FF = 3072
MEL = 80
FRAMES = 2048
STEPS = 4096
CLIPS = 2


def level_of(rng, shape, cuts, low, largest):
    level, own = 1.0, jax.random.fold_in(rng, 6)
    for dim, blocks in cuts:
        steps = jnp.exp(jax.random.uniform(jax.random.fold_in(own, dim), (blocks,), jnp.float32, low / len(cuts), largest / len(cuts)))
        level = level * jnp.repeat(steps, shape[dim] // blocks).reshape([-1 if axis == dim else 1 for axis in range(len(shape))])
    return level


def gaussian(own_key, dims, deviation, most, shards=(), held_as=jnp.bfloat16):
    level = level_of(own_key, dims, shards, -0.22, 0.18) if shards else 1.0
    values = jax.random.normal(own_key, dims, jnp.float32) * deviation * level
    return jnp.minimum(jnp.maximum(values, -most), most).astype(held_as)


def setup_inputs(seed: int = 0) -> dict:
    key_of = jax.random.split(jax.random.key(seed), 19)
    return {
        "spectrogram": gaussian(key_of[0], (CLIPS, STEPS, MEL), 1.0, 6.0, ((0, 2), (1, 4))),
        "first_kernel": gaussian(key_of[1], (3, MEL, D), (3 * MEL) ** -0.5, 0.375, ((2, 4),)),
        "first_bias": gaussian(key_of[2], (D,), 0.5, 3.0, ((0, 4),), jnp.float32),
        "second_kernel": gaussian(key_of[3], (3, D, D), (3 * D) ** -0.5, 0.125, ((1, 4),)),
        "second_bias": gaussian(key_of[4], (D,), 0.5, 3.0, (), jnp.float32),
        "attend_gain": jnp.clip(1.0 + 0.15 * jax.random.normal(key_of[5], (D,), jnp.float32), 0.25, 1.75),
        "attend_shift": gaussian(key_of[6], (D,), 0.3, 2.0, (), jnp.float32),
        "project_weight": gaussian(key_of[7], (D, 3, D), D ** -0.5, 0.21875, ((2, 4),)),
        "project_bias": gaussian(key_of[8], (2, D), 0.3, 2.0, ((1, 4),), jnp.float32),
        "output_weight": gaussian(key_of[9], (D, D), (D // 64) ** -0.5, 1.75, ((0, 4),)),
        "output_bias": gaussian(key_of[10], (D,), 0.3, 2.0, (), jnp.float32),
        "mixer_gain": jnp.clip(1.0 + 0.15 * jax.random.normal(key_of[11], (D,), jnp.float32), 0.25, 1.75),
        "mixer_shift": gaussian(key_of[12], (D,), 0.3, 2.0, (), jnp.float32),
        "expand_weight": gaussian(key_of[13], (D, FF), D ** -0.5, 0.21875, ((1, 4),)),
        "expand_bias": gaussian(key_of[14], (FF,), 0.3, 2.0, ((0, 4),), jnp.float32),
        "reduce_weight": gaussian(key_of[15], (FF, D), FF ** -0.5, 0.109375, ((0, 4),)),
        "reduce_bias": gaussian(key_of[16], (D,), 0.3, 2.0, (), jnp.float32),
        "cotangent": gaussian(key_of[17], (CLIPS, FRAMES, D), 1.0, 6.0, ((0, 2), (1, 4)), jnp.float32),
    }


@jax.custom_vjp
def low(v):
    return lax.optimization_barrier(v.astype(jnp.bfloat16)).astype(jnp.float32)

@jax.custom_vjp
def low_back(v):
    return v

def low_keep(v):
    return (low(v), None)

def low_pass(kept, grad):
    return (grad,)

def back_keep(v):
    return (v, None)

def back_low(kept, grad):
    return (low(grad),)
low.defvjp(low_keep, low_pass)
low_back.defvjp(back_keep, back_low)

def matmul(left, right):
    return jnp.dot(left, right, precision=lax.Precision.HIGHEST, preferred_element_type=jnp.float32)

def exact_gelu(value):
    return jax.nn.gelu(value, approximate=False)

def layer_norm(value, gain, shift):
    centre = value - lax.optimization_barrier(jnp.mean(value, axis=-1, keepdims=True))
    spread = lax.optimization_barrier(jnp.mean(centre * centre, axis=-1, keepdims=True))
    return centre * lax.rsqrt(spread + 1e-05) * gain + shift

def sinusoid(start, count, width):
    half = width // 2
    rates = jnp.exp(jnp.arange(half, dtype=jnp.float32) * (-math.log(10000.0) / (half - 1)))
    times = (start + jnp.arange(count)).astype(jnp.float32)
    angles = times[:, None] * rates[None, :]
    return jnp.concatenate([jnp.sin(angles), jnp.cos(angles)], axis=1)

def attend_head(query, keys, values):
    scores = low_back(jnp.einsum('qd,kd->qk', query, keys, precision=lax.Precision.HIGHEST) * HEAD_DIM ** (-0.5))
    soft = jax.nn.softmax(scores, axis=-1)
    return jnp.einsum('qk,kd->qd', low(soft), values, precision=lax.Precision.HIGHEST)

def forward_clip(weights, clip):
    first_kernel, first_bias, second_kernel, second_bias, attend_gain, attend_shift, project_weight, project_bias, output_weight, output_bias, mixer_gain, mixer_shift, expand_weight, expand_bias, reduce_weight, reduce_bias = weights
    steps = clip.shape[0]
    frames = steps // 2
    padded = jnp.pad(clip, ((1, 1), (0, 0)))
    taps = jnp.concatenate([padded[0:steps], padded[1:steps + 1], padded[2:steps + 2]], axis=1)
    pre_one = low_back(matmul(taps, first_kernel.reshape(3 * MEL, D)) + first_bias)
    hidden_one = low(exact_gelu(pre_one))
    hidden_pad = jnp.pad(hidden_one, ((1, 1), (0, 0)))
    taps_two = jnp.concatenate([hidden_pad[index:index + steps:2] for index in range(3)], axis=1)
    stem_pre = low_back(matmul(taps_two, second_kernel.reshape(3 * D, D)) + second_bias)
    resid_zero = exact_gelu(stem_pre) + sinusoid(0, frames, D)
    normed_one = low(layer_norm(resid_zero, attend_gain, attend_shift))
    packed = matmul(normed_one, project_weight.reshape(D, 3 * D)).reshape(frames, 3, D)
    offsets = jnp.stack([project_bias[0], jnp.zeros((D,), jnp.float32), project_bias[1]])
    packed = low_back(low(packed + offsets[None]))
    heads = packed.reshape(frames, 3, HEADS, HEAD_DIM).transpose(1, 2, 0, 3)
    checked = jax.checkpoint(attend_head)
    attended = lax.map(lambda trio: checked(trio[0], trio[1], trio[2]), (heads[0], heads[1], heads[2]))
    attended = low_back(low(attended.transpose(1, 0, 2).reshape(frames, D)))
    resid_one = resid_zero + low_back(matmul(attended, output_weight) + output_bias)
    normed_two = low(layer_norm(resid_one, mixer_gain, mixer_shift))
    expanded = low_back(matmul(normed_two, expand_weight) + expand_bias)
    active = low(exact_gelu(expanded))
    return resid_one + low_back(matmul(active, reduce_weight) + reduce_bias)

def reference(spectrogram, first_kernel, first_bias, second_kernel, second_bias, attend_gain, attend_shift, project_weight, project_bias, output_weight, output_bias, mixer_gain, mixer_shift, expand_weight, expand_bias, reduce_weight, reduce_bias, cotangent):
    weights = tuple((item.astype(jnp.float32) for item in (first_kernel, first_bias, second_kernel, second_bias, attend_gain, attend_shift, project_weight, project_bias, output_weight, output_bias, mixer_gain, mixer_shift, expand_weight, expand_bias, reduce_weight, reduce_bias)))
    inputs = spectrogram.astype(jnp.float32)

    def one_clip(carry, item):
        clip, incoming = item
        result, pull = jax.vjp(forward_clip, weights, clip)
        weight_grads, clip_grad = pull(incoming)
        return (jax.tree.map(jnp.add, carry, weight_grads), (result, clip_grad))
    start = jax.tree.map(jnp.zeros_like, weights)
    totals, (encoded, spectrogram_gradient) = lax.scan(one_clip, start, (inputs, cotangent))
    return (encoded, spectrogram_gradient, totals[0], totals[1], totals[2], totals[3], totals[4], totals[5], totals[6], totals[7], totals[8], totals[9], totals[10], totals[11], totals[12], totals[13], totals[14], totals[15])
```

```python
import functools
import math

import jax
import jax.numpy as jnp
from jax import lax
from jax.experimental import pallas as pl
from jax.experimental.pallas import tpu as pltpu
from jax.sharding import PartitionSpec as P

HEAD_DIM = 64
BF = jnp.bfloat16
F32 = jnp.float32
VMEM_LIMIT = 48 * 1024 * 1024


def product(left, right, left_dim=1, right_dim=0):
    dims = (((left_dim,), (right_dim,)), ((), ()))
    return lax.dot_general(left, right, dims, preferred_element_type=F32)


def after(value, *others):
    return lax.optimization_barrier((value, *others))[0]


def exact_gelu(value):
    return jax.nn.gelu(value, approximate=False)


def gelu_back(value, grad):
    return jax.vjp(exact_gelu, value)[1](grad)[0]


def layer_norm(value, gain, shift):
    centre = value - jnp.mean(value, axis=-1, keepdims=True)
    spread = jnp.mean(centre * centre, axis=-1, keepdims=True)
    return centre * lax.rsqrt(spread + 1e-05) * gain + shift


def norm_back(value, gain, grad):
    centre = value - jnp.mean(value, axis=-1, keepdims=True)
    spread = jnp.mean(centre * centre, axis=-1, keepdims=True)
    inverse = lax.rsqrt(spread + 1e-05)
    xhat = centre * inverse
    e = grad * gain
    back = (
        e - jnp.mean(e, axis=-1, keepdims=True) - xhat * jnp.mean(e * xhat, axis=-1, keepdims=True)
    ) * inverse
    return back, jnp.sum(grad * xhat, axis=0), jnp.sum(grad, axis=0)


def column_total(value):
    return jnp.sum(value.astype(F32), axis=0)


def sinusoid(start, count, width):
    half = width // 2
    rates = jnp.exp(jnp.arange(half, dtype=F32) * (-math.log(10000.0) / (half - 1)))
    times = (start + jnp.arange(count)).astype(F32)
    angles = times[:, None] * rates[None, :]
    return jnp.concatenate([jnp.sin(angles), jnp.cos(angles)], axis=1)


def turned(size, by):
    return [(i, (i + by) % size) for i in range(size)]


def gather_mp(block):
    size = lax.axis_size("mp")
    return [block] + [lax.ppermute(block, "mp", turned(size, -j)) for j in range(1, size)]


def exchange_mp(blocks):
    size = lax.axis_size("mp")
    got = [lax.ppermute(blocks[j], "mp", turned(size, j)) for j in range(1, size)]
    return [blocks[0]] + got


def row_blocks(value, count):
    rows = value.shape[0] // count
    return [value[j * rows : (j + 1) * rows] for j in range(count)]


def rolled_blocks(value):
    size, z = lax.axis_size("mp"), lax.axis_index("mp")
    rows = value.shape[0] // size
    return [
        lax.dynamic_slice_in_dim(value, lax.rem(z + j, size) * rows, rows, axis=0)
        for j in range(size)
    ]


def natural(blocks):
    size, z = lax.axis_size("mp"), lax.axis_index("mp")
    rows = blocks[0].shape[0]
    twice = jnp.concatenate(blocks + blocks, axis=0)
    return lax.dynamic_slice_in_dim(twice, lax.rem(size - z, size) * rows, rows * size, axis=0)


def total(parts):
    result = parts[0].astype(F32)
    for part in parts[1:]:
        result = result + part.astype(F32)
    return result


def scatter_sum(blocks):
    return total(exchange_mp([blocks[0]] + [block.astype(BF) for block in blocks[1:]]))


def swapped(value, axis, bit):
    size = lax.axis_size(axis)
    return lax.ppermute(value, axis, [(i, i ^ bit) for i in range(size)])


def passed_along(value, by):
    size = lax.axis_size("seq")
    pairs = [(i, i + by) for i in range(size) if 0 <= i + by < size]
    return lax.ppermute(value, "seq", pairs)


def plane_sum(value):
    rows, columns = value.shape
    dp, seq = lax.axis_index("dp"), lax.axis_index("seq")
    dps, seqs = lax.axis_size("dp"), lax.axis_size("seq")
    core = lax.rem(seq, 2)
    half = columns // 2
    mine = lax.dynamic_slice_in_dim(value, core * half, half, axis=1)
    other = lax.dynamic_slice_in_dim(value, (1 - core) * half, half, axis=1)
    mine = mine + swapped(other.astype(BF), "seq", 1).astype(F32)
    quarter = rows // 4
    index = lax.rem(dp, 2) * 2 + lax.div(seq, 2)

    def pairs(d):
        return [
            (p * seqs + s, (p ^ (d >> 1)) * seqs + (s ^ (2 * (d & 1))))
            for p in range(dps)
            for s in range(seqs)
        ]

    def piece(d):
        return lax.dynamic_slice_in_dim(mine, jnp.bitwise_xor(index, d) * quarter, quarter, axis=0)

    result = piece(0)
    got = [lax.ppermute(piece(d).astype(BF), ("dp", "seq"), pairs(d)) for d in (1, 2, 3)]
    result = total([result] + got).astype(BF)
    if dps > 2:
        groups = [[i for i in range(dps) if i % 2 == bit] for bit in range(2)]
        result = lax.psum(result, "dp", axis_index_groups=groups)
    blocks = [result] + [lax.ppermute(result, ("dp", "seq"), pairs(d)) for d in (1, 2, 3)]
    stacked = jnp.stack(blocks)
    ordered = [
        lax.dynamic_index_in_dim(stacked, jnp.bitwise_xor(index, i), 0, keepdims=False)
        for i in range(4)
    ]
    mine = jnp.concatenate(ordered, axis=0)
    other = swapped(mine, "seq", 1)
    return jnp.where(
        core == 0,
        jnp.concatenate([mine, other], axis=1),
        jnp.concatenate([other, mine], axis=1),
    )


def attend_kernel(heads, scale, query_ref, *refs):
    pair_refs, (out_ref, turned_ref, level_ref, held) = refs[:-4], refs[-4:]
    width = heads * HEAD_DIM
    count = pair_refs[0].shape[0]
    outs, levels = [], []
    for head in range(heads):
        cols = slice(head * HEAD_DIM, (head + 1) * HEAD_DIM)
        query = query_ref[:, cols]
        top = None
        for index, pair in enumerate(pair_refs):
            scores = product(pair[:, cols], query, 1, 1) * scale
            held[index * count : (index + 1) * count, :] = scores
            high = jnp.max(scores, axis=0, keepdims=True)
            top = high if top is None else jnp.maximum(top, high)
        weight, out = 0.0, 0.0
        vcols = slice(width + head * HEAD_DIM, width + (head + 1) * HEAD_DIM)
        for index, pair in enumerate(pair_refs):
            soft = jnp.exp(held[index * count : (index + 1) * count, :] - top)
            weight = weight + jnp.sum(soft, axis=0, keepdims=True)
            out = out + product(pair[:, vcols], soft.astype(BF), 0, 0)
        outs.append(out / weight)
        levels.append(top + jnp.log(weight))
    joined = jnp.concatenate(outs, axis=0)
    turned_ref[...] = joined
    out_ref[...] = joined.T.astype(BF)
    level_ref[...] = jnp.concatenate(levels, axis=0)


def attend(query, pairs):
    rows, width = query.shape
    heads = width // HEAD_DIM
    keys = rows * len(pairs)
    return pl.pallas_call(
        functools.partial(attend_kernel, heads, HEAD_DIM ** (-0.5)),
        out_shape=[
            jax.ShapeDtypeStruct((rows, width), BF),
            jax.ShapeDtypeStruct((width, rows), F32),
            jax.ShapeDtypeStruct((heads, rows), F32),
        ],
        scratch_shapes=[pltpu.VMEM((keys, rows), F32)],
        compiler_params=pltpu.CompilerParams(vmem_limit_bytes=VMEM_LIMIT),
        cost_estimate=pl.CostEstimate(
            flops=16 * rows * keys * width,
            bytes_accessed=rows * width * 8 + keys * width * 4,
            transcendentals=rows * keys * heads,
        ),
        name="attend",
    )(query, *pairs)


def attend_back_kernel(heads, scale, query_ref, grad_ref, turned_ref, level_ref, *refs):
    count = (len(refs) - 1) // 2
    pair_refs, query_out, pair_outs = refs[:count], refs[count], refs[count + 1 :]
    width = heads * HEAD_DIM
    grads_turned = grad_ref[...].astype(F32).T
    query_grads = []
    pair_grads = [([], []) for _ in range(count)]
    for head in range(heads):
        cols = slice(head * HEAD_DIM, (head + 1) * HEAD_DIM)
        vcols = slice(width + head * HEAD_DIM, width + (head + 1) * HEAD_DIM)
        query = query_ref[:, cols]
        grad = grad_ref[:, cols]
        level = level_ref[head : head + 1, :]
        delta = jnp.sum(grads_turned[cols, :] * turned_ref[cols, :], axis=0, keepdims=True)
        query_grad = 0.0
        for index in range(count):
            pair = pair_refs[index]
            key = pair[:, cols]
            soft = jnp.exp(product(key, query, 1, 1) * scale - level)
            grad_soft = product(pair[:, vcols], grad, 1, 1)
            low = (soft * (grad_soft - delta)).astype(BF)
            pair_grads[index][0].append(product(low, query) * scale)
            pair_grads[index][1].append(product(soft.astype(BF), grad))
            query_grad = query_grad + product(key, low, 0, 0)
        query_grads.append(query_grad * scale)
    query_out[...] = jnp.concatenate(query_grads, axis=0).T.astype(query_out.dtype)
    for index in range(count):
        joined = jnp.concatenate(pair_grads[index][0] + pair_grads[index][1], axis=1)
        pair_outs[index][...] = joined.astype(pair_outs[index].dtype)


def attend_back(query, grad, turned_out, level, pairs, kinds, name):
    rows, width = query.shape
    heads = width // HEAD_DIM
    keys = rows * len(pairs)
    return pl.pallas_call(
        functools.partial(attend_back_kernel, heads, HEAD_DIM ** (-0.5)),
        out_shape=[jax.ShapeDtypeStruct((rows, width), F32)]
        + [jax.ShapeDtypeStruct((rows, 2 * width), kind) for kind in kinds],
        compiler_params=pltpu.CompilerParams(vmem_limit_bytes=VMEM_LIMIT),
        cost_estimate=pl.CostEstimate(
            flops=40 * rows * keys * width,
            bytes_accessed=rows * width * 8 + keys * width * 8,
            transcendentals=rows * keys * heads,
        ),
        name=name,
    )(query, grad, turned_out, level, *pairs)


def on_device(
    spectrogram,
    first_kernel,
    first_bias,
    second_kernel,
    second_bias,
    attend_gain,
    attend_shift,
    project_weight,
    project_bias,
    output_weight,
    output_bias,
    mixer_gain,
    mixer_shift,
    expand_weight,
    expand_bias,
    reduce_weight,
    reduce_bias,
    cotangent,
):
    _, steps, bands = spectrogram.shape
    frames = steps // 2
    width = first_kernel.shape[2]
    model = second_kernel.shape[2]
    hidden = expand_weight.shape[1]
    mps, seqs = lax.axis_size("mp"), lax.axis_size("seq")
    z, seq = lax.axis_index("mp"), lax.axis_index("seq")
    core = lax.rem(seq, 2)
    rows = frames // mps

    paired = spectrogram.reshape(frames, 2 * bands)
    before = passed_along(paired[-1:], 1)
    following = passed_along(paired[:1], -1)
    ahead = jnp.concatenate([before, paired, following], axis=0)
    window = jnp.concatenate(
        [ahead[:-2, bands:], ahead[1:-1], ahead[2:, :bands]], axis=1
    )
    prior = jnp.concatenate([before, paired[:1, :bands]], axis=1)
    latter = jnp.concatenate([paired[-1:, bands:], following], axis=1)
    first_matrix = first_kernel.reshape(3 * bands, width)
    even_in = jnp.concatenate([window[:, : 3 * bands], latter], axis=0)
    odd_in = jnp.concatenate([prior, window[:, bands:]], axis=0)
    pre_even = product(even_in, first_matrix) + first_bias
    pre_odd = product(odd_in, first_matrix) + first_bias
    inside = jnp.logical_or(jnp.arange(frames + 1) > 0, seq > 0)[:, None]
    hidden_even = exact_gelu(pre_even[:frames]).astype(BF)
    hidden_odd = jnp.where(inside, exact_gelu(pre_odd), 0.0).astype(BF)
    taps = jnp.concatenate([hidden_odd[:frames], hidden_even, hidden_odd[1:]], axis=1)
    second_matrix = second_kernel.reshape(3 * width, model)
    stem_part = product(taps, second_matrix)
    stem_pre = scatter_sum(rolled_blocks(stem_part)) + second_bias
    resid_zero = exact_gelu(stem_pre) + sinusoid(seq * frames + z * rows, rows, model)
    normed_one_blocks = gather_mp(layer_norm(resid_zero, attend_gain, attend_shift).astype(BF))
    normed_one = jnp.concatenate(normed_one_blocks, axis=0)

    project_matrix = project_weight.reshape(model, 3 * width)
    offsets = jnp.concatenate([project_bias[0], jnp.zeros_like(project_bias[0]), project_bias[1]])
    packed = (product(normed_one, project_matrix) + offsets).astype(BF)
    query, pair = packed[:, :width], packed[:, width:]
    pair_far = swapped(pair, "seq", 2)
    pair_core = swapped(pair, "seq", 1)
    pair_far_core = swapped(pair_far, "seq", 1)
    half = model // 2
    weight_half = lax.dynamic_slice_in_dim(output_weight, core * half, half, axis=1)
    weight_half = after(weight_half, pair)
    got = jnp.stack(gather_mp(weight_half)[1:])
    got_other = swapped(got, "seq", 1)
    sides = jnp.where(
        core == 0,
        jnp.concatenate([got, got_other], axis=2),
        jnp.concatenate([got_other, got], axis=2),
    )
    output_whole = jnp.concatenate(
        [output_weight, sides.reshape((mps - 1) * width, model)], axis=0
    )
    attended, attended_turned, level = attend(query, [pair, pair_core, pair_far, pair_far_core])
    heads_got = exchange_mp(row_blocks(attended, mps))
    attended_rows = jnp.concatenate([heads_got[-j % mps] for j in range(mps)], axis=1)
    resid_one = resid_zero + product(attended_rows, output_whole) + output_bias
    normed_two = jnp.concatenate(
        gather_mp(layer_norm(resid_one, mixer_gain, mixer_shift).astype(BF)), axis=0
    )

    own_cotangent = rolled_blocks(cotangent.reshape(frames, model))
    grad_mlp = jnp.concatenate(own_cotangent, axis=0).astype(BF)
    grad_active = product(grad_mlp, reduce_weight, 1, 1)
    expanded = product(normed_two, expand_weight) + expand_bias
    active = exact_gelu(expanded).astype(BF)
    grad_expanded = gelu_back(expanded, grad_active).astype(BF)
    grad_normed_two = scatter_sum(row_blocks(product(grad_expanded, expand_weight, 1, 1), mps))
    back_two, mixer_gain_part, mixer_shift_part = norm_back(resid_one, mixer_gain, grad_normed_two)
    grad_resid_one = own_cotangent[0] + back_two
    grad_attn = grad_resid_one.astype(BF)
    grad_heads = product(grad_attn, output_whole, 1, 1).astype(BF)
    rows_got = exchange_mp([grad_heads[:, j * width : (j + 1) * width] for j in range(mps)])
    grad_attended = jnp.concatenate([rows_got[-j % mps] for j in range(mps)], axis=0)

    active_late = after(active, grad_attended)
    reduce_weight_part = product(active_late, grad_mlp, 0, 0)
    expand_weight_part = product(normed_two, grad_expanded, 0, 0)
    mlp_sums = lax.psum((expand_weight_part.astype(BF), reduce_weight_part.astype(BF)), ("dp", "seq"))
    encoded_part = scatter_sum(row_blocks(product(active_late, reduce_weight), mps))
    encoded_own = (resid_one + encoded_part + reduce_bias).astype(BF)
    encoded = natural(gather_mp(encoded_own)).astype(F32)
    grad_attn_all = gather_mp(after(grad_attn, grad_attended))
    output_weight_part = product(attended, jnp.concatenate(grad_attn_all, axis=0), 0, 0)

    query_grad_far, far, far_core = attend_back(
        query, grad_attended, attended_turned, level, [pair_far, pair_far_core], (F32, BF), "back_far"
    )
    far = far + swapped(far_core, "seq", 1).astype(F32)
    far_got = swapped(far.astype(BF), "seq", 2)
    query_grad_near, near, near_core = attend_back(
        query, grad_attended, attended_turned, level, [pair, pair_core], (F32, BF), "back_near"
    )
    near = near + swapped(near_core, "seq", 1).astype(F32)
    grad_packed = jnp.concatenate(
        [query_grad_far + query_grad_near, near + far_got.astype(F32)], axis=1
    ).astype(BF)
    project_columns = column_total(grad_packed)
    grad_normed_one = scatter_sum(row_blocks(product(grad_packed, project_matrix, 1, 1), mps))
    project_part = product(grad_packed, normed_one, 0, 0)
    late_sums = lax.psum((project_part.astype(BF), output_weight_part.astype(BF)), ("dp", "seq"))
    back_one, attend_gain_part, attend_shift_part = norm_back(
        resid_zero, attend_gain, grad_normed_one
    )
    grad_stem_own = gelu_back(stem_pre, grad_resid_one + back_one).astype(BF)

    small_own = jnp.stack(
        [
            attend_gain_part,
            attend_shift_part,
            mixer_gain_part,
            mixer_shift_part,
            column_total(grad_attn),
            column_total(grad_stem_own),
        ]
    )
    small_own = jnp.concatenate([small_own, jnp.zeros((10, model), F32)], axis=0).astype(BF)
    gathered = gather_mp(jnp.concatenate([grad_stem_own, small_own], axis=0))
    grad_stem = natural([block[:rows] for block in gathered])
    small = natural([block[rows:] for block in gathered]).reshape(mps, 16, model)
    small = jnp.sum(small.astype(F32), axis=0)[:6]
    stem_before = passed_along(grad_stem[-1:], 1)
    stem_following = passed_along(grad_stem[:1], -1)
    second_part = product(taps, grad_stem, 0, 0)
    stem_ahead = jnp.concatenate([stem_before, grad_stem, stem_following], axis=0)
    grad_taps = product(stem_ahead, second_matrix, 1, 1)
    grad_even = grad_taps[1:, width : 2 * width]
    grad_odd = grad_taps[:-1, 2 * width :] + grad_taps[1:, :width]
    grad_pre_even = gelu_back(pre_even, grad_even).astype(BF)
    grad_pre_odd = jnp.where(inside, gelu_back(pre_odd, grad_odd), 0.0).astype(BF)
    first_bias_part = column_total(grad_pre_even[:frames]) + column_total(grad_pre_odd[1:])
    first_part = product(window[:, : 3 * bands], grad_pre_even[:frames], 0, 0) + product(
        window[:, bands:], grad_pre_odd[1:], 0, 0
    )
    back_window = jnp.concatenate(
        [grad_pre_odd[:frames], grad_pre_even[:frames], grad_pre_odd[1:], grad_pre_even[1:]], axis=1
    )
    back_matrix = jnp.transpose(first_kernel[::-1], (0, 2, 1)).reshape(3 * width, bands)
    spectrum_part = jnp.concatenate(
        [
            product(back_window[:, : 3 * width], back_matrix),
            product(back_window[:, width:], back_matrix),
        ],
        axis=1,
    )
    spectrum_own = scatter_sum(rolled_blocks(spectrum_part)).astype(BF)
    spectrogram_gradient = natural(gather_mp(spectrum_own)).astype(F32).reshape(1, steps, bands)

    small_flat = jnp.concatenate(
        [
            small.reshape(-1),
            column_total(cotangent.reshape(frames, model).astype(BF)),
            column_total(grad_expanded),
            project_columns[:width],
            project_columns[2 * width :],
            first_bias_part,
        ]
    )
    first_flat = first_part.reshape(-1, model)
    used = 3 * width + first_flat.shape[0]
    small_rows = -(-small_flat.shape[0] // model)
    padded_rows = -(-(used + small_rows) // 32) * 32
    small_flat = jnp.pad(small_flat, (0, (padded_rows - used) * model - small_flat.shape[0]))
    last = plane_sum(
        jnp.concatenate([second_part, first_flat, small_flat.reshape(-1, model)], axis=0)
    ).astype(F32)
    second_kernel_gradient = last[: 3 * width].reshape(3, width, model)
    first_kernel_gradient = last[3 * width : used].reshape(3, bands, width)
    sums = last[used:].reshape(-1)
    places = {}
    place = 0
    for name, size in (
        ("attend_gain", model),
        ("attend_shift", model),
        ("mixer_gain", model),
        ("mixer_shift", model),
        ("output_bias", model),
        ("second_bias", model),
        ("reduce_bias", model),
        ("expand_bias", hidden),
        ("project_bias", 2 * width),
        ("first_bias", width),
    ):
        places[name] = sums[place : place + size]
        place += size
    return (
        encoded.reshape(1, frames, model),
        spectrogram_gradient,
        first_kernel_gradient,
        places["first_bias"],
        second_kernel_gradient,
        places["second_bias"],
        places["attend_gain"],
        places["attend_shift"],
        late_sums[0].astype(F32).T.reshape(model, 3, width),
        places["project_bias"].reshape(2, width),
        late_sums[1].astype(F32),
        places["output_bias"],
        places["mixer_gain"],
        places["mixer_shift"],
        mlp_sums[0].astype(F32),
        places["expand_bias"],
        mlp_sums[1].astype(F32),
        places["reduce_bias"],
    )


def solution(mesh):
    return jax.shard_map(
        on_device,
        mesh=mesh,
        in_specs=(
            P("dp", "seq", None),
            P(None, None, "mp"),
            P("mp"),
            P(None, "mp", None),
            P(),
            P(),
            P(),
            P(None, None, "mp"),
            P(None, "mp"),
            P("mp", None),
            P(),
            P(),
            P(),
            P(None, "mp"),
            P("mp"),
            P("mp", None),
            P(),
            P("dp", "seq", None),
        ),
        out_specs=(
            P("dp", "seq", None),
            P("dp", "seq", None),
            P(None, None, "mp"),
            P("mp"),
            P(None, "mp", None),
            P(),
            P(),
            P(),
            P(None, None, "mp"),
            P(None, "mp"),
            P("mp", None),
            P(),
            P(),
            P(),
            P(None, "mp"),
            P("mp"),
            P("mp", None),
            P(),
        ),
        check_vma=False,
    )
```

```python
import functools
import math

import jax
import jax.numpy as jnp
from jax import lax
from jax.experimental import pallas as pl
from jax.experimental.pallas import tpu as pltpu
from jax.sharding import PartitionSpec as P

HEAD_DIM = 64
BF = jnp.bfloat16
F32 = jnp.float32
VMEM_LIMIT = 60 * 1024 * 1024
SMALL = pl.CostEstimate(flops=1, bytes_accessed=1, transcendentals=0)


def product(left, right, left_dim=1, right_dim=0):
    dims = (((left_dim,), (right_dim,)), ((), ()))
    return lax.dot_general(left, right, dims, preferred_element_type=F32)


def after(value, *others):
    return lax.optimization_barrier((value, *others))[0]


def exact_gelu(value):
    return jax.nn.gelu(value, approximate=False)


def gelu_back(value, grad):
    return jax.vjp(exact_gelu, value)[1](grad)[0]


def layer_norm(value, gain, shift):
    centre = value - jnp.mean(value, axis=-1, keepdims=True)
    spread = jnp.mean(centre * centre, axis=-1, keepdims=True)
    return centre * lax.rsqrt(spread + 1e-05) * gain + shift


def norm_back(value, gain, grad):
    centre = value - jnp.mean(value, axis=-1, keepdims=True)
    spread = jnp.mean(centre * centre, axis=-1, keepdims=True)
    inverse = lax.rsqrt(spread + 1e-05)
    xhat = centre * inverse
    e = grad * gain
    back = (
        e - jnp.mean(e, axis=-1, keepdims=True) - xhat * jnp.mean(e * xhat, axis=-1, keepdims=True)
    ) * inverse
    return back, jnp.sum(grad * xhat, axis=0), jnp.sum(grad, axis=0)


def column_total(value):
    return jnp.sum(value.astype(F32), axis=0)


def sinusoid(start, count, width):
    half = width // 2
    rates = jnp.exp(jnp.arange(half, dtype=F32) * (-math.log(10000.0) / (half - 1)))
    times = (start + jnp.arange(count)).astype(F32)
    angles = times[:, None] * rates[None, :]
    return jnp.concatenate([jnp.sin(angles), jnp.cos(angles)], axis=1)


def turned(size, by):
    return [(i, (i + by) % size) for i in range(size)]


def gather_mp(block, name):
    size = lax.axis_size("mp")
    with jax.named_scope(name):
        return [block] + [lax.ppermute(block, "mp", turned(size, -j)) for j in range(1, size)]


def exchange_mp(blocks, name):
    size = lax.axis_size("mp")
    with jax.named_scope(name):
        got = [lax.ppermute(blocks[j], "mp", turned(size, j)) for j in range(1, size)]
    return [blocks[0]] + got


def row_blocks(value, count):
    rows = value.shape[0] // count
    return [value[j * rows : (j + 1) * rows] for j in range(count)]


def rolled_blocks(value):
    size, z = lax.axis_size("mp"), lax.axis_index("mp")
    rows = value.shape[0] // size
    return [
        lax.dynamic_slice_in_dim(value, lax.rem(z + j, size) * rows, rows, axis=0)
        for j in range(size)
    ]


def natural(blocks):
    size, z = lax.axis_size("mp"), lax.axis_index("mp")
    rows = blocks[0].shape[0]
    twice = jnp.concatenate(blocks + blocks, axis=0)
    return lax.dynamic_slice_in_dim(twice, lax.rem(size - z, size) * rows, rows * size, axis=0)


def total(parts):
    result = parts[0].astype(F32)
    for part in parts[1:]:
        result = result + part.astype(F32)
    return result


def scatter_sum(blocks, name):
    return total(exchange_mp([blocks[0]] + [block.astype(BF) for block in blocks[1:]], name))


def swapped(value, axis, bit, name):
    size = lax.axis_size(axis)
    with jax.named_scope(name):
        return lax.ppermute(value, axis, [(i, i ^ bit) for i in range(size)])


def passed_along(value, by):
    size = lax.axis_size("seq")
    pairs = [(i, i + by) for i in range(size) if 0 <= i + by < size]
    return lax.ppermute(value, "seq", pairs)


def plane_index():
    return lax.rem(lax.axis_index("dp"), 2) * 2 + lax.div(lax.axis_index("seq"), 2)


def plane_move(value, d, name):
    dps, seqs = lax.axis_size("dp"), lax.axis_size("seq")
    pairs = [
        (p * seqs + s, (p ^ (d >> 1)) * seqs + (s ^ (2 * (d & 1))))
        for p in range(dps)
        for s in range(seqs)
    ]
    with jax.named_scope(name):
        return lax.ppermute(value, ("dp", "seq"), pairs)


def rest_of_dp(value):
    dps = lax.axis_size("dp")
    if dps > 2:
        groups = [[i for i in range(dps) if i % 2 == bit] for bit in range(2)]
        value = lax.psum(value, "dp", axis_index_groups=groups)
    return value


def plane_scatter(mine, name):
    quarter = mine.shape[0] // 4
    index = plane_index()

    def piece(d):
        return lax.dynamic_slice_in_dim(mine, jnp.bitwise_xor(index, d) * quarter, quarter, axis=0)

    got = [plane_move(piece(d).astype(BF), d, name) for d in (1, 2, 3)]
    return rest_of_dp(total([piece(0)] + got).astype(BF))


def plane_gather(piece):
    dps = lax.axis_size("dp")
    if dps == 2:
        return lax.all_gather(piece, ("dp", "seq"), axis=0, tiled=True)
    pairs = [[i, i + 1] for i in range(0, dps, 2)]
    return lax.all_gather(
        lax.all_gather(piece, "seq", axis=0, tiled=True),
        "dp",
        axis=0,
        tiled=True,
        axis_index_groups=pairs,
    )


def core_eighths(value):
    core = lax.rem(lax.axis_index("seq"), 2)
    rows, columns = value.shape
    pieces = value.reshape(4, 2, rows // 8, columns)
    return [
        lax.dynamic_index_in_dim(pieces, which, 1, keepdims=False).reshape(rows // 2, columns)
        for which in (core, 1 - core)
    ]


def core_rows(held, core, mine_out, other_out):
    rows = held.shape[0] // 8
    others = []
    for quarter in range(4):
        here = pl.ds(pl.multiple_of((2 * quarter + core) * rows, rows), rows)
        there = pl.ds(pl.multiple_of((2 * quarter + 1 - core) * rows, rows), rows)
        mine_out[quarter * rows : (quarter + 1) * rows, :] = held[here, :]
        others.append(held[there, :])
    other_out[...] = jnp.concatenate(others, axis=0).astype(BF)


def finish_kernel(bands, loose, vectors, gathered_ref, second_out, first_out, *refs):
    outs, (whole, small) = refs[:-2], refs[-2:]
    whole[...] = gathered_ref[...].astype(F32)
    eighth = whole.shape[0] // 8
    rows, few = eighth - loose // 8, loose // 8
    for p in range(8):
        second_out[p * rows : (p + 1) * rows, :] = whole[p * eighth : p * eighth + rows, :]
        small[p * few : (p + 1) * few, :] = whole[p * eighth + rows : (p + 1) * eighth, :]
    width = first_out.shape[1]
    for tap in range(3):
        first_out[tap * bands : (tap + 1) * bands, :] = small[
            :bands, tap * width : (tap + 1) * width
        ]
    for out, (row, start, stop) in zip(outs, vectors):
        out[...] = small[bands + row, start:stop]


def finish(gathered, bands, loose, width, vectors):
    rows, model = gathered.shape
    return pl.pallas_call(
        functools.partial(finish_kernel, bands, loose, vectors),
        out_shape=[
            jax.ShapeDtypeStruct((rows - loose, model), F32),
            jax.ShapeDtypeStruct((3 * bands, width), F32),
        ]
        + [jax.ShapeDtypeStruct((stop - start,), F32) for _, start, stop in vectors],
        scratch_shapes=[pltpu.VMEM((rows, model), F32), pltpu.VMEM((loose, model), F32)],
        compiler_params=pltpu.CompilerParams(vmem_limit_bytes=VMEM_LIMIT),
        cost_estimate=SMALL,
        name="finish",
    )(gathered)


def attend_kernel(heads, scale, query_ref, *refs):
    pair_refs, (out_ref, turned_ref, level_ref, held) = refs[:-4], refs[-4:]
    width = heads * HEAD_DIM
    count = pair_refs[0].shape[0]
    outs, levels = [], []
    for head in range(heads):
        cols = slice(head * HEAD_DIM, (head + 1) * HEAD_DIM)
        query = query_ref[:, cols]
        top = None
        for index, pair in enumerate(pair_refs):
            scores = product(pair[:, cols], query, 1, 1) * scale
            held[index * count : (index + 1) * count, :] = scores
            high = jnp.max(scores, axis=0, keepdims=True)
            top = high if top is None else jnp.maximum(top, high)
        weight, out = 0.0, 0.0
        vcols = slice(width + head * HEAD_DIM, width + (head + 1) * HEAD_DIM)
        for index, pair in enumerate(pair_refs):
            soft = jnp.exp(held[index * count : (index + 1) * count, :] - top)
            weight = weight + jnp.sum(soft, axis=0, keepdims=True)
            out = out + product(pair[:, vcols], soft.astype(BF), 0, 0)
        outs.append(out / weight)
        levels.append(top + jnp.log(weight))
    joined = jnp.concatenate(outs, axis=0)
    turned_ref[...] = joined
    out_ref[...] = joined.T.astype(BF)
    level_ref[...] = jnp.concatenate(levels, axis=0)


def attend(query, pairs):
    rows, width = query.shape
    heads = width // HEAD_DIM
    keys = rows * len(pairs)
    return pl.pallas_call(
        functools.partial(attend_kernel, heads, HEAD_DIM ** (-0.5)),
        out_shape=[
            jax.ShapeDtypeStruct((rows, width), BF),
            jax.ShapeDtypeStruct((width, rows), F32),
            jax.ShapeDtypeStruct((heads, rows), F32),
        ],
        scratch_shapes=[pltpu.VMEM((keys, rows), F32)],
        compiler_params=pltpu.CompilerParams(vmem_limit_bytes=VMEM_LIMIT),
        cost_estimate=SMALL,
        name="attend",
    )(query, *pairs)


def attend_back_kernel(heads, scale, query_ref, grad_ref, turned_ref, level_ref, *refs):
    pair_refs, (query_out, near_out, far_out, core_out) = refs[:4], refs[4:]
    width = heads * HEAD_DIM
    grads_turned = grad_ref[...].astype(F32).T
    query_grads = []
    pair_grads = [([], []) for _ in range(4)]
    for head in range(heads):
        cols = slice(head * HEAD_DIM, (head + 1) * HEAD_DIM)
        vcols = slice(width + head * HEAD_DIM, width + (head + 1) * HEAD_DIM)
        query = query_ref[:, cols]
        grad = grad_ref[:, cols]
        level = level_ref[head : head + 1, :]
        delta = jnp.sum(grads_turned[cols, :] * turned_ref[cols, :], axis=0, keepdims=True)
        query_grad = 0.0
        for index in range(4):
            pair = pair_refs[index]
            key = pair[:, cols]
            soft = jnp.exp(product(key, query, 1, 1) * scale - level)
            grad_soft = product(pair[:, vcols], grad, 1, 1)
            low = (soft * (grad_soft - delta)).astype(BF)
            pair_grads[index][0].append(product(low, query) * scale)
            pair_grads[index][1].append(product(soft.astype(BF), grad))
            query_grad = query_grad + product(key, low, 0, 0)
        query_grads.append(query_grad * scale)
    query_out[...] = jnp.concatenate(query_grads, axis=0).T
    near, near_core, far, far_core = [
        jnp.concatenate(keys + values, axis=1) for keys, values in pair_grads
    ]
    near_out[...] = near
    far_out[...] = far
    core_out[0] = near_core.astype(BF)
    core_out[1] = far_core.astype(BF)


def attend_back(query, grad, turned_out, level, pairs):
    rows, width = query.shape
    heads = width // HEAD_DIM
    return pl.pallas_call(
        functools.partial(attend_back_kernel, heads, HEAD_DIM ** (-0.5)),
        out_shape=[
            jax.ShapeDtypeStruct((rows, width), F32),
            jax.ShapeDtypeStruct((rows, 2 * width), F32),
            jax.ShapeDtypeStruct((rows, 2 * width), F32),
            jax.ShapeDtypeStruct((2, rows, 2 * width), BF),
        ],
        compiler_params=pltpu.CompilerParams(vmem_limit_bytes=VMEM_LIMIT),
        cost_estimate=SMALL,
        name="attend_back",
    )(query, grad, turned_out, level, *pairs)


def gelu_parts(value):
    share = 0.5 + 0.5 * lax.erf(value * math.sqrt(0.5))
    slope = share + value * jnp.exp(-0.5 * value * value) * (1.0 / math.sqrt(2.0 * math.pi))
    return value * share, slope


def across_of(weights_ref, place, j, hidden, width):
    mps = weights_ref.shape[0] // hidden
    start = pl.multiple_of(lax.rem(place + j, mps) * hidden, hidden)
    return weights_ref[pl.ds(start, hidden), :width]


def norm_parts(value):
    centre = value - jnp.mean(value, axis=-1, keepdims=True)
    inverse = lax.rsqrt(jnp.mean(centre * centre, axis=-1, keepdims=True) + 1e-05)
    return centre * inverse, inverse


def norm_pull(grad, gain, xhat, inverse):
    e = grad * gain
    shared = jnp.mean(e, axis=-1, keepdims=True) + xhat * jnp.mean(e * xhat, axis=-1, keepdims=True)
    return (e - shared) * inverse


def join_kernel(place_ref, weights_ref, resid_ref, vectors_ref, *refs):
    heads_refs, (resid_out, normed_out) = refs[:-2], refs[-2:]
    mps, width = len(heads_refs), heads_refs[0].shape[1]
    hidden = weights_ref.shape[0] // mps
    resid = resid_ref[...] + vectors_ref[0:1, :]
    for j in range(mps):
        part = across_of(weights_ref, place_ref[0], -j % mps, hidden, width)
        resid = resid + product(heads_refs[j][...], part, 1, 1)
    resid_out[...] = resid
    xhat, _ = norm_parts(resid)
    normed_out[...] = (xhat * vectors_ref[2:3, :] + vectors_ref[3:4, :]).astype(BF)


def join(place, weights, heads, resid, vectors):
    rows, model = resid.shape
    wide = weights.shape[1] % 256 + 256 if weights.shape[1] % 256 else 256
    vmem = pl.BlockSpec(memory_space=pltpu.VMEM)
    return pl.pallas_call(
        join_kernel,
        grid=(1,),
        in_specs=[
            pl.BlockSpec(memory_space=pltpu.SMEM),
            pl.BlockSpec((weights.shape[0], wide), lambda i: (0, weights.shape[1] // wide - 1)),
        ]
        + [vmem] * (2 + len(heads)),
        out_specs=[vmem, vmem],
        out_shape=[
            jax.ShapeDtypeStruct((rows, model), F32),
            jax.ShapeDtypeStruct((rows, model), BF),
        ],
        compiler_params=pltpu.CompilerParams(vmem_limit_bytes=VMEM_LIMIT),
        cost_estimate=SMALL,
        name="join",
    )(place, weights, resid, vectors, *heads)


def middle_kernel(
    mps,
    width,
    place_ref,
    weights_ref,
    across_ref,
    resid_ref,
    normed_ref,
    cotangent_ref,
    vectors_ref,
    shown_ref,
    grad_ref,
    sums_ref,
    grad_heads_ref,
    forward,
    backward,
):
    rows, model = resid_ref.shape
    hidden = across_ref.shape[0] // mps
    step = pl.program_id(0)

    @pl.when(step == 0)
    def _():
        forward[...] = jnp.zeros_like(forward)
        backward[...] = jnp.zeros_like(backward)

    expand = weights_ref[:, :model]
    reduce = weights_ref[:, model : 2 * model]
    tail = weights_ref[:, weights_ref.shape[1] - 128 :]
    lane = lax.broadcasted_iota(jnp.int32, (rows, 128), 1)
    bias_lane = 2 * model + width - (weights_ref.shape[1] - 128)
    ones = jnp.where(jnp.logical_or(lane == bias_lane, lane == bias_lane + 1), 1.0, 0.0).astype(BF)
    value = product(normed_ref[...], expand, 1, 1) + product(ones, tail, 1, 1)
    active, slope = gelu_parts(value)
    forward[...] += product(active.astype(BF), reduce)
    grad_mlp = cotangent_ref[...].astype(BF)
    grad = (product(grad_mlp, reduce, 1, 1) * slope).astype(BF)
    backward[...] += product(grad, expand)

    @pl.when(step == pl.num_programs(0) - 1)
    def _():
        resid = resid_ref[...]
        shown_ref[:, model:] = (resid + forward[...] + vectors_ref[1:2, :]).astype(BF)
        xhat, inverse = norm_parts(resid)
        grad = backward[...]
        grad_resid = cotangent_ref[...] + norm_pull(grad, vectors_ref[2:3, :], xhat, inverse)
        grad_ref[...] = grad_resid
        attn = grad_resid.astype(BF)
        shown_ref[:, :model] = attn
        sums_ref[...] = jnp.concatenate(
            [
                jnp.sum(grad * xhat, axis=0, keepdims=True),
                jnp.sum(grad, axis=0, keepdims=True),
                jnp.sum(attn.astype(F32), axis=0, keepdims=True),
                jnp.zeros((5, model), F32),
            ],
            axis=0,
        )
        for j in range(mps):
            part = across_of(across_ref, place_ref[0], j, hidden, width)
            grad_heads_ref[j] = product(attn, part).astype(BF)


def middle(place, weights, resid, normed, cotangent, vectors, mps, width):
    rows, model = resid.shape
    wide = weights.shape[1] % 256 + 256 if weights.shape[1] % 256 else 256
    chunk = 512
    vmem = pl.BlockSpec(memory_space=pltpu.VMEM)
    return pl.pallas_call(
        functools.partial(middle_kernel, mps, width),
        grid=(weights.shape[0] // chunk,),
        in_specs=[
            pl.BlockSpec(memory_space=pltpu.SMEM),
            pl.BlockSpec((chunk, weights.shape[1]), lambda i: (i, 0)),
            pl.BlockSpec((weights.shape[0], wide), lambda i: (0, weights.shape[1] // wide - 1)),
        ]
        + [vmem] * 4,
        out_specs=[vmem] * 4,
        out_shape=[
            jax.ShapeDtypeStruct((rows, 2 * model), BF),
            jax.ShapeDtypeStruct((rows, model), F32),
            jax.ShapeDtypeStruct((8, model), F32),
            jax.ShapeDtypeStruct((mps, rows, width), BF),
        ],
        scratch_shapes=[pltpu.VMEM((rows, model), F32)] * 2,
        compiler_params=pltpu.CompilerParams(vmem_limit_bytes=VMEM_LIMIT),
        cost_estimate=SMALL,
        name="middle",
    )(place, weights, weights, resid, normed, cotangent, vectors)


def feed_kernel(chunk, expand_ref, reduce_ref, bias_ref, grad_ref, *refs):
    normed_refs, refs = refs[:-5], refs[-5:]
    expand_out, reduce_out, bias_out, normed, normed_turned = refs
    rows = normed_refs[0].shape[0]
    for j, ref in enumerate(normed_refs):
        normed[j * rows : (j + 1) * rows, :] = ref[...]
    normed_turned[...] = normed[...].T
    hidden = expand_ref.shape[1]
    for start in range(0, hidden, chunk):
        here = slice(start, start + chunk)
        value = product(normed[...], expand_ref[:, here]) + bias_ref[:, here]
        active, slope = gelu_parts(value)
        grad = product(grad_ref[...], reduce_ref[here, :], 1, 1) * slope
        low = grad.astype(BF)
        reduce_out[here, :] = product(active.astype(BF), grad_ref[...], 0, 0).astype(BF)
        expand_out[:, here] = product(normed_turned[...], low).astype(BF)
        bias_out[:, here] = jnp.sum(low.astype(F32), axis=0, keepdims=True)


def feed(expand, reduce, bias, grad, normed_blocks):
    model, hidden = expand.shape
    rows = grad.shape[0]
    return pl.pallas_call(
        functools.partial(feed_kernel, 256),
        out_shape=[
            jax.ShapeDtypeStruct((model, hidden), BF),
            jax.ShapeDtypeStruct((hidden, model), BF),
            jax.ShapeDtypeStruct((1, hidden), F32),
        ],
        scratch_shapes=[pltpu.VMEM((rows, model), BF), pltpu.VMEM((model, rows), BF)],
        compiler_params=pltpu.CompilerParams(vmem_limit_bytes=VMEM_LIMIT),
        cost_estimate=SMALL,
        name="feed",
    )(expand, reduce, bias, grad, *normed_blocks)


def pack_kernel(place_ref, query_ref, pair_ref, core_ref, other_ref, weight_ref, *outs):
    packed_out, own_out, others_out, sums_out = outs
    query = query_ref[...]
    pair = pair_ref[...] + core_ref[0].astype(F32) + other_ref[...].astype(F32)
    packed = jnp.concatenate([query, pair], axis=1).astype(BF)
    packed_out[...] = packed
    sums_out[...] = jnp.sum(packed.astype(F32), axis=0, keepdims=True)
    rows = own_out.shape[0]
    mps = others_out.shape[0] + 1

    def part(j):
        start = pl.multiple_of(lax.rem(place_ref[0] + j, mps) * rows, rows)
        return product(packed_out[pl.ds(start, rows), :], weight_ref[...])

    own_out[...] = part(0)
    for j in range(1, mps):
        others_out[j - 1] = part(j).astype(BF)


def pack(place, query, pair, pair_core, pair_far, weight, mps):
    frames, width = query.shape
    model, rows = weight.shape[1], frames // mps
    vmem = pl.BlockSpec(memory_space=pltpu.VMEM)
    return pl.pallas_call(
        pack_kernel,
        in_specs=[pl.BlockSpec(memory_space=pltpu.SMEM)] + [vmem] * 5,
        out_shape=[
            jax.ShapeDtypeStruct((frames, 3 * width), BF),
            jax.ShapeDtypeStruct((rows, model), F32),
            jax.ShapeDtypeStruct((mps - 1, rows, model), BF),
            jax.ShapeDtypeStruct((1, 3 * width), F32),
        ],
        compiler_params=pltpu.CompilerParams(vmem_limit_bytes=VMEM_LIMIT),
        cost_estimate=SMALL,
        name="pack",
    )(place, query, pair, pair_core, pair_far, weight)


def pull_kernel(resid_ref, grad_ref, stem_ref, gain_ref, sums_ref, *refs):
    got_refs, out_ref = refs[:-1], refs[-1]
    rows, model = resid_ref.shape
    grad = got_refs[0][...].astype(F32)
    for ref in got_refs[1:]:
        grad = grad + ref[...].astype(F32)
    xhat, inverse = norm_parts(resid_ref[...])
    grad_resid = grad_ref[...] + norm_pull(grad, gain_ref[...], xhat, inverse)
    _, slope = gelu_parts(stem_ref[...])
    low = (grad_resid * slope).astype(BF)
    out_ref[:rows, :] = low
    sums = jnp.concatenate(
        [
            jnp.sum(grad * xhat, axis=0, keepdims=True),
            jnp.sum(grad, axis=0, keepdims=True),
            sums_ref[0:3, :],
            jnp.sum(low.astype(F32), axis=0, keepdims=True),
            jnp.zeros((10, model), F32),
        ],
        axis=0,
    )
    out_ref[rows:, :] = sums.astype(BF)


def pull(resid, grad, stem, gain, sums, got):
    rows, model = resid.shape
    return pl.pallas_call(
        pull_kernel,
        out_shape=jax.ShapeDtypeStruct((rows + 16, model), BF),
        compiler_params=pltpu.CompilerParams(vmem_limit_bytes=VMEM_LIMIT),
        cost_estimate=SMALL,
        name="pull",
    )(resid, grad, stem, gain, sums, *got)


def project_kernel(places_ref, packed_ref, normed_ref, attended_ref, attn_ref, *refs):
    mine_out, other_out, held = refs
    wide = packed_ref.shape[1]
    held[:wide, :] = product(packed_ref[...], normed_ref[...], 0, 0)
    held[wide:, :] = product(attended_ref[...], attn_ref[...], 0, 0)
    core_rows(held, places_ref[1], mine_out, other_out)


def project_weights(places, packed, normed, attended, shown):
    frames, wide = packed.shape
    width, model = attended.shape[1], normed.shape[1]
    vmem = pl.BlockSpec(memory_space=pltpu.VMEM)
    half = (wide + width) // 2
    return pl.pallas_call(
        project_kernel,
        grid=(1,),
        in_specs=[pl.BlockSpec(memory_space=pltpu.SMEM)]
        + [vmem] * 3
        + [pl.BlockSpec((frames, model), lambda i: (0, 0))],
        out_specs=[vmem, vmem],
        out_shape=[
            jax.ShapeDtypeStruct((half, model), F32),
            jax.ShapeDtypeStruct((half, model), BF),
        ],
        scratch_shapes=[pltpu.VMEM((wide + width, model), F32)],
        compiler_params=pltpu.CompilerParams(vmem_limit_bytes=VMEM_LIMIT),
        cost_estimate=SMALL,
        name="project_weights",
    )(places, packed, normed, attended, shown)


def second_kernel_body(mps, places_ref, taps_ref, gathered_ref, *refs):
    grad_out, sums_out, mine_out, other_out, held = refs
    rows = gathered_ref.shape[0] // mps
    own = rows - 16
    sums = 0.0
    for j in range(mps):
        grad_out[j * own : (j + 1) * own, :] = gathered_ref[j * rows : j * rows + own, :]
        sums = sums + gathered_ref[j * rows + own : (j + 1) * rows, :].astype(F32)
    sums_out[...] = sums
    held[...] = product(taps_ref[...], grad_out[...], 0, 0)
    core_rows(held, places_ref[1], mine_out, other_out)


def second_weight(places, taps, gathered, mps):
    frames, wide = taps.shape
    model = gathered.shape[1]
    vmem = pl.BlockSpec(memory_space=pltpu.VMEM)
    return pl.pallas_call(
        functools.partial(second_kernel_body, mps),
        in_specs=[pl.BlockSpec(memory_space=pltpu.SMEM)] + [vmem] * 2,
        out_shape=[
            jax.ShapeDtypeStruct((frames, model), BF),
            jax.ShapeDtypeStruct((16, model), F32),
            jax.ShapeDtypeStruct((wide // 2, model), F32),
            jax.ShapeDtypeStruct((wide // 2, model), BF),
        ],
        scratch_shapes=[pltpu.VMEM((wide, model), F32)],
        compiler_params=pltpu.CompilerParams(vmem_limit_bytes=VMEM_LIMIT),
        cost_estimate=SMALL,
        name="second_weight",
    )(places, taps, gathered)


def stem_back_kernel(
    bands,
    places_ref,
    grad_ref,
    edges_ref,
    matrix_ref,
    even_ref,
    odd_ref,
    rim_ref,
    window_ref,
    back_ref,
    sums_ref,
    reduce_ref,
    expand_ref,
    project_ref,
    held,
    spectrum_out,
):
    frames = grad_ref.shape[0]
    width = even_ref.shape[1]
    row = lax.broadcasted_iota(jnp.int32, (frames, width), 0)

    def later(value, last):
        return jnp.where(row == frames - 1, last, pltpu.roll(value, frames - 1, 0))

    def earlier(value, start):
        return jnp.where(row == 0, start, pltpu.roll(value, 1, 0))

    def slope(value):
        return gelu_parts(value)[1]

    def rounded(value):
        return value.astype(BF).astype(F32)

    taps = product(grad_ref[...], matrix_ref[...], 1, 1)
    rims = product(edges_ref[...], matrix_ref[...], 1, 1)
    even = rounded(taps[:, width : 2 * width] * slope(even_ref[...]))
    odd = taps[:, 2 * width :] + later(taps[:, :width], rims[1:2, :width])
    odd = rounded(odd * slope(odd_ref[...]))
    rim_slope = slope(rim_ref[...])
    inside = (places_ref[2] > 0).astype(F32)
    odd_before = rounded((rims[0:1, 2 * width :] + taps[0:1, :width]) * rim_slope[0:1] * inside)
    even_after = rounded(rims[1:2, width : 2 * width] * rim_slope[1:2])
    bias = jnp.sum(even + odd, axis=0, keepdims=True)
    both = jnp.concatenate([even, odd], axis=1).astype(BF)
    weight = product(window_ref[...], both, 0, 0)
    weight = weight[: 3 * bands, :width] + weight[bands:, width:]
    spare = held.shape[1] - 3 * width
    held[:bands, :] = jnp.concatenate(
        [weight[k * bands : (k + 1) * bands] for k in range(3)] + [jnp.zeros((bands, spare), F32)],
        axis=1,
    )
    last = jnp.concatenate(
        [project_ref[:, :width], project_ref[:, 2 * width :], bias, jnp.zeros((1, spare), F32)],
        axis=1,
    )
    blank = jnp.zeros((held.shape[0] - bands - 9, held.shape[1]), F32)
    held[bands:, :] = jnp.concatenate(
        [sums_ref[0:6, :], reduce_ref[...], expand_ref[...], last, blank], axis=0
    )
    before = earlier(odd, odd_before).astype(BF)
    following = later(even, even_after).astype(BF)
    even, odd = even.astype(BF), odd.astype(BF)
    back = [back_ref[k * width : (k + 1) * width, :] for k in range(3)]
    spectrum_out[:, :bands] = (
        product(before, back[0]) + product(even, back[1]) + product(odd, back[2])
    )
    spectrum_out[:, bands:] = (
        product(even, back[0]) + product(odd, back[1]) + product(following, back[2])
    )


def stem_back(places, grad, edges, matrix, even, odd, rim, window, back_matrix, *sums):
    frames, width = even.shape
    bands, model = back_matrix.shape[1], grad.shape[1]
    vmem = pl.BlockSpec(memory_space=pltpu.VMEM)
    return pl.pallas_call(
        functools.partial(stem_back_kernel, bands),
        in_specs=[pl.BlockSpec(memory_space=pltpu.SMEM)] + [vmem] * (8 + len(sums)),
        out_shape=[
            jax.ShapeDtypeStruct((bands + 16, model), F32),
            jax.ShapeDtypeStruct((frames, 2 * bands), F32),
        ],
        compiler_params=pltpu.CompilerParams(vmem_limit_bytes=VMEM_LIMIT),
        cost_estimate=SMALL,
        name="stem_back",
    )(places, grad, edges, matrix, even, odd, rim, window, back_matrix, *sums)


def on_device(
    spectrogram,
    first_kernel,
    first_bias,
    second_kernel,
    second_bias,
    attend_gain,
    attend_shift,
    project_weight,
    project_bias,
    output_weight,
    output_bias,
    mixer_gain,
    mixer_shift,
    expand_weight,
    expand_bias,
    reduce_weight,
    reduce_bias,
    cotangent,
):
    _, steps, bands = spectrogram.shape
    frames = steps // 2
    width = first_kernel.shape[2]
    model = second_kernel.shape[2]
    hidden = expand_weight.shape[1]
    mps, seqs = lax.axis_size("mp"), lax.axis_size("seq")
    z, seq = lax.axis_index("mp"), lax.axis_index("seq")
    core = lax.rem(seq, 2)
    rows = frames // mps

    dps = lax.axis_size("dp")
    part = hidden // (dps * seqs)
    start = (lax.axis_index("dp") * seqs + seq) * part
    bias_high = expand_bias.astype(BF)
    bias_low = (expand_bias - bias_high.astype(F32)).astype(BF)
    spare = -(2 * model + width + 2) % 128
    held = jnp.concatenate(
        [
            lax.dynamic_slice_in_dim(expand_weight.T, start, part, axis=0),
            lax.dynamic_slice_in_dim(reduce_weight, start, part, axis=0),
            lax.dynamic_slice_in_dim(output_weight.T, start, part, axis=0),
            lax.dynamic_slice_in_dim(
                jnp.stack([bias_high, bias_low], axis=1), start, part, axis=0
            ),
            jnp.zeros((part, spare), BF),
        ],
        axis=1,
    )
    weights_all = lax.all_gather(held, ("mp", "dp", "seq"), axis=0, tiled=True)

    paired = spectrogram.reshape(frames, 2 * bands)
    before = passed_along(paired[-1:], 1)
    following = passed_along(paired[:1], -1)
    ahead = jnp.concatenate([before, paired, following], axis=0)
    window = jnp.concatenate(
        [ahead[:-2, bands:], ahead[1:-1], ahead[2:, :bands]], axis=1
    )
    prior = jnp.concatenate([before, paired[:1, :bands]], axis=1)
    latter = jnp.concatenate([paired[-1:, bands:], following], axis=1)
    first_matrix = first_kernel.reshape(3 * bands, width)
    even_in = jnp.concatenate([window[:, : 3 * bands], latter], axis=0)
    odd_in = jnp.concatenate([prior, window[:, bands:]], axis=0)
    pre_even = product(even_in, first_matrix) + first_bias
    pre_odd = product(odd_in, first_matrix) + first_bias
    inside = jnp.logical_or(jnp.arange(frames + 1) > 0, seq > 0)[:, None]
    hidden_even = exact_gelu(pre_even[:frames]).astype(BF)
    hidden_odd = jnp.where(inside, exact_gelu(pre_odd), 0.0).astype(BF)
    taps = jnp.concatenate([hidden_odd[:frames], hidden_even, hidden_odd[1:]], axis=1)
    second_matrix = second_kernel.reshape(3 * width, model)
    stem_part = product(taps, second_matrix)
    stem_pre = scatter_sum(rolled_blocks(stem_part), "stem_sum") + second_bias
    resid_zero = exact_gelu(stem_pre) + sinusoid(seq * frames + z * rows, rows, model)
    normed_one = lax.all_gather(
        layer_norm(resid_zero, attend_gain, attend_shift).astype(BF), "mp", axis=0, tiled=True
    )

    project_matrix = project_weight.transpose(1, 2, 0).reshape(3 * width, model)
    offsets = jnp.concatenate([project_bias[0], jnp.zeros_like(project_bias[0]), project_bias[1]])
    packed = (product(normed_one, project_matrix, 1, 1) + offsets).astype(BF)
    own_cotangent = rolled_blocks(cotangent.reshape(frames, model))
    grad_mlp = jnp.concatenate(own_cotangent, axis=0).astype(BF)
    vectors = jnp.stack([output_bias, reduce_bias, mixer_gain, mixer_shift])
    reduce_bias_part = column_total(cotangent.reshape(frames, model).astype(BF))[None]
    back_matrix = jnp.transpose(first_kernel[::-1], (0, 2, 1)).reshape(3 * width, bands)
    rim = jnp.concatenate([pre_odd[:1], pre_even[frames:], jnp.zeros((6, width), F32)], axis=0)
    even_level, odd_level = pre_even[:frames], pre_odd[1:]
    early = (
        normed_one,
        own_cotangent[0],
        grad_mlp,
        vectors,
        reduce_bias_part,
        back_matrix,
        rim,
        even_level,
        odd_level,
        window,
        taps,
    )
    packed, early = lax.optimization_barrier((packed, early))
    (
        normed_one,
        own_cotangent,
        grad_mlp,
        vectors,
        reduce_bias_part,
        back_matrix,
        rim,
        even_level,
        odd_level,
        window,
        taps,
    ) = early
    query, pair = packed[:, :width], packed[:, width:]
    pair_far = swapped(pair, "seq", 2, "pair_far")
    pair_core = swapped(pair, "seq", 1, "pair_core")
    pair_far_core = swapped(pair_far, "seq", 1, "pair_far_core")
    attended, attended_turned, level = attend(query, [pair, pair_core, pair_far, pair_far_core])
    heads_got = exchange_mp(rolled_blocks(attended), "attended")
    resid_one, normed_two_own = join(z.reshape(1), weights_all, heads_got, resid_zero, vectors)
    normed_two_all = gather_mp(normed_two_own, "normed_two")
    shown_own, grad_resid_one, middle_sums, grad_heads = middle(
        z.reshape(1),
        weights_all,
        resid_one,
        normed_two_own,
        own_cotangent,
        vectors,
        mps,
        width,
    )
    shown = lax.all_gather(shown_own, "mp", axis=0, tiled=True)
    places = jnp.stack([z, core])
    grad_heads, normed_two_all = lax.optimization_barrier((grad_heads, normed_two_all))
    rows_got = exchange_mp([grad_heads[j] for j in range(mps)], "grad_heads")
    expand_weight_part, reduce_weight_part, expand_bias_part = feed(
        expand_weight,
        reduce_weight,
        expand_bias.reshape(1, hidden),
        after(grad_mlp, grad_heads),
        normed_two_all,
    )
    rows_got, expand_bias_part = lax.optimization_barrier((rows_got, expand_bias_part))
    grad_attended = natural([rows_got[-j % mps] for j in range(mps)])
    feed_sums = lax.psum((expand_weight_part, reduce_weight_part), ("dp", "seq"))

    query_grad, near, far, cores = attend_back(
        query,
        grad_attended,
        attended_turned,
        level,
        [pair, pair_core, pair_far, pair_far_core],
    )
    cores_got = swapped(cores, "seq", 1, "grad_core")
    far_got = swapped((far + cores_got[1].astype(F32)).astype(BF), "seq", 2, "grad_far")
    grad_packed, own_part, other_parts, project_columns = pack(
        z.reshape(1),
        query_grad, near, cores_got, far_got, project_matrix, mps
    )
    normed_got = exchange_mp(
        [own_part] + [other_parts[j] for j in range(mps - 1)], "grad_normed_one"
    )

    project_mine, project_other = project_weights(
        places, grad_packed, normed_one, attended, after(shown, grad_packed)
    )
    project_got = swapped(project_other, "seq", 1, "project_core")
    normed_got, project_got = lax.optimization_barrier((normed_got, project_got))

    grad_stem_own = pull(
        resid_zero, grad_resid_one, stem_pre, attend_gain.reshape(1, model), middle_sums, normed_got
    )
    project_mine = after(project_mine + project_got.astype(F32), grad_stem_own)
    project_piece = plane_scatter(project_mine, "project_scatter")
    with jax.named_scope("grad_stem"):
        gathered = lax.all_gather(grad_stem_own, "mp", axis=0, tiled=True)
    gathered, project_piece = lax.optimization_barrier((gathered, project_piece))
    grad_stem, small, second_mine, second_other = second_weight(places, taps, gathered, mps)
    stem_before = passed_along(grad_stem[-1:], 1)
    stem_following = passed_along(grad_stem[:1], -1)
    project_all = plane_gather(project_piece)
    second_got = swapped(second_other, "seq", 1, "second_core")
    edges = jnp.concatenate([stem_before, stem_following, jnp.zeros((14, model), BF)], axis=0)
    loose, spectrum_part = stem_back(
        jnp.stack([z, core, seq]),
        grad_stem,
        edges,
        second_matrix,
        even_level,
        odd_level,
        rim,
        window,
        back_matrix,
        small,
        reduce_bias_part,
        expand_bias_part,
        project_columns,
    )
    loose, feed_sums = lax.optimization_barrier((loose, feed_sums))
    loose_mine, loose_other = core_eighths(loose)
    loose_got = swapped(loose_other.astype(BF), "seq", 1, "small_core")
    spectrum_blocks = rolled_blocks(spectrum_part)
    spectrum_got = exchange_mp(
        [spectrum_blocks[0]] + [block.astype(BF) for block in spectrum_blocks[1:]], "spectrum"
    )

    parts = (second_mine + second_got.astype(F32), loose_mine + loose_got.astype(F32))
    joined = jnp.concatenate([part.reshape(4, -1, model) for part in parts], axis=1)
    piece = plane_scatter(joined.reshape(-1, model), "last_scatter")
    encoded = shown[:, model:].astype(F32)
    expand_sum, reduce_sum = [value.astype(F32) for value in feed_sums]
    piece, spectrum_got, encoded, expand_sum, reduce_sum, project_all = lax.optimization_barrier(
        (piece, spectrum_got, encoded, expand_sum, reduce_sum, project_all)
    )
    spectrum_own = total(spectrum_got).astype(BF)
    spectrum_all = gather_mp(spectrum_own, "spectrum_back")
    with jax.named_scope("last_gather"):
        last = plane_gather(piece)
    spectrogram_gradient = natural(spectrum_all).astype(F32).reshape(1, steps, bands)
    project_sum = project_all[: 3 * width].astype(F32)
    output_sum = project_all[3 * width :].astype(F32)
    rows_of = (model, model, model, model, model, model, model, hidden)
    cuts = tuple((row, 0, size) for row, size in enumerate(rows_of))
    cuts += ((8, 0, 2 * width), (8, 2 * width, 3 * width))
    second_sum, first_sum, *sums = finish(last, bands, bands + 16, width, cuts)
    return (
        encoded.reshape(1, frames, model),
        spectrogram_gradient,
        first_sum.reshape(3, bands, width),
        sums[9],
        second_sum.reshape(3, width, model),
        sums[5],
        sums[0],
        sums[1],
        project_sum.T.reshape(model, 3, width),
        sums[8].reshape(2, width),
        output_sum,
        sums[4],
        sums[2],
        sums[3],
        expand_sum,
        sums[7],
        reduce_sum,
        sums[6],
    )


def solution(mesh):
    return jax.shard_map(
        on_device,
        mesh=mesh,
        in_specs=(
            P("dp", "seq", None),
            P(None, None, "mp"),
            P("mp"),
            P(None, "mp", None),
            P(),
            P(),
            P(),
            P(None, None, "mp"),
            P(None, "mp"),
            P("mp", None),
            P(),
            P(),
            P(),
            P(None, "mp"),
            P("mp"),
            P("mp", None),
            P(),
            P("dp", "seq", None),
        ),
        out_specs=(
            P("dp", "seq", None),
            P("dp", "seq", None),
            P(None, None, "mp"),
            P("mp"),
            P(None, "mp", None),
            P(),
            P(),
            P(),
            P(None, None, "mp"),
            P(None, "mp"),
            P("mp", None),
            P(),
            P(),
            P(),
            P(None, "mp"),
            P("mp"),
            P("mp", None),
            P(),
        ),
        check_vma=False,
    )
```

```python
import functools
import math

import jax
import jax.numpy as jnp
from jax import lax
from jax.experimental import pallas as pl
from jax.experimental.pallas import tpu as pltpu
from jax.sharding import PartitionSpec as P

HEAD_DIM = 64
BF = jnp.bfloat16
F32 = jnp.float32
VMEM_LIMIT = 60 * 1024 * 1024
SMALL = pl.CostEstimate(flops=1, bytes_accessed=1, transcendentals=0)


def product(left, right, left_dim=1, right_dim=0):
    dims = (((left_dim,), (right_dim,)), ((), ()))
    return lax.dot_general(left, right, dims, preferred_element_type=F32)


def after(value, *others):
    return lax.optimization_barrier((value, *others))[0]


def exact_gelu(value):
    return jax.nn.gelu(value, approximate=False)


def gelu_back(value, grad):
    return jax.vjp(exact_gelu, value)[1](grad)[0]


def layer_norm(value, gain, shift):
    centre = value - jnp.mean(value, axis=-1, keepdims=True)
    spread = jnp.mean(centre * centre, axis=-1, keepdims=True)
    return centre * lax.rsqrt(spread + 1e-05) * gain + shift


def norm_back(value, gain, grad):
    centre = value - jnp.mean(value, axis=-1, keepdims=True)
    spread = jnp.mean(centre * centre, axis=-1, keepdims=True)
    inverse = lax.rsqrt(spread + 1e-05)
    xhat = centre * inverse
    e = grad * gain
    back = (
        e - jnp.mean(e, axis=-1, keepdims=True) - xhat * jnp.mean(e * xhat, axis=-1, keepdims=True)
    ) * inverse
    return back, jnp.sum(grad * xhat, axis=0), jnp.sum(grad, axis=0)


def column_total(value):
    return jnp.sum(value.astype(F32), axis=0)


def sinusoid(start, count, width):
    half = width // 2
    rates = jnp.exp(jnp.arange(half, dtype=F32) * (-math.log(10000.0) / (half - 1)))
    times = (start + jnp.arange(count)).astype(F32)
    angles = times[:, None] * rates[None, :]
    return jnp.concatenate([jnp.sin(angles), jnp.cos(angles)], axis=1)


def turned(size, by):
    return [(i, (i + by) % size) for i in range(size)]


def gather_mp(block, name):
    size = lax.axis_size("mp")
    with jax.named_scope(name):
        return [block] + [lax.ppermute(block, "mp", turned(size, -j)) for j in range(1, size)]


def exchange_mp(blocks, name):
    size = lax.axis_size("mp")
    with jax.named_scope(name):
        got = [lax.ppermute(blocks[j], "mp", turned(size, j)) for j in range(1, size)]
    return [blocks[0]] + got


def row_blocks(value, count):
    rows = value.shape[0] // count
    return [value[j * rows : (j + 1) * rows] for j in range(count)]


def rolled_blocks(value):
    size, z = lax.axis_size("mp"), lax.axis_index("mp")
    rows = value.shape[0] // size
    return [
        lax.dynamic_slice_in_dim(value, lax.rem(z + j, size) * rows, rows, axis=0)
        for j in range(size)
    ]


def natural(blocks):
    size, z = lax.axis_size("mp"), lax.axis_index("mp")
    rows = blocks[0].shape[0]
    twice = jnp.concatenate(blocks + blocks, axis=0)
    return lax.dynamic_slice_in_dim(twice, lax.rem(size - z, size) * rows, rows * size, axis=0)


def total(parts):
    result = parts[0].astype(F32)
    for part in parts[1:]:
        result = result + part.astype(F32)
    return result


def scatter_sum(blocks, name):
    return total(exchange_mp([blocks[0]] + [block.astype(BF) for block in blocks[1:]], name))


def swapped(value, axis, bit, name):
    size = lax.axis_size(axis)
    with jax.named_scope(name):
        return lax.ppermute(value, axis, [(i, i ^ bit) for i in range(size)])


def passed_along(value, by):
    size = lax.axis_size("seq")
    pairs = [(i, i + by) for i in range(size) if 0 <= i + by < size]
    return lax.ppermute(value, "seq", pairs)


def plane_index():
    return lax.rem(lax.axis_index("dp"), 2) * 2 + lax.div(lax.axis_index("seq"), 2)


def plane_move(value, d, name):
    dps, seqs = lax.axis_size("dp"), lax.axis_size("seq")
    pairs = [
        (p * seqs + s, (p ^ (d >> 1)) * seqs + (s ^ (2 * (d & 1))))
        for p in range(dps)
        for s in range(seqs)
    ]
    with jax.named_scope(name):
        return lax.ppermute(value, ("dp", "seq"), pairs)


def rest_of_dp(value):
    dps = lax.axis_size("dp")
    if dps > 2:
        groups = [[i for i in range(dps) if i % 2 == bit] for bit in range(2)]
        value = lax.psum(value, "dp", axis_index_groups=groups)
    return value


def plane_scatter(quarters, name):
    index = plane_index()

    def piece(d):
        return lax.dynamic_index_in_dim(quarters, jnp.bitwise_xor(index, d), 0, keepdims=False)

    got = [plane_move(piece(d).astype(BF), d, name) for d in (1, 2, 3)]
    return rest_of_dp(total([piece(0)] + got).astype(BF))


def plane_gather(piece):
    dps = lax.axis_size("dp")
    if dps == 2:
        return lax.all_gather(piece, ("dp", "seq"), axis=0, tiled=True)
    pairs = [[i, i + 1] for i in range(0, dps, 2)]
    return lax.all_gather(
        lax.all_gather(piece, "seq", axis=0, tiled=True),
        "dp",
        axis=0,
        tiled=True,
        axis_index_groups=pairs,
    )


def core_rows(held, core, mine_out, other_out, start=0):
    rows = held.shape[0] // 8
    mine, others = [], []
    for quarter in range(4):
        here = pl.ds(pl.multiple_of((2 * quarter + core) * rows, rows), rows)
        there = pl.ds(pl.multiple_of((2 * quarter + 1 - core) * rows, rows), rows)
        mine.append(held[here, :])
        others.append(held[there, :])
    place = slice(start, start + 4 * rows)
    mine_out[place, :] = jnp.concatenate(mine, axis=0).astype(mine_out.dtype)
    other_out[place, :] = jnp.concatenate(others, axis=0).astype(BF)


def finish_wide_kernel(wide_ref, expand_out, reduce_out, project_out, output_out):
    part = expand_out.shape[0] // 8
    split = project_out.shape[0] // part
    for p in range(8):
        here = slice(p * part, (p + 1) * part)
        block = wide_ref[3 * p * part : 3 * (p + 1) * part, :].astype(F32)
        expand_out[here, :] = block[:part]
        reduce_out[here, :] = block[part : 2 * part]
        if p < split:
            project_out[here, :] = block[2 * part :]
        else:
            output_out[(p - split) * part : (p - split + 1) * part, :] = block[2 * part :]


def finish_wide(wide, width):
    model = wide.shape[1]
    return pl.pallas_call(
        finish_wide_kernel,
        out_shape=[
            jax.ShapeDtypeStruct((rows, model), F32) for rows in (model, model, 3 * width, width)
        ],
        compiler_params=pltpu.CompilerParams(vmem_limit_bytes=VMEM_LIMIT),
        cost_estimate=SMALL,
        name="finish_wide",
    )(wide)


def finish_kernel(bands, loose, vectors, gathered_ref, second_out, first_out, *refs):
    outs, (whole, small) = refs[:-2], refs[-2:]
    eighth = gathered_ref.shape[1]
    rows, few = eighth - loose // 8, loose // 8
    for p in range(8):
        whole[...] = gathered_ref[p].astype(F32)
        second_out[p * rows : (p + 1) * rows, :] = whole[:rows, :]
        small[p * few : (p + 1) * few, :] = whole[rows:, :]
    width = first_out.shape[1]
    for tap in range(3):
        first_out[tap * bands : (tap + 1) * bands, :] = small[
            :bands, tap * width : (tap + 1) * width
        ]
    for out, (row, start, stop) in zip(outs, vectors):
        if out.ndim == 1:
            out[...] = small[bands + row, start:stop]
        else:
            for k in range(out.shape[0]):
                place = start + k * width
                out[k : k + 1, :] = small[bands + row : bands + row + 1, place : place + width]


def finish(gathered, bands, loose, width, vectors):
    _, rows, model = gathered.shape
    return pl.pallas_call(
        functools.partial(finish_kernel, bands, loose, vectors),
        out_shape=[
            jax.ShapeDtypeStruct((8 * rows - loose, model), F32),
            jax.ShapeDtypeStruct((3 * bands, width), F32),
        ]
        + [
            jax.ShapeDtypeStruct(
                (2, width) if stop - start == 2 * width else (stop - start,), F32
            )
            for _, start, stop in vectors
        ],
        scratch_shapes=[pltpu.VMEM((rows, model), F32), pltpu.VMEM((loose, model), F32)],
        compiler_params=pltpu.CompilerParams(vmem_limit_bytes=VMEM_LIMIT),
        cost_estimate=SMALL,
        name="finish",
    )(gathered)


def spectrum_kernel(place_ref, *refs):
    parts, (out_ref, held) = refs[:-2], refs[-2:]
    for j, part in enumerate(parts):
        held[lax.rem(place_ref[0] + j, len(parts))] = part[...].astype(F32)
    result = held[0]
    for j in range(1, len(parts)):
        result = result + held[j]
    out_ref[...] = result


def spectrum_sum(place, parts):
    vmem = pl.BlockSpec(memory_space=pltpu.VMEM)
    shape = parts[0].shape
    return pl.pallas_call(
        spectrum_kernel,
        in_specs=[pl.BlockSpec(memory_space=pltpu.SMEM)] + [vmem] * len(parts),
        out_shape=jax.ShapeDtypeStruct(shape, F32),
        scratch_shapes=[pltpu.VMEM((len(parts), *shape), F32)],
        compiler_params=pltpu.CompilerParams(vmem_limit_bytes=VMEM_LIMIT),
        cost_estimate=SMALL,
        name="spectrum_sum",
    )(place, *parts)


def attend_kernel(heads, scale, query_ref, *refs):
    pair_refs, (out_ref, turned_ref, level_ref, held) = refs[:-4], refs[-4:]
    width = heads * HEAD_DIM
    count = pair_refs[0].shape[0]
    outs, levels = [], []
    for head in range(heads):
        cols = slice(head * HEAD_DIM, (head + 1) * HEAD_DIM)
        query = query_ref[:, cols]
        top = None
        for index, pair in enumerate(pair_refs):
            scores = product(pair[:, cols], query, 1, 1) * scale
            held[index * count : (index + 1) * count, :] = scores
            high = jnp.max(scores, axis=0, keepdims=True)
            top = high if top is None else jnp.maximum(top, high)
        weight, out = 0.0, 0.0
        vcols = slice(width + head * HEAD_DIM, width + (head + 1) * HEAD_DIM)
        for index, pair in enumerate(pair_refs):
            soft = jnp.exp(held[index * count : (index + 1) * count, :] - top)
            weight = weight + jnp.sum(soft, axis=0, keepdims=True)
            out = out + product(pair[:, vcols], soft.astype(BF), 0, 0)
        outs.append(out / weight)
        levels.append(top + jnp.log(weight))
    joined = jnp.concatenate(outs, axis=0)
    turned_ref[...] = joined
    out_ref[...] = joined.T.astype(BF)
    level_ref[...] = jnp.concatenate(levels, axis=0)


def attend(query, pairs):
    rows, width = query.shape
    heads = width // HEAD_DIM
    keys = rows * len(pairs)
    return pl.pallas_call(
        functools.partial(attend_kernel, heads, HEAD_DIM ** (-0.5)),
        out_shape=[
            jax.ShapeDtypeStruct((rows, width), BF),
            jax.ShapeDtypeStruct((width, rows), F32),
            jax.ShapeDtypeStruct((heads, rows), F32),
        ],
        scratch_shapes=[pltpu.VMEM((keys, rows), F32)],
        compiler_params=pltpu.CompilerParams(vmem_limit_bytes=VMEM_LIMIT),
        cost_estimate=SMALL,
        name="attend",
    )(query, *pairs)


def attend_back_kernel(heads, scale, query_ref, grad_ref, turned_ref, level_ref, *refs):
    pair_refs, (query_out, near_out, far_out, core_out) = refs[:4], refs[4:]
    width = heads * HEAD_DIM
    grads_turned = grad_ref[...].astype(F32).T
    query_grads = []
    pair_grads = [([], []) for _ in range(4)]
    for head in range(heads):
        cols = slice(head * HEAD_DIM, (head + 1) * HEAD_DIM)
        vcols = slice(width + head * HEAD_DIM, width + (head + 1) * HEAD_DIM)
        query = query_ref[:, cols]
        grad = grad_ref[:, cols]
        level = level_ref[head : head + 1, :]
        delta = jnp.sum(grads_turned[cols, :] * turned_ref[cols, :], axis=0, keepdims=True)
        query_grad = 0.0
        for index in range(4):
            pair = pair_refs[index]
            key = pair[:, cols]
            soft = jnp.exp(product(key, query, 1, 1) * scale - level)
            grad_soft = product(pair[:, vcols], grad, 1, 1)
            low = (soft * (grad_soft - delta)).astype(BF)
            pair_grads[index][0].append(product(low, query) * scale)
            pair_grads[index][1].append(product(soft.astype(BF), grad))
            query_grad = query_grad + product(key, low, 0, 0)
        query_grads.append(query_grad * scale)
    query_out[...] = jnp.concatenate(query_grads, axis=0).T.astype(BF)
    near, near_core, far, far_core = [
        jnp.concatenate(keys + values, axis=1) for keys, values in pair_grads
    ]
    near_out[...] = near.astype(BF)
    far_out[...] = far.astype(BF)
    core_out[0] = near_core.astype(BF)
    core_out[1] = far_core.astype(BF)


def attend_back(query, grad, turned_out, level, pairs):
    rows, width = query.shape
    heads = width // HEAD_DIM
    return pl.pallas_call(
        functools.partial(attend_back_kernel, heads, HEAD_DIM ** (-0.5)),
        out_shape=[
            jax.ShapeDtypeStruct((rows, width), BF),
            jax.ShapeDtypeStruct((rows, 2 * width), BF),
            jax.ShapeDtypeStruct((rows, 2 * width), BF),
            jax.ShapeDtypeStruct((2, rows, 2 * width), BF),
        ],
        compiler_params=pltpu.CompilerParams(vmem_limit_bytes=VMEM_LIMIT),
        cost_estimate=SMALL,
        name="attend_back",
    )(query, grad, turned_out, level, *pairs)


def gelu_parts(value):
    share = 0.5 + 0.5 * lax.erf(value * math.sqrt(0.5))
    slope = share + value * jnp.exp(-0.5 * value * value) * (1.0 / math.sqrt(2.0 * math.pi))
    return value * share, slope


def across_of(weights_ref, j, mps, width):
    rows = weights_ref.shape[0] // (8 * mps)
    places = [(p * mps + j % mps) * rows for p in range(8)]
    return jnp.concatenate([weights_ref[place : place + rows, :width] for place in places], axis=0)


def norm_parts(value):
    centre = value - jnp.mean(value, axis=-1, keepdims=True)
    inverse = lax.rsqrt(jnp.mean(centre * centre, axis=-1, keepdims=True) + 1e-05)
    return centre * inverse, inverse


def norm_pull(grad, gain, xhat, inverse):
    e = grad * gain
    shared = jnp.mean(e, axis=-1, keepdims=True) + xhat * jnp.mean(e * xhat, axis=-1, keepdims=True)
    return (e - shared) * inverse


def join_kernel(weights_ref, resid_ref, vectors_ref, *refs):
    heads_refs, (resid_out, normed_out) = refs[:-2], refs[-2:]
    mps, width = len(heads_refs), heads_refs[0].shape[1]
    resid = resid_ref[...] + vectors_ref[0:1, :]
    for j in range(mps):
        part = across_of(weights_ref, -j, mps, width)
        resid = resid + product(heads_refs[j][...], part, 1, 1)
    resid_out[...] = resid
    xhat, _ = norm_parts(resid)
    normed_out[...] = (xhat * vectors_ref[2:3, :] + vectors_ref[3:4, :]).astype(BF)


def join(weights, heads, resid, vectors):
    rows, model = resid.shape
    wide = weights.shape[1] % 256 + 256 if weights.shape[1] % 256 else 256
    vmem = pl.BlockSpec(memory_space=pltpu.VMEM)
    return pl.pallas_call(
        join_kernel,
        grid=(1,),
        in_specs=[
            pl.BlockSpec((weights.shape[0], wide), lambda i: (0, weights.shape[1] // wide - 1)),
        ]
        + [vmem] * (2 + len(heads)),
        out_specs=[vmem, vmem],
        out_shape=[
            jax.ShapeDtypeStruct((rows, model), F32),
            jax.ShapeDtypeStruct((rows, model), BF),
        ],
        compiler_params=pltpu.CompilerParams(vmem_limit_bytes=VMEM_LIMIT),
        cost_estimate=SMALL,
        name="join",
    )(weights, resid, vectors, *heads)


def middle_kernel(
    mps,
    width,
    weights_ref,
    across_ref,
    resid_ref,
    normed_ref,
    cotangent_ref,
    vectors_ref,
    shown_ref,
    grad_ref,
    sums_ref,
    *refs,
):
    grad_heads_refs, (forward, backward) = refs[:mps], refs[mps:]
    rows, model = resid_ref.shape
    step = pl.program_id(0)

    @pl.when(step == 0)
    def _():
        forward[...] = jnp.zeros_like(forward)
        backward[...] = jnp.zeros_like(backward)

    expand = weights_ref[:, :model]
    reduce = weights_ref[:, model : 2 * model]
    tail = weights_ref[:, weights_ref.shape[1] - 128 :]
    lane = lax.broadcasted_iota(jnp.int32, (rows, 128), 1)
    bias_lane = 2 * model + width - (weights_ref.shape[1] - 128)
    ones = jnp.where(jnp.logical_or(lane == bias_lane, lane == bias_lane + 1), 1.0, 0.0).astype(BF)
    value = product(normed_ref[...], expand, 1, 1) + product(ones, tail, 1, 1)
    active, slope = gelu_parts(value)
    forward[...] += product(active.astype(BF), reduce)
    grad_mlp = cotangent_ref[...].astype(BF)
    grad = (product(grad_mlp, reduce, 1, 1) * slope).astype(BF)
    backward[...] += product(grad, expand)

    @pl.when(step == pl.num_programs(0) - 1)
    def _():
        resid = resid_ref[...]
        shown_ref[:, model:] = (resid + forward[...] + vectors_ref[1:2, :]).astype(BF)
        xhat, inverse = norm_parts(resid)
        grad = backward[...]
        grad_resid = cotangent_ref[...] + norm_pull(grad, vectors_ref[2:3, :], xhat, inverse)
        grad_ref[...] = grad_resid
        attn = grad_resid.astype(BF)
        shown_ref[:, :model] = attn
        sums_ref[...] = jnp.concatenate(
            [
                jnp.sum(grad * xhat, axis=0, keepdims=True),
                jnp.sum(grad, axis=0, keepdims=True),
                jnp.sum(attn.astype(F32), axis=0, keepdims=True),
                jnp.zeros((5, model), F32),
            ],
            axis=0,
        )
        for j in range(mps):
            part = across_of(across_ref, j, mps, width)
            grad_heads_refs[j][...] = product(attn, part).astype(BF)


def middle(weights, resid, normed, cotangent, vectors, mps, width):
    rows, model = resid.shape
    wide = weights.shape[1] % 256 + 256 if weights.shape[1] % 256 else 256
    chunk = 512
    vmem = pl.BlockSpec(memory_space=pltpu.VMEM)
    return pl.pallas_call(
        functools.partial(middle_kernel, mps, width),
        grid=(weights.shape[0] // chunk,),
        in_specs=[
            pl.BlockSpec((chunk, weights.shape[1]), lambda i: (i, 0)),
            pl.BlockSpec((weights.shape[0], wide), lambda i: (0, weights.shape[1] // wide - 1)),
        ]
        + [vmem] * 4,
        out_specs=[vmem] * (3 + mps),
        out_shape=[
            jax.ShapeDtypeStruct((rows, 2 * model), BF),
            jax.ShapeDtypeStruct((rows, model), F32),
            jax.ShapeDtypeStruct((8, model), F32),
        ]
        + [jax.ShapeDtypeStruct((rows, width), BF)] * mps,
        scratch_shapes=[pltpu.VMEM((rows, model), F32)] * 2,
        compiler_params=pltpu.CompilerParams(vmem_limit_bytes=VMEM_LIMIT),
        cost_estimate=SMALL,
        name="middle",
    )(weights, weights, resid, normed, cotangent, vectors)


def feed_kernel(chunk, places_ref, expand_ref, reduce_ref, bias_ref, grad_ref, *refs):
    normed_refs, refs = refs[:-7], refs[-7:]
    mine_out, other_out, bias_out, normed, normed_turned, held, second_held = refs
    rows = normed_refs[0].shape[0]
    for j, ref in enumerate(normed_refs):
        normed[j * rows : (j + 1) * rows, :] = ref[...]
    normed_turned[...] = normed[...].T
    hidden = expand_ref.shape[1]
    for start in range(0, hidden, chunk):
        here = slice(start, start + chunk)
        value = product(normed[...], expand_ref[:, here]) + bias_ref[:, here]
        active, slope = gelu_parts(value)
        grad = product(grad_ref[...], reduce_ref[here, :], 1, 1) * slope
        low = grad.astype(BF)
        second_held[here, :] = product(active.astype(BF), grad_ref[...], 0, 0)
        held[:, here] = product(normed_turned[...], low)
        bias_out[:, here] = jnp.sum(low.astype(F32), axis=0, keepdims=True)
    core_rows(held, places_ref[1], mine_out, other_out)
    core_rows(second_held, places_ref[1], mine_out, other_out, held.shape[0] // 2)


def feed(places, expand, reduce, bias, grad, normed_blocks):
    model, hidden = expand.shape
    rows = grad.shape[0]
    vmem = pl.BlockSpec(memory_space=pltpu.VMEM)
    half = (model + hidden) // 2
    return pl.pallas_call(
        functools.partial(feed_kernel, 256),
        in_specs=[pl.BlockSpec(memory_space=pltpu.SMEM)] + [vmem] * (4 + len(normed_blocks)),
        out_shape=[
            jax.ShapeDtypeStruct((half, model), BF),
            jax.ShapeDtypeStruct((half, model), BF),
            jax.ShapeDtypeStruct((1, hidden), F32),
        ],
        scratch_shapes=[
            pltpu.VMEM((rows, model), BF),
            pltpu.VMEM((model, rows), BF),
            pltpu.VMEM((model, hidden), F32),
            pltpu.VMEM((hidden, model), F32),
        ],
        compiler_params=pltpu.CompilerParams(vmem_limit_bytes=VMEM_LIMIT),
        cost_estimate=SMALL,
        name="feed",
    )(places, expand, reduce, bias, grad, *normed_blocks)


def project_kernel(places_ref, packed_ref, normed_ref, attended_ref, attn_ref, *refs):
    mine_out, other_out, held = refs
    wide = packed_ref.shape[1]
    held[:wide, :] = product(packed_ref[...], normed_ref[...], 0, 0)
    held[wide:, :] = product(attended_ref[...], attn_ref[...], 0, 0)
    core_rows(held, places_ref[1], mine_out, other_out)


def project_weights(places, packed, normed, attended, shown):
    frames, wide = packed.shape
    width, model = attended.shape[1], normed.shape[1]
    vmem = pl.BlockSpec(memory_space=pltpu.VMEM)
    half = (wide + width) // 2
    return pl.pallas_call(
        project_kernel,
        grid=(1,),
        in_specs=[pl.BlockSpec(memory_space=pltpu.SMEM)]
        + [vmem] * 3
        + [pl.BlockSpec((frames, model), lambda i: (0, 0))],
        out_specs=[vmem, vmem],
        out_shape=[jax.ShapeDtypeStruct((half, model), BF)] * 2,
        scratch_shapes=[pltpu.VMEM((wide + width, model), F32)],
        compiler_params=pltpu.CompilerParams(vmem_limit_bytes=VMEM_LIMIT),
        cost_estimate=SMALL,
        name="project_weights",
    )(places, packed, normed, attended, shown)


def pieces_kernel(places_ref, feed_ref, feed_got_ref, project_ref, project_got_ref, *outs):
    part = project_ref.shape[0] // 4
    pairs = (
        (feed_ref, feed_got_ref, 0),
        (feed_ref, feed_got_ref, 4 * part),
        (project_ref, project_got_ref, 0),
    )
    for d, out in enumerate(outs):
        for which, (mine, got, start) in enumerate(pairs):
            place = start + jnp.bitwise_xor(places_ref[3], d) * part
            here = pl.ds(pl.multiple_of(place, part), part)
            value = mine[here, :].astype(F32) + got[here, :].astype(F32)
            out[which * part : (which + 1) * part, :] = value.astype(out.dtype)


def pieces(places, feed_mine, feed_got, project_mine, project_got):
    vmem = pl.BlockSpec(memory_space=pltpu.VMEM)
    model = feed_mine.shape[1]
    part = 3 * project_mine.shape[0] // 4
    return pl.pallas_call(
        pieces_kernel,
        in_specs=[pl.BlockSpec(memory_space=pltpu.SMEM)] + [vmem] * 4,
        out_shape=[jax.ShapeDtypeStruct((part, model), F32)]
        + [jax.ShapeDtypeStruct((part, model), BF)] * 3,
        compiler_params=pltpu.CompilerParams(vmem_limit_bytes=VMEM_LIMIT),
        cost_estimate=SMALL,
        name="pieces",
    )(places, feed_mine, feed_got, project_mine, project_got)


def pack_kernel(place_ref, query_ref, pair_ref, core_ref, other_ref, weight_ref, *outs):
    packed_out, sums_out, own_out, *others_out = outs
    pair = pair_ref[...].astype(F32) + core_ref[0].astype(F32) + other_ref[...].astype(F32)
    packed = jnp.concatenate([query_ref[...], pair.astype(BF)], axis=1)
    packed_out[...] = packed
    sums_out[...] = jnp.sum(packed.astype(F32), axis=0, keepdims=True)
    rows = own_out.shape[0]
    mps = len(others_out) + 1

    def part(j):
        start = pl.multiple_of(lax.rem(place_ref[0] + j, mps) * rows, rows)
        return product(packed_out[pl.ds(start, rows), :], weight_ref[...])

    own_out[...] = part(0)
    for j in range(1, mps):
        others_out[j - 1][...] = part(j).astype(BF)


def pack(place, query, pair, pair_core, pair_far, weight, mps):
    frames, width = query.shape
    model, rows = weight.shape[1], frames // mps
    vmem = pl.BlockSpec(memory_space=pltpu.VMEM)
    return pl.pallas_call(
        pack_kernel,
        grid=(1,),
        in_specs=[
            pl.BlockSpec(memory_space=pltpu.SMEM),
            vmem,
            vmem,
            pl.BlockSpec((1, frames, 2 * width), lambda i: (0, 0, 0)),
            vmem,
            vmem,
        ],
        out_specs=[vmem] * (2 + mps),
        out_shape=[
            jax.ShapeDtypeStruct((frames, 3 * width), BF),
            jax.ShapeDtypeStruct((1, 3 * width), F32),
            jax.ShapeDtypeStruct((rows, model), F32),
        ]
        + [jax.ShapeDtypeStruct((rows, model), BF)] * (mps - 1),
        compiler_params=pltpu.CompilerParams(vmem_limit_bytes=VMEM_LIMIT),
        cost_estimate=SMALL,
        name="pack",
    )(place, query, pair, pair_core, pair_far, weight)


def pull_kernel(resid_ref, grad_ref, stem_ref, gain_ref, sums_ref, *refs):
    got_refs, out_ref = refs[:-1], refs[-1]
    rows, model = resid_ref.shape
    grad = got_refs[0][...].astype(F32)
    for ref in got_refs[1:]:
        grad = grad + ref[...].astype(F32)
    xhat, inverse = norm_parts(resid_ref[...])
    grad_resid = grad_ref[...] + norm_pull(grad, gain_ref[...], xhat, inverse)
    _, slope = gelu_parts(stem_ref[...])
    low = (grad_resid * slope).astype(BF)
    out_ref[:rows, :] = low
    sums = jnp.concatenate(
        [
            jnp.sum(grad * xhat, axis=0, keepdims=True),
            jnp.sum(grad, axis=0, keepdims=True),
            sums_ref[0:3, :],
            jnp.sum(low.astype(F32), axis=0, keepdims=True),
            jnp.zeros((10, model), F32),
        ],
        axis=0,
    )
    out_ref[rows:, :] = sums.astype(BF)


def pull(resid, grad, stem, gain, sums, got):
    rows, model = resid.shape
    return pl.pallas_call(
        pull_kernel,
        out_shape=jax.ShapeDtypeStruct((rows + 16, model), BF),
        compiler_params=pltpu.CompilerParams(vmem_limit_bytes=VMEM_LIMIT),
        cost_estimate=SMALL,
        name="pull",
    )(resid, grad, stem, gain, sums, *got)


def second_kernel_body(mps, places_ref, taps_ref, gathered_ref, *refs):
    grad_out, sums_out, mine_out, other_out, held = refs
    rows = gathered_ref.shape[0] // mps
    own = rows - 16
    sums = 0.0
    for j in range(mps):
        grad_out[j * own : (j + 1) * own, :] = gathered_ref[j * rows : j * rows + own, :]
        sums = sums + gathered_ref[j * rows + own : (j + 1) * rows, :].astype(F32)
    sums_out[...] = sums
    held[...] = product(taps_ref[...], grad_out[...], 0, 0)
    core_rows(held, places_ref[1], mine_out, other_out)


def second_weight(places, taps, gathered, mps):
    frames, tall = taps.shape
    model = gathered.shape[1]
    vmem = pl.BlockSpec(memory_space=pltpu.VMEM)
    return pl.pallas_call(
        functools.partial(second_kernel_body, mps),
        in_specs=[pl.BlockSpec(memory_space=pltpu.SMEM)] + [vmem] * 2,
        out_shape=[
            jax.ShapeDtypeStruct((frames, model), BF),
            jax.ShapeDtypeStruct((16, model), F32),
            jax.ShapeDtypeStruct((tall // 2, model), F32),
            jax.ShapeDtypeStruct((tall // 2, model), BF),
        ],
        scratch_shapes=[pltpu.VMEM((tall, model), F32)],
        compiler_params=pltpu.CompilerParams(vmem_limit_bytes=VMEM_LIMIT),
        cost_estimate=SMALL,
        name="second_weight",
    )(places, taps, gathered)


def stem_back_kernel(
    bands,
    places_ref,
    grad_ref,
    edges_ref,
    matrix_ref,
    even_ref,
    odd_ref,
    rim_ref,
    window_ref,
    back_ref,
    sums_ref,
    reduce_ref,
    expand_ref,
    project_ref,
    loose_out,
    spectrum_out,
    held,
):
    frames = grad_ref.shape[0]
    width = even_ref.shape[1]
    row = lax.broadcasted_iota(jnp.int32, (frames, width), 0)

    def later(value, last):
        return jnp.where(row == frames - 1, last, pltpu.roll(value, frames - 1, 0))

    def earlier(value, start):
        return jnp.where(row == 0, start, pltpu.roll(value, 1, 0))

    def slope(value):
        return gelu_parts(value)[1]

    def rounded(value):
        return value.astype(BF).astype(F32)

    taps = product(grad_ref[...], matrix_ref[...], 1, 1)
    rims = product(edges_ref[...], matrix_ref[...], 1, 1)
    even = rounded(taps[:, width : 2 * width] * slope(even_ref[...]))
    odd = taps[:, 2 * width :] + later(taps[:, :width], rims[1:2, :width])
    odd = rounded(odd * slope(odd_ref[...]))
    rim_slope = slope(rim_ref[...])
    inside = (places_ref[2] > 0).astype(F32)
    odd_before = rounded((rims[0:1, 2 * width :] + taps[0:1, :width]) * rim_slope[0:1] * inside)
    even_after = rounded(rims[1:2, width : 2 * width] * rim_slope[1:2])
    bias = jnp.sum(even + odd, axis=0, keepdims=True)
    both = jnp.concatenate([even, odd], axis=1).astype(BF)
    weight = product(window_ref[...], both, 0, 0)
    weight = weight[: 3 * bands, :width] + weight[bands:, width:]
    spare = held.shape[1] - 3 * width
    held[:bands, :] = jnp.concatenate(
        [weight[k * bands : (k + 1) * bands] for k in range(3)] + [jnp.zeros((bands, spare), F32)],
        axis=1,
    )
    last = jnp.concatenate(
        [project_ref[:, :width], project_ref[:, 2 * width :], bias, jnp.zeros((1, spare), F32)],
        axis=1,
    )
    blank = jnp.zeros((held.shape[0] - bands - 9, held.shape[1]), F32)
    held[bands:, :] = jnp.concatenate(
        [sums_ref[0:6, :], reduce_ref[...], expand_ref[...], last, blank], axis=0
    )
    few = loose_out.shape[1]
    for p in range(8):
        loose_out[p] = held[p * few : (p + 1) * few, :]
    before = earlier(odd, odd_before).astype(BF)
    following = later(even, even_after).astype(BF)
    even, odd = even.astype(BF), odd.astype(BF)
    back = [back_ref[k * width : (k + 1) * width, :] for k in range(3)]
    spectrum = [
        product(before, back[0]) + product(even, back[1]) + product(odd, back[2]),
        product(even, back[0]) + product(odd, back[1]) + product(following, back[2]),
    ]
    spectrum_out[...] = jnp.concatenate(spectrum, axis=1).astype(BF)


def stem_back(places, grad, edges, matrix, even, odd, rim, window, back_matrix, *sums):
    frames, width = even.shape
    bands, model = back_matrix.shape[1], grad.shape[1]
    vmem = pl.BlockSpec(memory_space=pltpu.VMEM)
    return pl.pallas_call(
        functools.partial(stem_back_kernel, bands),
        in_specs=[pl.BlockSpec(memory_space=pltpu.SMEM)] + [vmem] * (8 + len(sums)),
        out_shape=[
            jax.ShapeDtypeStruct((8, (bands + 16) // 8, model), F32),
            jax.ShapeDtypeStruct((frames, 2 * bands), BF),
        ],
        scratch_shapes=[pltpu.VMEM((bands + 16, model), F32)],
        compiler_params=pltpu.CompilerParams(vmem_limit_bytes=VMEM_LIMIT),
        cost_estimate=SMALL,
        name="stem_back",
    )(places, grad, edges, matrix, even, odd, rim, window, back_matrix, *sums)


def on_device(
    spectrogram,
    first_kernel,
    first_bias,
    second_kernel,
    second_bias,
    attend_gain,
    attend_shift,
    project_weight,
    project_bias,
    output_weight,
    output_bias,
    mixer_gain,
    mixer_shift,
    expand_weight,
    expand_bias,
    reduce_weight,
    reduce_bias,
    cotangent,
):
    _, steps, bands = spectrogram.shape
    frames = steps // 2
    width = first_kernel.shape[2]
    model = second_kernel.shape[2]
    hidden = expand_weight.shape[1]
    mps, seqs = lax.axis_size("mp"), lax.axis_size("seq")
    z, seq = lax.axis_index("mp"), lax.axis_index("seq")
    core = lax.rem(seq, 2)
    rows = frames // mps

    part = hidden // 8
    start = (2 * plane_index() + core) * part
    bias_high = expand_bias.astype(BF)
    bias_low = (expand_bias - bias_high.astype(F32)).astype(BF)
    spare = -(2 * model + width + 2) % 128
    held = jnp.concatenate(
        [
            lax.dynamic_slice_in_dim(expand_weight.T, start, part, axis=0),
            lax.dynamic_slice_in_dim(reduce_weight, start, part, axis=0),
            lax.dynamic_slice_in_dim(output_weight.T, start, part, axis=0),
            lax.dynamic_slice_in_dim(
                jnp.stack([bias_high, bias_low], axis=1), start, part, axis=0
            ),
            jnp.zeros((part, spare), BF),
        ],
        axis=1,
    )
    weights_got = gather_mp(held, "weights_mp")

    paired = spectrogram.reshape(frames, 2 * bands)
    before = passed_along(paired[-1:], 1)
    following = passed_along(paired[:1], -1)
    ahead = jnp.concatenate([before, paired, following], axis=0)
    window = jnp.concatenate(
        [ahead[:-2, bands:], ahead[1:-1], ahead[2:, :bands]], axis=1
    )
    prior = jnp.concatenate([before, paired[:1, :bands]], axis=1)
    latter = jnp.concatenate([paired[-1:, bands:], following], axis=1)
    first_matrix = first_kernel.reshape(3 * bands, width)
    even_in = jnp.concatenate([window[:, : 3 * bands], latter], axis=0)
    odd_in = jnp.concatenate([prior, window[:, bands:]], axis=0)
    pre_even = product(even_in, first_matrix) + first_bias
    pre_odd = product(odd_in, first_matrix) + first_bias
    inside = jnp.logical_or(jnp.arange(frames + 1) > 0, seq > 0)[:, None]
    hidden_even = exact_gelu(pre_even[:frames]).astype(BF)
    hidden_odd = jnp.where(inside, exact_gelu(pre_odd), 0.0).astype(BF)
    taps = jnp.concatenate([hidden_odd[:frames], hidden_even, hidden_odd[1:]], axis=1)
    second_matrix = second_kernel.reshape(3 * width, model)
    stem_part = product(taps, second_matrix)
    own_cotangent = rolled_blocks(cotangent.reshape(frames, model))
    early = (
        own_cotangent[0],
        jnp.concatenate(own_cotangent, axis=0).astype(BF),
        jnp.stack([output_bias, reduce_bias, mixer_gain, mixer_shift]),
        column_total(cotangent.reshape(frames, model).astype(BF))[None],
        jnp.transpose(first_kernel[::-1], (0, 2, 1)).reshape(3 * width, bands),
        jnp.concatenate([pre_odd[:1], pre_even[frames:], jnp.zeros((6, width), F32)], axis=0),
        pre_even[:frames],
        pre_odd[1:],
        window,
        taps,
        sinusoid(seq * frames + z * rows, rows, model),
        jnp.stack([z, core, seq, plane_index()]),
        z.reshape(1),
        attend_gain.reshape(1, model),
        expand_bias.reshape(1, hidden),
    )
    stem_part, weights_got, early = lax.optimization_barrier((stem_part, weights_got, early))
    own_cotangent, grad_mlp, vectors, reduce_bias_part, back_matrix = early[:5]
    rim, even_level, odd_level, window, taps, table = early[5:11]
    places, place, attend_gain_row, expand_bias_row = early[11:]
    with jax.named_scope("weights_plane"):
        weights_all = plane_gather(jnp.concatenate(weights_got, axis=0))
    stem_pre = scatter_sum(rolled_blocks(stem_part), "stem_sum") + second_bias
    resid_zero = exact_gelu(stem_pre) + table
    normed_one = lax.all_gather(
        layer_norm(resid_zero, attend_gain, attend_shift).astype(BF), "mp", axis=0, tiled=True
    )

    project_matrix = project_weight.transpose(1, 2, 0).reshape(3 * width, model)
    offsets = jnp.concatenate([project_bias[0], jnp.zeros_like(project_bias[0]), project_bias[1]])
    packed = (product(normed_one, project_matrix, 1, 1) + offsets).astype(BF)
    query, pair = packed[:, :width], packed[:, width:]
    pair_far = swapped(pair, "seq", 2, "pair_far")
    pair_core = swapped(pair, "seq", 1, "pair_core")
    pair_far_core = swapped(pair_far, "seq", 1, "pair_far_core")
    attended, attended_turned, level = attend(query, [pair, pair_core, pair_far, pair_far_core])
    heads_got = exchange_mp(rolled_blocks(attended), "attended")
    resid_one, normed_two_own = join(weights_all, heads_got, resid_zero, vectors)
    normed_two_all = gather_mp(normed_two_own, "normed_two")
    shown_own, grad_resid_one, middle_sums, *grad_heads = middle(
        weights_all,
        resid_one,
        normed_two_own,
        own_cotangent,
        vectors,
        mps,
        width,
    )
    shown = lax.all_gather(shown_own, "mp", axis=0, tiled=True)
    rows_got = exchange_mp(grad_heads, "grad_heads")
    grad_attended = natural([rows_got[-j % mps] for j in range(mps)])
    grad_attended, normed_two_all = lax.optimization_barrier((grad_attended, normed_two_all))

    query_grad, near, far, cores = attend_back(
        query,
        grad_attended,
        attended_turned,
        level,
        [pair, pair_core, pair_far, pair_far_core],
    )
    cores_got = swapped(cores, "seq", 1, "grad_core")
    far = (far.astype(F32) + cores_got[1].astype(F32)).astype(BF)
    far_got = swapped(far, "seq", 2, "grad_far")
    feed_mine, feed_other, expand_bias_part = feed(
        places,
        expand_weight,
        reduce_weight,
        expand_bias_row,
        after(grad_mlp, far),
        normed_two_all,
    )
    far_got, feed_other = lax.optimization_barrier((far_got, feed_other))
    feed_got = swapped(feed_other, "seq", 1, "feed_core")
    grad_packed, project_columns, *normed_parts = pack(
        place, query_grad, near, cores_got, far_got, project_matrix, mps
    )
    normed_got = exchange_mp(normed_parts, "grad_normed_one")

    project_mine, project_other = project_weights(places, grad_packed, normed_one, attended, shown)
    project_got = swapped(project_other, "seq", 1, "project_core")
    wide_pieces = pieces(places, feed_mine, feed_got, project_mine, project_got)
    normed_got, wide_pieces = lax.optimization_barrier((normed_got, wide_pieces))
    wide_parts = [
        plane_move(piece, d, "wide_scatter") for d, piece in zip((1, 2, 3), wide_pieces[1:])
    ]

    grad_stem_own = pull(
        resid_zero, grad_resid_one, stem_pre, attend_gain_row, middle_sums, normed_got
    )
    with jax.named_scope("grad_stem"):
        gathered = lax.all_gather(grad_stem_own, "mp", axis=0, tiled=True)
    gathered, wide_parts = lax.optimization_barrier((gathered, wide_parts))
    with jax.named_scope("wide_gather"):
        wide_all = plane_gather(rest_of_dp(total([wide_pieces[0]] + wide_parts).astype(BF)))
    last_row = (mps - 1) * (rows + 16) + rows - 1
    stem_before = passed_along(gathered[last_row : last_row + 1], 1)
    stem_following = passed_along(gathered[:1], -1)
    grad_stem, small, second_mine, second_other = second_weight(places, taps, gathered, mps)
    second_got = swapped(second_other, "seq", 1, "second_core")
    edges = jnp.concatenate([stem_before, stem_following, jnp.zeros((14, model), BF)], axis=0)
    loose, spectrum_part = stem_back(
        places,
        grad_stem,
        edges,
        second_matrix,
        even_level,
        odd_level,
        rim,
        window,
        back_matrix,
        small,
        reduce_bias_part,
        expand_bias_part,
        project_columns,
    )
    halves = loose.reshape(4, 2, -1, model)
    loose_mine = lax.dynamic_index_in_dim(halves, core, 1, keepdims=False)
    loose_other = lax.dynamic_index_in_dim(halves, 1 - core, 1, keepdims=False)
    loose_got = swapped(loose_other.astype(BF), "seq", 1, "small_core")

    joined = jnp.concatenate(
        [
            (second_mine + second_got.astype(F32)).reshape(4, -1, model),
            loose_mine + loose_got.astype(F32),
        ],
        axis=1,
    )
    spectrum_parts = gather_mp(spectrum_part, "spectrum")
    joined, shown = lax.optimization_barrier((joined, shown))
    piece = plane_scatter(joined, "last_scatter")
    encoded = shown[:, model:].astype(F32)
    piece, encoded = lax.optimization_barrier((piece, encoded))
    with jax.named_scope("last_gather"):
        last = plane_gather(piece[None])
    last, spectrum_parts, wide_all = lax.optimization_barrier((last, spectrum_parts, wide_all))
    expand_sum, reduce_sum, project_sum, output_sum = finish_wide(wide_all, width)
    spectrogram_gradient = spectrum_sum(place, spectrum_parts).reshape(1, steps, bands)
    rows_of = (model, model, model, model, model, model, model, hidden)
    cuts = tuple((row, 0, size) for row, size in enumerate(rows_of))
    cuts += ((8, 0, 2 * width), (8, 2 * width, 3 * width))
    second_sum, first_sum, *sums = finish(last, bands, bands + 16, width, cuts)
    return (
        encoded.reshape(1, frames, model),
        spectrogram_gradient,
        first_sum.reshape(3, bands, width),
        sums[9],
        second_sum.reshape(3, width, model),
        sums[5],
        sums[0],
        sums[1],
        project_sum.T.reshape(model, 3, width),
        sums[8],
        output_sum,
        sums[4],
        sums[2],
        sums[3],
        expand_sum,
        sums[7],
        reduce_sum,
        sums[6],
    )


def solution(mesh):
    return jax.shard_map(
        on_device,
        mesh=mesh,
        in_specs=(
            P("dp", "seq", None),
            P(None, None, "mp"),
            P("mp"),
            P(None, "mp", None),
            P(),
            P(),
            P(),
            P(None, None, "mp"),
            P(None, "mp"),
            P("mp", None),
            P(),
            P(),
            P(),
            P(None, "mp"),
            P("mp"),
            P("mp", None),
            P(),
            P("dp", "seq", None),
        ),
        out_specs=(
            P("dp", "seq", None),
            P("dp", "seq", None),
            P(None, None, "mp"),
            P("mp"),
            P(None, "mp", None),
            P(),
            P(),
            P(),
            P(None, None, "mp"),
            P(None, "mp"),
            P("mp", None),
            P(),
            P(),
            P(),
            P(None, "mp"),
            P("mp"),
            P("mp", None),
            P(),
        ),
        check_vma=False,
    )
```

```python
import functools
import math

import jax
import jax.numpy as jnp
from jax import lax
from jax.experimental import pallas as pl
from jax.experimental.pallas import tpu as pltpu
from jax.sharding import PartitionSpec as P

HEAD_DIM = 64
BF = jnp.bfloat16
F32 = jnp.float32
VMEM_LIMIT = 60 * 1024 * 1024
SMALL = pl.CostEstimate(flops=1, bytes_accessed=1, transcendentals=0)


def product(left, right, left_dim=1, right_dim=0):
    dims = (((left_dim,), (right_dim,)), ((), ()))
    return lax.dot_general(left, right, dims, preferred_element_type=F32)


def after(value, *others):
    return lax.optimization_barrier((value, *others))[0]


def exact_gelu(value):
    return jax.nn.gelu(value, approximate=False)


def gelu_back(value, grad):
    return jax.vjp(exact_gelu, value)[1](grad)[0]


def layer_norm(value, gain, shift):
    centre = value - jnp.mean(value, axis=-1, keepdims=True)
    spread = jnp.mean(centre * centre, axis=-1, keepdims=True)
    return centre * lax.rsqrt(spread + 1e-05) * gain + shift


def norm_back(value, gain, grad):
    centre = value - jnp.mean(value, axis=-1, keepdims=True)
    spread = jnp.mean(centre * centre, axis=-1, keepdims=True)
    inverse = lax.rsqrt(spread + 1e-05)
    xhat = centre * inverse
    e = grad * gain
    back = (
        e - jnp.mean(e, axis=-1, keepdims=True) - xhat * jnp.mean(e * xhat, axis=-1, keepdims=True)
    ) * inverse
    return back, jnp.sum(grad * xhat, axis=0), jnp.sum(grad, axis=0)


def column_total(value):
    return jnp.sum(value.astype(F32), axis=0)


def sinusoid(start, count, width):
    half = width // 2
    rates = jnp.exp(jnp.arange(half, dtype=F32) * (-math.log(10000.0) / (half - 1)))
    times = (start + jnp.arange(count)).astype(F32)
    angles = times[:, None] * rates[None, :]
    return jnp.concatenate([jnp.sin(angles), jnp.cos(angles)], axis=1)


def turned(size, by):
    return [(i, (i + by) % size) for i in range(size)]


def gather_mp(block, name):
    size = lax.axis_size("mp")
    with jax.named_scope(name):
        return [block] + [lax.ppermute(block, "mp", turned(size, -j)) for j in range(1, size)]


def exchange_mp(blocks, name):
    size = lax.axis_size("mp")
    with jax.named_scope(name):
        got = [lax.ppermute(blocks[j], "mp", turned(size, j)) for j in range(1, size)]
    return [blocks[0]] + got


def row_blocks(value, count):
    rows = value.shape[0] // count
    return [value[j * rows : (j + 1) * rows] for j in range(count)]


def rolled_blocks(value):
    size, z = lax.axis_size("mp"), lax.axis_index("mp")
    rows = value.shape[0] // size
    return [
        lax.dynamic_slice_in_dim(value, lax.rem(z + j, size) * rows, rows, axis=0)
        for j in range(size)
    ]


def natural(blocks):
    size, z = lax.axis_size("mp"), lax.axis_index("mp")
    rows = blocks[0].shape[0]
    twice = jnp.concatenate(blocks + blocks, axis=0)
    return lax.dynamic_slice_in_dim(twice, lax.rem(size - z, size) * rows, rows * size, axis=0)


def total(parts):
    result = parts[0].astype(F32)
    for part in parts[1:]:
        result = result + part.astype(F32)
    return result


def scatter_sum(blocks, name):
    return total(exchange_mp([blocks[0]] + [block.astype(BF) for block in blocks[1:]], name))


def swapped(value, axis, bit, name):
    size = lax.axis_size(axis)
    with jax.named_scope(name):
        return lax.ppermute(value, axis, [(i, i ^ bit) for i in range(size)])


def passed_along(value, by):
    size = lax.axis_size("seq")
    pairs = [(i, i + by) for i in range(size) if 0 <= i + by < size]
    return lax.ppermute(value, "seq", pairs)


def plane_index():
    return lax.rem(lax.axis_index("dp"), 2) * 2 + lax.div(lax.axis_index("seq"), 2)


def plane_move(value, d, name):
    dps, seqs = lax.axis_size("dp"), lax.axis_size("seq")
    pairs = [
        (p * seqs + s, (p ^ (d >> 1)) * seqs + (s ^ (2 * (d & 1))))
        for p in range(dps)
        for s in range(seqs)
    ]
    with jax.named_scope(name):
        return lax.ppermute(value, ("dp", "seq"), pairs)


def rest_of_dp(value):
    dps = lax.axis_size("dp")
    if dps > 2:
        groups = [[i for i in range(dps) if i % 2 == bit] for bit in range(2)]
        value = lax.psum(value, "dp", axis_index_groups=groups)
    return value


def plane_scatter(quarters, name):
    index = plane_index()

    def piece(d):
        return lax.dynamic_index_in_dim(quarters, jnp.bitwise_xor(index, d), 0, keepdims=False)

    got = [plane_move(piece(d).astype(BF), d, name) for d in (1, 2, 3)]
    return rest_of_dp(total([piece(0)] + got).astype(BF))


def plane_gather(piece):
    dps = lax.axis_size("dp")
    if dps == 2:
        return lax.all_gather(piece, ("dp", "seq"), axis=0, tiled=True)
    pairs = [[i, i + 1] for i in range(0, dps, 2)]
    return lax.all_gather(
        lax.all_gather(piece, "seq", axis=0, tiled=True),
        "dp",
        axis=0,
        tiled=True,
        axis_index_groups=pairs,
    )


def core_rows(held, core, mine_out, other_out, start=0):
    rows = held.shape[0] // 8
    mine, others = [], []
    for quarter in range(4):
        here = pl.ds(pl.multiple_of((2 * quarter + core) * rows, rows), rows)
        there = pl.ds(pl.multiple_of((2 * quarter + 1 - core) * rows, rows), rows)
        mine.append(held[here, :])
        others.append(held[there, :])
    place = slice(start, start + 4 * rows)
    mine_out[place, :] = jnp.concatenate(mine, axis=0).astype(mine_out.dtype)
    other_out[place, :] = jnp.concatenate(others, axis=0).astype(BF)


def finish_wide_kernel(wide_ref, expand_out, reduce_out, project_out, output_out):
    part = expand_out.shape[0] // 8
    split = project_out.shape[0] // part
    for p in range(8):
        here = slice(p * part, (p + 1) * part)
        block = wide_ref[3 * p * part : 3 * (p + 1) * part, :].astype(F32)
        expand_out[here, :] = block[:part]
        reduce_out[here, :] = block[part : 2 * part]
        if p < split:
            project_out[here, :] = block[2 * part :]
        else:
            output_out[(p - split) * part : (p - split + 1) * part, :] = block[2 * part :]


def finish_wide(wide, width):
    model = wide.shape[1]
    return pl.pallas_call(
        finish_wide_kernel,
        out_shape=[
            jax.ShapeDtypeStruct((rows, model), F32) for rows in (model, model, 3 * width, width)
        ],
        compiler_params=pltpu.CompilerParams(vmem_limit_bytes=VMEM_LIMIT),
        cost_estimate=SMALL,
        name="finish_wide",
    )(wide)


def finish_kernel(bands, loose, vectors, gathered_ref, second_out, first_out, *refs):
    outs, (whole, small) = refs[:-2], refs[-2:]
    eighth = gathered_ref.shape[1]
    rows, few = eighth - loose // 8, loose // 8
    for p in range(8):
        whole[...] = gathered_ref[p].astype(F32)
        second_out[p * rows : (p + 1) * rows, :] = whole[:rows, :]
        small[p * few : (p + 1) * few, :] = whole[rows:, :]
    width = first_out.shape[1]
    for tap in range(3):
        first_out[tap * bands : (tap + 1) * bands, :] = small[
            :bands, tap * width : (tap + 1) * width
        ]
    for out, (row, start, stop) in zip(outs, vectors):
        if out.ndim == 1:
            out[...] = small[bands + row, start:stop]
        else:
            for k in range(out.shape[0]):
                place = start + k * width
                out[k : k + 1, :] = small[bands + row : bands + row + 1, place : place + width]


def finish(gathered, bands, loose, width, vectors):
    _, rows, model = gathered.shape
    return pl.pallas_call(
        functools.partial(finish_kernel, bands, loose, vectors),
        out_shape=[
            jax.ShapeDtypeStruct((8 * rows - loose, model), F32),
            jax.ShapeDtypeStruct((3 * bands, width), F32),
        ]
        + [
            jax.ShapeDtypeStruct(
                (2, width) if stop - start == 2 * width else (stop - start,), F32
            )
            for _, start, stop in vectors
        ],
        scratch_shapes=[pltpu.VMEM((rows, model), F32), pltpu.VMEM((loose, model), F32)],
        compiler_params=pltpu.CompilerParams(vmem_limit_bytes=VMEM_LIMIT),
        cost_estimate=SMALL,
        name="finish",
    )(gathered)


def spectrum_kernel(place_ref, *refs):
    parts, (out_ref, held) = refs[:-2], refs[-2:]
    for j, part in enumerate(parts):
        held[lax.rem(place_ref[0] + j, len(parts))] = part[...].astype(F32)
    result = held[0]
    for j in range(1, len(parts)):
        result = result + held[j]
    out_ref[...] = result


def spectrum_sum(place, parts):
    vmem = pl.BlockSpec(memory_space=pltpu.VMEM)
    shape = parts[0].shape
    return pl.pallas_call(
        spectrum_kernel,
        in_specs=[pl.BlockSpec(memory_space=pltpu.SMEM)] + [vmem] * len(parts),
        out_shape=jax.ShapeDtypeStruct(shape, F32),
        scratch_shapes=[pltpu.VMEM((len(parts), *shape), F32)],
        compiler_params=pltpu.CompilerParams(vmem_limit_bytes=VMEM_LIMIT),
        cost_estimate=SMALL,
        name="spectrum_sum",
    )(place, *parts)


def attend_kernel(heads, scale, place_ref, query_ref, *refs):
    pair_refs, (out_ref, turned_ref, level_ref), refs = refs[:4], refs[4:7], refs[7:]
    block_refs, held = refs[:-1], refs[-1]
    width = heads * HEAD_DIM
    count = pair_refs[0].shape[0]
    outs, levels = [], []
    for head in range(heads):
        cols = slice(head * HEAD_DIM, (head + 1) * HEAD_DIM)
        query = query_ref[:, cols] * jnp.asarray(scale, BF)
        top = None
        for index, pair in enumerate(pair_refs):
            scores = product(pair[:, cols], query, 1, 1)
            held[index * count : (index + 1) * count, :] = scores
            high = jnp.max(scores, axis=0, keepdims=True)
            top = high if top is None else jnp.maximum(top, high)
        weight, out = 0.0, 0.0
        vcols = slice(width + head * HEAD_DIM, width + (head + 1) * HEAD_DIM)
        for index, pair in enumerate(pair_refs):
            soft = jnp.exp(held[index * count : (index + 1) * count, :] - top)
            weight = weight + jnp.sum(soft, axis=0, keepdims=True)
            out = out + product(pair[:, vcols], soft.astype(BF), 0, 0)
        outs.append(out / weight)
        levels.append(top + jnp.log(weight))
    joined = jnp.concatenate(outs, axis=0)
    turned_ref[...] = joined
    out_ref[...] = joined.T.astype(BF)
    level_ref[...] = jnp.concatenate(levels, axis=0)
    rows = block_refs[0].shape[0]
    for j, block in enumerate(block_refs):
        start = pl.multiple_of(lax.rem(place_ref[0] + j, len(block_refs)) * rows, rows)
        block[...] = out_ref[pl.ds(start, rows), :]


def attend(place, query, pairs, mps):
    rows, width = query.shape
    heads = width // HEAD_DIM
    vmem = pl.BlockSpec(memory_space=pltpu.VMEM)
    return pl.pallas_call(
        functools.partial(attend_kernel, heads, HEAD_DIM ** (-0.5)),
        in_specs=[pl.BlockSpec(memory_space=pltpu.SMEM)] + [vmem] * 5,
        out_shape=[
            jax.ShapeDtypeStruct((rows, width), BF),
            jax.ShapeDtypeStruct((width, rows), F32),
            jax.ShapeDtypeStruct((heads, rows), F32),
        ]
        + [jax.ShapeDtypeStruct((rows // mps, width), BF)] * mps,
        scratch_shapes=[pltpu.VMEM((rows * len(pairs), rows), F32)],
        compiler_params=pltpu.CompilerParams(vmem_limit_bytes=VMEM_LIMIT),
        cost_estimate=SMALL,
        name="attend",
    )(place, query, *pairs)


def attend_back_kernel(heads, scale, place_ref, query_ref, turned_ref, level_ref, *refs):
    pair_refs, refs = refs[:4], refs[4:]
    block_refs, (query_out, near_out, far_out, core_out, grad_ref) = refs[:-5], refs[-5:]
    width = heads * HEAD_DIM
    rows = block_refs[0].shape[0]
    for j, block in enumerate(block_refs):
        start = pl.multiple_of(lax.rem(place_ref[0] + j, len(block_refs)) * rows, rows)
        grad_ref[pl.ds(start, rows), :] = block[...]
    grads_turned = grad_ref[...].astype(F32).T
    query_grads = []
    pair_grads = [([], []) for _ in range(4)]
    for head in range(heads):
        cols = slice(head * HEAD_DIM, (head + 1) * HEAD_DIM)
        vcols = slice(width + head * HEAD_DIM, width + (head + 1) * HEAD_DIM)
        query = query_ref[:, cols] * jnp.asarray(scale, BF)
        grad = grad_ref[:, cols]
        level = level_ref[head : head + 1, :]
        delta = jnp.sum(grads_turned[cols, :] * turned_ref[cols, :], axis=0, keepdims=True)
        query_grad = 0.0
        for index in range(4):
            pair = pair_refs[index]
            key = pair[:, cols]
            soft = jnp.exp(product(key, query, 1, 1) - level)
            grad_soft = product(pair[:, vcols], grad, 1, 1)
            low = (soft * (grad_soft - delta)).astype(BF)
            pair_grads[index][0].append(product(low, query))
            pair_grads[index][1].append(product(soft.astype(BF), grad))
            query_grad = query_grad + product(key, low, 0, 0)
        query_grads.append(query_grad * scale)
    query_out[...] = jnp.concatenate(query_grads, axis=0).T.astype(BF)
    near, near_core, far, far_core = [
        jnp.concatenate(keys + values, axis=1) for keys, values in pair_grads
    ]
    near_out[...] = near.astype(BF)
    far_out[...] = far.astype(BF)
    core_out[0] = near_core.astype(BF)
    core_out[1] = far_core.astype(BF)


def attend_back(place, query, turned_out, level, pairs, blocks):
    rows, width = query.shape
    heads = width // HEAD_DIM
    vmem = pl.BlockSpec(memory_space=pltpu.VMEM)
    return pl.pallas_call(
        functools.partial(attend_back_kernel, heads, HEAD_DIM ** (-0.5)),
        in_specs=[pl.BlockSpec(memory_space=pltpu.SMEM)] + [vmem] * (7 + len(blocks)),
        out_shape=[
            jax.ShapeDtypeStruct((rows, width), BF),
            jax.ShapeDtypeStruct((rows, 2 * width), BF),
            jax.ShapeDtypeStruct((rows, 2 * width), BF),
            jax.ShapeDtypeStruct((2, rows, 2 * width), BF),
        ],
        scratch_shapes=[pltpu.VMEM((rows, width), BF)],
        compiler_params=pltpu.CompilerParams(vmem_limit_bytes=VMEM_LIMIT),
        cost_estimate=SMALL,
        name="attend_back",
    )(place, query, turned_out, level, *pairs, *blocks)


def gelu_parts(value):
    share = 0.5 + 0.5 * lax.erf(value * math.sqrt(0.5))
    slope = share + value * jnp.exp(-0.5 * value * value) * (1.0 / math.sqrt(2.0 * math.pi))
    return value * share, slope


def across_of(weights_ref, j, mps, width):
    rows = weights_ref.shape[0] // (8 * mps)
    places = [(p * mps + j % mps) * rows for p in range(8)]
    return jnp.concatenate([weights_ref[place : place + rows, :width] for place in places], axis=0)


def norm_parts(value):
    centre = value - jnp.mean(value, axis=-1, keepdims=True)
    inverse = lax.rsqrt(jnp.mean(centre * centre, axis=-1, keepdims=True) + 1e-05)
    return centre * inverse, inverse


def norm_pull(grad, gain, xhat, inverse):
    e = grad * gain
    shared = jnp.mean(e, axis=-1, keepdims=True) + xhat * jnp.mean(e * xhat, axis=-1, keepdims=True)
    return (e - shared) * inverse


def join_kernel(weights_ref, resid_ref, vectors_ref, *refs):
    heads_refs, (resid_out, normed_out) = refs[:-2], refs[-2:]
    mps, width = len(heads_refs), heads_refs[0].shape[1]
    resid = resid_ref[...] + vectors_ref[0:1, :]
    for j in range(mps):
        part = across_of(weights_ref, -j, mps, width)
        resid = resid + product(heads_refs[j][...], part, 1, 1)
    resid_out[...] = resid
    xhat, _ = norm_parts(resid)
    normed_out[...] = (xhat * vectors_ref[2:3, :] + vectors_ref[3:4, :]).astype(BF)


def join(weights, heads, resid, vectors):
    rows, model = resid.shape
    wide = weights.shape[1] % 256 + 256 if weights.shape[1] % 256 else 256
    vmem = pl.BlockSpec(memory_space=pltpu.VMEM)
    return pl.pallas_call(
        join_kernel,
        grid=(1,),
        in_specs=[
            pl.BlockSpec((weights.shape[0], wide), lambda i: (0, weights.shape[1] // wide - 1)),
        ]
        + [vmem] * (2 + len(heads)),
        out_specs=[vmem, vmem],
        out_shape=[
            jax.ShapeDtypeStruct((rows, model), F32),
            jax.ShapeDtypeStruct((rows, model), BF),
        ],
        compiler_params=pltpu.CompilerParams(vmem_limit_bytes=VMEM_LIMIT),
        cost_estimate=SMALL,
        name="join",
    )(weights, resid, vectors, *heads)


def middle_kernel(
    mps,
    width,
    weights_ref,
    across_ref,
    resid_ref,
    normed_ref,
    cotangent_ref,
    vectors_ref,
    shown_ref,
    grad_ref,
    sums_ref,
    *refs,
):
    grad_heads_refs, (forward, backward) = refs[:mps], refs[mps:]
    rows, model = resid_ref.shape
    step = pl.program_id(0)

    @pl.when(step == 0)
    def _():
        forward[...] = jnp.zeros_like(forward)
        backward[...] = jnp.zeros_like(backward)

    expand = weights_ref[:, :model]
    reduce = weights_ref[:, model : 2 * model]
    tail = weights_ref[:, weights_ref.shape[1] - 128 :]
    lane = lax.broadcasted_iota(jnp.int32, (rows, 128), 1)
    bias_lane = 2 * model + width - (weights_ref.shape[1] - 128)
    ones = jnp.where(jnp.logical_or(lane == bias_lane, lane == bias_lane + 1), 1.0, 0.0).astype(BF)
    value = product(normed_ref[...], expand, 1, 1) + product(ones, tail, 1, 1)
    active, slope = gelu_parts(value)
    forward[...] += product(active.astype(BF), reduce)
    grad_mlp = cotangent_ref[...].astype(BF)
    grad = (product(grad_mlp, reduce, 1, 1) * slope).astype(BF)
    backward[...] += product(grad, expand)

    @pl.when(step == pl.num_programs(0) - 1)
    def _():
        resid = resid_ref[...]
        shown_ref[:, model:] = (resid + forward[...] + vectors_ref[1:2, :]).astype(BF)
        xhat, inverse = norm_parts(resid)
        grad = backward[...]
        grad_resid = cotangent_ref[...] + norm_pull(grad, vectors_ref[2:3, :], xhat, inverse)
        grad_ref[...] = grad_resid
        attn = grad_resid.astype(BF)
        shown_ref[:, :model] = attn
        sums_ref[...] = jnp.concatenate(
            [
                jnp.sum(grad * xhat, axis=0, keepdims=True),
                jnp.sum(grad, axis=0, keepdims=True),
                jnp.sum(attn.astype(F32), axis=0, keepdims=True),
                jnp.zeros((5, model), F32),
            ],
            axis=0,
        )
        for j in range(mps):
            part = across_of(across_ref, j, mps, width)
            grad_heads_refs[j][...] = product(attn, part).astype(BF)


def middle(weights, resid, normed, cotangent, vectors, mps, width):
    rows, model = resid.shape
    wide = weights.shape[1] % 256 + 256 if weights.shape[1] % 256 else 256
    chunk = 1024
    vmem = pl.BlockSpec(memory_space=pltpu.VMEM)
    return pl.pallas_call(
        functools.partial(middle_kernel, mps, width),
        grid=(weights.shape[0] // chunk,),
        in_specs=[
            pl.BlockSpec((chunk, weights.shape[1]), lambda i: (i, 0)),
            pl.BlockSpec((weights.shape[0], wide), lambda i: (0, weights.shape[1] // wide - 1)),
        ]
        + [vmem] * 4,
        out_specs=[vmem] * (3 + mps),
        out_shape=[
            jax.ShapeDtypeStruct((rows, 2 * model), BF),
            jax.ShapeDtypeStruct((rows, model), F32),
            jax.ShapeDtypeStruct((8, model), F32),
        ]
        + [jax.ShapeDtypeStruct((rows, width), BF)] * mps,
        scratch_shapes=[pltpu.VMEM((rows, model), F32)] * 2,
        compiler_params=pltpu.CompilerParams(vmem_limit_bytes=VMEM_LIMIT),
        cost_estimate=SMALL,
        name="middle",
    )(weights, weights, resid, normed, cotangent, vectors)


def feed_kernel(chunk, places_ref, expand_ref, reduce_ref, bias_ref, grad_ref, *refs):
    normed_refs, refs = refs[:-7], refs[-7:]
    mine_out, other_out, bias_out, normed, normed_turned, held, second_held = refs
    rows = normed_refs[0].shape[0]
    for j, ref in enumerate(normed_refs):
        normed[j * rows : (j + 1) * rows, :] = ref[...]
    normed_turned[...] = normed[...].T
    hidden = expand_ref.shape[1]
    for start in range(0, hidden, chunk):
        here = slice(start, start + chunk)
        value = product(normed[...], expand_ref[:, here]) + bias_ref[:, here]
        active, slope = gelu_parts(value)
        grad = product(grad_ref[...], reduce_ref[here, :], 1, 1) * slope
        low = grad.astype(BF)
        second_held[here, :] = product(active.astype(BF), grad_ref[...], 0, 0)
        held[:, here] = product(normed_turned[...], low)
        bias_out[:, here] = jnp.sum(low.astype(F32), axis=0, keepdims=True)
    core_rows(held, places_ref[1], mine_out, other_out)
    core_rows(second_held, places_ref[1], mine_out, other_out, held.shape[0] // 2)


def feed(places, expand, reduce, bias, grad, normed_blocks):
    model, hidden = expand.shape
    rows = grad.shape[0]
    vmem = pl.BlockSpec(memory_space=pltpu.VMEM)
    half = (model + hidden) // 2
    return pl.pallas_call(
        functools.partial(feed_kernel, 256),
        in_specs=[pl.BlockSpec(memory_space=pltpu.SMEM)] + [vmem] * (4 + len(normed_blocks)),
        out_shape=[
            jax.ShapeDtypeStruct((half, model), BF),
            jax.ShapeDtypeStruct((half, model), BF),
            jax.ShapeDtypeStruct((1, hidden), F32),
        ],
        scratch_shapes=[
            pltpu.VMEM((rows, model), BF),
            pltpu.VMEM((model, rows), BF),
            pltpu.VMEM((model, hidden), F32),
            pltpu.VMEM((hidden, model), F32),
        ],
        compiler_params=pltpu.CompilerParams(vmem_limit_bytes=VMEM_LIMIT),
        cost_estimate=SMALL,
        name="feed",
    )(places, expand, reduce, bias, grad, *normed_blocks)


def project_kernel(places_ref, packed_ref, normed_ref, attended_ref, attn_ref, *refs):
    mine_out, other_out, held = refs
    wide = packed_ref.shape[1]
    held[:wide, :] = product(packed_ref[...], normed_ref[...], 0, 0)
    held[wide:, :] = product(attended_ref[...], attn_ref[...], 0, 0)
    core_rows(held, places_ref[1], mine_out, other_out)


def project_weights(places, packed, normed, attended, shown):
    frames, wide = packed.shape
    width, model = attended.shape[1], normed.shape[1]
    vmem = pl.BlockSpec(memory_space=pltpu.VMEM)
    half = (wide + width) // 2
    return pl.pallas_call(
        project_kernel,
        grid=(1,),
        in_specs=[pl.BlockSpec(memory_space=pltpu.SMEM)]
        + [vmem] * 3
        + [pl.BlockSpec((frames, model), lambda i: (0, 0))],
        out_specs=[vmem, vmem],
        out_shape=[jax.ShapeDtypeStruct((half, model), BF)] * 2,
        scratch_shapes=[pltpu.VMEM((wide + width, model), F32)],
        compiler_params=pltpu.CompilerParams(vmem_limit_bytes=VMEM_LIMIT),
        cost_estimate=SMALL,
        name="project_weights",
    )(places, packed, normed, attended, shown)


def pieces_kernel(places_ref, feed_ref, feed_got_ref, project_ref, project_got_ref, *outs):
    part = project_ref.shape[0] // 4
    pairs = (
        (feed_ref, feed_got_ref, 0),
        (feed_ref, feed_got_ref, 4 * part),
        (project_ref, project_got_ref, 0),
    )
    for d, out in enumerate(outs):
        for which, (mine, got, start) in enumerate(pairs):
            place = start + jnp.bitwise_xor(places_ref[3], d) * part
            here = pl.ds(pl.multiple_of(place, part), part)
            value = mine[here, :].astype(F32) + got[here, :].astype(F32)
            out[which * part : (which + 1) * part, :] = value.astype(out.dtype)


def pieces(places, feed_mine, feed_got, project_mine, project_got):
    vmem = pl.BlockSpec(memory_space=pltpu.VMEM)
    model = feed_mine.shape[1]
    part = 3 * project_mine.shape[0] // 4
    return pl.pallas_call(
        pieces_kernel,
        in_specs=[pl.BlockSpec(memory_space=pltpu.SMEM)] + [vmem] * 4,
        out_shape=[jax.ShapeDtypeStruct((part, model), F32)]
        + [jax.ShapeDtypeStruct((part, model), BF)] * 3,
        compiler_params=pltpu.CompilerParams(vmem_limit_bytes=VMEM_LIMIT),
        cost_estimate=SMALL,
        name="pieces",
    )(places, feed_mine, feed_got, project_mine, project_got)


def pack_kernel(place_ref, query_ref, pair_ref, core_ref, other_ref, weight_ref, *outs):
    packed_out, sums_out, own_out, *others_out = outs
    pair = pair_ref[...].astype(F32) + core_ref[0].astype(F32) + other_ref[...].astype(F32)
    packed = jnp.concatenate([query_ref[...], pair.astype(BF)], axis=1)
    packed_out[...] = packed
    sums_out[...] = jnp.sum(packed.astype(F32), axis=0, keepdims=True)
    rows = own_out.shape[0]
    mps = len(others_out) + 1

    def part(j):
        start = pl.multiple_of(lax.rem(place_ref[0] + j, mps) * rows, rows)
        return product(packed_out[pl.ds(start, rows), :], weight_ref[...])

    own_out[...] = part(0)
    for j in range(1, mps):
        others_out[j - 1][...] = part(j).astype(BF)


def pack(place, query, pair, pair_core, pair_far, weight, mps):
    frames, width = query.shape
    model, rows = weight.shape[1], frames // mps
    vmem = pl.BlockSpec(memory_space=pltpu.VMEM)
    return pl.pallas_call(
        pack_kernel,
        grid=(1,),
        in_specs=[
            pl.BlockSpec(memory_space=pltpu.SMEM),
            vmem,
            vmem,
            pl.BlockSpec((1, frames, 2 * width), lambda i: (0, 0, 0)),
            vmem,
            vmem,
        ],
        out_specs=[vmem] * (2 + mps),
        out_shape=[
            jax.ShapeDtypeStruct((frames, 3 * width), BF),
            jax.ShapeDtypeStruct((1, 3 * width), F32),
            jax.ShapeDtypeStruct((rows, model), F32),
        ]
        + [jax.ShapeDtypeStruct((rows, model), BF)] * (mps - 1),
        compiler_params=pltpu.CompilerParams(vmem_limit_bytes=VMEM_LIMIT),
        cost_estimate=SMALL,
        name="pack",
    )(place, query, pair, pair_core, pair_far, weight)


def pull_kernel(resid_ref, grad_ref, stem_ref, gain_ref, sums_ref, *refs):
    got_refs, out_ref = refs[:-1], refs[-1]
    rows, model = resid_ref.shape
    grad = got_refs[0][...].astype(F32)
    for ref in got_refs[1:]:
        grad = grad + ref[...].astype(F32)
    xhat, inverse = norm_parts(resid_ref[...])
    grad_resid = grad_ref[...] + norm_pull(grad, gain_ref[...], xhat, inverse)
    _, slope = gelu_parts(stem_ref[...])
    low = (grad_resid * slope).astype(BF)
    out_ref[:rows, :] = low
    sums = jnp.concatenate(
        [
            jnp.sum(grad * xhat, axis=0, keepdims=True),
            jnp.sum(grad, axis=0, keepdims=True),
            sums_ref[0:3, :],
            jnp.sum(low.astype(F32), axis=0, keepdims=True),
            jnp.zeros((10, model), F32),
        ],
        axis=0,
    )
    out_ref[rows:, :] = sums.astype(BF)


def pull(resid, grad, stem, gain, sums, got):
    rows, model = resid.shape
    return pl.pallas_call(
        pull_kernel,
        out_shape=jax.ShapeDtypeStruct((rows + 16, model), BF),
        compiler_params=pltpu.CompilerParams(vmem_limit_bytes=VMEM_LIMIT),
        cost_estimate=SMALL,
        name="pull",
    )(resid, grad, stem, gain, sums, *got)


def second_kernel_body(mps, places_ref, taps_ref, gathered_ref, *refs):
    grad_out, sums_out, mine_out, other_out, held = refs
    rows = gathered_ref.shape[0] // mps
    own = rows - 16
    sums = 0.0
    for j in range(mps):
        grad_out[j * own : (j + 1) * own, :] = gathered_ref[j * rows : j * rows + own, :]
        sums = sums + gathered_ref[j * rows + own : (j + 1) * rows, :].astype(F32)
    sums_out[...] = sums
    held[...] = product(taps_ref[...], grad_out[...], 0, 0)
    core_rows(held, places_ref[1], mine_out, other_out)


def second_weight(places, taps, gathered, mps):
    frames, tall = taps.shape
    model = gathered.shape[1]
    vmem = pl.BlockSpec(memory_space=pltpu.VMEM)
    return pl.pallas_call(
        functools.partial(second_kernel_body, mps),
        in_specs=[pl.BlockSpec(memory_space=pltpu.SMEM)] + [vmem] * 2,
        out_shape=[
            jax.ShapeDtypeStruct((frames, model), BF),
            jax.ShapeDtypeStruct((16, model), F32),
            jax.ShapeDtypeStruct((tall // 2, model), F32),
            jax.ShapeDtypeStruct((tall // 2, model), BF),
        ],
        scratch_shapes=[pltpu.VMEM((tall, model), F32)],
        compiler_params=pltpu.CompilerParams(vmem_limit_bytes=VMEM_LIMIT),
        cost_estimate=SMALL,
        name="second_weight",
    )(places, taps, gathered)


def stem_back_kernel(
    bands,
    places_ref,
    grad_ref,
    edges_ref,
    matrix_ref,
    even_ref,
    odd_ref,
    rim_ref,
    window_ref,
    back_ref,
    sums_ref,
    reduce_ref,
    expand_ref,
    project_ref,
    loose_out,
    spectrum_out,
    held,
):
    frames = grad_ref.shape[0]
    width = even_ref.shape[1]
    row = lax.broadcasted_iota(jnp.int32, (frames, width), 0)

    def later(value, last):
        return jnp.where(row == frames - 1, last, pltpu.roll(value, frames - 1, 0))

    def earlier(value, start):
        return jnp.where(row == 0, start, pltpu.roll(value, 1, 0))

    def slope(value):
        return gelu_parts(value)[1]

    def rounded(value):
        return value.astype(BF).astype(F32)

    taps = product(grad_ref[...], matrix_ref[...], 1, 1)
    rims = product(edges_ref[...], matrix_ref[...], 1, 1)
    even = rounded(taps[:, width : 2 * width] * slope(even_ref[...]))
    odd = taps[:, 2 * width :] + later(taps[:, :width], rims[1:2, :width])
    odd = rounded(odd * slope(odd_ref[...]))
    rim_slope = slope(rim_ref[...])
    inside = (places_ref[2] > 0).astype(F32)
    odd_before = rounded((rims[0:1, 2 * width :] + taps[0:1, :width]) * rim_slope[0:1] * inside)
    even_after = rounded(rims[1:2, width : 2 * width] * rim_slope[1:2])
    bias = jnp.sum(even + odd, axis=0, keepdims=True)
    both = jnp.concatenate([even, odd], axis=1).astype(BF)
    weight = product(window_ref[...], both, 0, 0)
    weight = weight[: 3 * bands, :width] + weight[bands:, width:]
    spare = held.shape[1] - 3 * width
    held[:bands, :] = jnp.concatenate(
        [weight[k * bands : (k + 1) * bands] for k in range(3)] + [jnp.zeros((bands, spare), F32)],
        axis=1,
    )
    last = jnp.concatenate(
        [project_ref[:, :width], project_ref[:, 2 * width :], bias, jnp.zeros((1, spare), F32)],
        axis=1,
    )
    blank = jnp.zeros((held.shape[0] - bands - 9, held.shape[1]), F32)
    held[bands:, :] = jnp.concatenate(
        [sums_ref[0:6, :], reduce_ref[...], expand_ref[...], last, blank], axis=0
    )
    few = loose_out.shape[1]
    for p in range(8):
        loose_out[p] = held[p * few : (p + 1) * few, :]
    before = earlier(odd, odd_before).astype(BF)
    following = later(even, even_after).astype(BF)
    even, odd = even.astype(BF), odd.astype(BF)
    back = [back_ref[k * width : (k + 1) * width, :] for k in range(3)]
    spectrum = [
        product(before, back[0]) + product(even, back[1]) + product(odd, back[2]),
        product(even, back[0]) + product(odd, back[1]) + product(following, back[2]),
    ]
    spectrum_out[...] = jnp.concatenate(spectrum, axis=1).astype(BF)


def stem_back(places, grad, edges, matrix, even, odd, rim, window, back_matrix, *sums):
    frames, width = even.shape
    bands, model = back_matrix.shape[1], grad.shape[1]
    vmem = pl.BlockSpec(memory_space=pltpu.VMEM)
    return pl.pallas_call(
        functools.partial(stem_back_kernel, bands),
        in_specs=[pl.BlockSpec(memory_space=pltpu.SMEM)] + [vmem] * (8 + len(sums)),
        out_shape=[
            jax.ShapeDtypeStruct((8, (bands + 16) // 8, model), F32),
            jax.ShapeDtypeStruct((frames, 2 * bands), BF),
        ],
        scratch_shapes=[pltpu.VMEM((bands + 16, model), F32)],
        compiler_params=pltpu.CompilerParams(vmem_limit_bytes=VMEM_LIMIT),
        cost_estimate=SMALL,
        name="stem_back",
    )(places, grad, edges, matrix, even, odd, rim, window, back_matrix, *sums)


def on_device(
    spectrogram,
    first_kernel,
    first_bias,
    second_kernel,
    second_bias,
    attend_gain,
    attend_shift,
    project_weight,
    project_bias,
    output_weight,
    output_bias,
    mixer_gain,
    mixer_shift,
    expand_weight,
    expand_bias,
    reduce_weight,
    reduce_bias,
    cotangent,
):
    _, steps, bands = spectrogram.shape
    frames = steps // 2
    width = first_kernel.shape[2]
    model = second_kernel.shape[2]
    hidden = expand_weight.shape[1]
    mps, seqs = lax.axis_size("mp"), lax.axis_size("seq")
    z, seq = lax.axis_index("mp"), lax.axis_index("seq")
    core = lax.rem(seq, 2)
    rows = frames // mps

    part = hidden // 8
    start = (2 * plane_index() + core) * part
    bias_high = expand_bias.astype(BF)
    bias_low = (expand_bias - bias_high.astype(F32)).astype(BF)
    spare = -(2 * model + width + 2) % 128
    held = jnp.concatenate(
        [
            lax.dynamic_slice_in_dim(expand_weight.T, start, part, axis=0),
            lax.dynamic_slice_in_dim(reduce_weight, start, part, axis=0),
            lax.dynamic_slice_in_dim(output_weight.T, start, part, axis=0),
            lax.dynamic_slice_in_dim(
                jnp.stack([bias_high, bias_low], axis=1), start, part, axis=0
            ),
            jnp.zeros((part, spare), BF),
        ],
        axis=1,
    )
    weights_got = gather_mp(held, "weights_mp")

    paired = spectrogram.reshape(frames, 2 * bands)
    before = passed_along(paired[-1:], 1)
    following = passed_along(paired[:1], -1)
    ahead = jnp.concatenate([before, paired, following], axis=0)
    window = jnp.concatenate(
        [ahead[:-2, bands:], ahead[1:-1], ahead[2:, :bands]], axis=1
    )
    prior = jnp.concatenate([before, paired[:1, :bands]], axis=1)
    latter = jnp.concatenate([paired[-1:, bands:], following], axis=1)
    first_matrix = first_kernel.reshape(3 * bands, width)
    even_in = jnp.concatenate([window[:, : 3 * bands], latter], axis=0)
    odd_in = jnp.concatenate([prior, window[:, bands:]], axis=0)
    pre_even = product(even_in, first_matrix) + first_bias
    pre_odd = product(odd_in, first_matrix) + first_bias
    inside = jnp.logical_or(jnp.arange(frames + 1) > 0, seq > 0)[:, None]
    hidden_even = exact_gelu(pre_even[:frames]).astype(BF)
    hidden_odd = jnp.where(inside, exact_gelu(pre_odd), 0.0).astype(BF)
    taps = jnp.concatenate([hidden_odd[:frames], hidden_even, hidden_odd[1:]], axis=1)
    second_matrix = second_kernel.reshape(3 * width, model)
    stem_part = product(taps, second_matrix)
    own_cotangent = rolled_blocks(cotangent.reshape(frames, model))
    early = (
        own_cotangent[0],
        jnp.concatenate(own_cotangent, axis=0).astype(BF),
        jnp.stack([output_bias, reduce_bias, mixer_gain, mixer_shift]),
        column_total(cotangent.reshape(frames, model).astype(BF))[None],
        jnp.transpose(first_kernel[::-1], (0, 2, 1)).reshape(3 * width, bands),
        jnp.concatenate([pre_odd[:1], pre_even[frames:], jnp.zeros((6, width), F32)], axis=0),
        pre_even[:frames],
        pre_odd[1:],
        window,
        taps,
        sinusoid(seq * frames + z * rows, rows, model),
        jnp.stack([z, core, seq, plane_index()]),
        z.reshape(1),
        attend_gain.reshape(1, model),
        expand_bias.reshape(1, hidden),
    )
    stem_part, weights_got, early = lax.optimization_barrier((stem_part, weights_got, early))
    own_cotangent, grad_mlp, vectors, reduce_bias_part, back_matrix = early[:5]
    rim, even_level, odd_level, window, taps, table = early[5:11]
    places, place, attend_gain_row, expand_bias_row = early[11:]
    with jax.named_scope("weights_plane"):
        weights_all = plane_gather(jnp.concatenate(weights_got, axis=0))
    stem_pre = scatter_sum(rolled_blocks(stem_part), "stem_sum") + second_bias
    resid_zero = exact_gelu(stem_pre) + table
    normed_one = lax.all_gather(
        layer_norm(resid_zero, attend_gain, attend_shift).astype(BF), "mp", axis=0, tiled=True
    )

    project_matrix = project_weight.transpose(1, 2, 0).reshape(3 * width, model)
    offsets = jnp.concatenate([project_bias[0], jnp.zeros_like(project_bias[0]), project_bias[1]])
    packed = (product(normed_one, project_matrix, 1, 1) + offsets).astype(BF)
    query, pair = packed[:, :width], packed[:, width:]
    pair_far = swapped(pair, "seq", 2, "pair_far")
    pair_core = swapped(pair, "seq", 1, "pair_core")
    pair_far_core = swapped(pair_far, "seq", 1, "pair_far_core")
    pairs = [pair, pair_core, pair_far, pair_far_core]
    attended, attended_turned, level, *attended_blocks = attend(place, query, pairs, mps)
    heads_got = exchange_mp(attended_blocks, "attended")
    resid_one, normed_two_own = join(weights_all, heads_got, resid_zero, vectors)
    normed_two_all = gather_mp(normed_two_own, "normed_two")
    shown_own, grad_resid_one, middle_sums, *grad_heads = middle(
        weights_all,
        resid_one,
        normed_two_own,
        own_cotangent,
        vectors,
        mps,
        width,
    )
    shown = lax.all_gather(shown_own, "mp", axis=0, tiled=True)
    rows_got = exchange_mp(grad_heads, "grad_heads")
    grad_attended = natural([rows_got[-j % mps] for j in range(mps)])
    grad_attended, normed_two_all = lax.optimization_barrier((grad_attended, normed_two_all))

    query_grad, near, far, cores = attend_back(
        place,
        query,
        attended_turned,
        level,
        pairs,
        [grad_attended],
    )
    cores_got = swapped(cores, "seq", 1, "grad_core")
    far = (far.astype(F32) + cores_got[1].astype(F32)).astype(BF)
    far_got = swapped(far, "seq", 2, "grad_far")
    feed_mine, feed_other, expand_bias_part = feed(
        places,
        expand_weight,
        reduce_weight,
        expand_bias_row,
        after(grad_mlp, far),
        normed_two_all,
    )
    far_got, feed_other = lax.optimization_barrier((far_got, feed_other))
    feed_got = swapped(feed_other, "seq", 1, "feed_core")
    grad_packed, project_columns, *normed_parts = pack(
        place, query_grad, near, cores_got, far_got, project_matrix, mps
    )
    normed_got = exchange_mp(normed_parts, "grad_normed_one")

    project_mine, project_other = project_weights(places, grad_packed, normed_one, attended, shown)
    project_got = swapped(project_other, "seq", 1, "project_core")
    wide_pieces = pieces(places, feed_mine, feed_got, project_mine, project_got)
    normed_got, wide_pieces = lax.optimization_barrier((normed_got, wide_pieces))
    wide_parts = [
        plane_move(piece, d, "wide_scatter") for d, piece in zip((1, 2, 3), wide_pieces[1:])
    ]

    grad_stem_own = pull(
        resid_zero, grad_resid_one, stem_pre, attend_gain_row, middle_sums, normed_got
    )
    with jax.named_scope("grad_stem"):
        gathered = lax.all_gather(grad_stem_own, "mp", axis=0, tiled=True)
    gathered, wide_parts = lax.optimization_barrier((gathered, wide_parts))
    with jax.named_scope("wide_gather"):
        wide_all = plane_gather(rest_of_dp(total([wide_pieces[0]] + wide_parts).astype(BF)))
    last_row = (mps - 1) * (rows + 16) + rows - 1
    stem_before = passed_along(gathered[last_row : last_row + 1], 1)
    stem_following = passed_along(gathered[:1], -1)
    grad_stem, small, second_mine, second_other = second_weight(places, taps, gathered, mps)
    second_got = swapped(second_other, "seq", 1, "second_core")
    edges = jnp.concatenate([stem_before, stem_following, jnp.zeros((14, model), BF)], axis=0)
    loose, spectrum_part = stem_back(
        places,
        grad_stem,
        edges,
        second_matrix,
        even_level,
        odd_level,
        rim,
        window,
        back_matrix,
        small,
        reduce_bias_part,
        expand_bias_part,
        project_columns,
    )
    halves = loose.reshape(4, 2, -1, model)
    loose_mine = lax.dynamic_index_in_dim(halves, core, 1, keepdims=False)
    loose_other = lax.dynamic_index_in_dim(halves, 1 - core, 1, keepdims=False)
    loose_got = swapped(loose_other.astype(BF), "seq", 1, "small_core")

    joined = jnp.concatenate(
        [
            (second_mine + second_got.astype(F32)).reshape(4, -1, model),
            loose_mine + loose_got.astype(F32),
        ],
        axis=1,
    )
    spectrum_parts = gather_mp(spectrum_part, "spectrum")
    joined, shown = lax.optimization_barrier((joined, shown))
    piece = plane_scatter(joined, "last_scatter")
    encoded = shown[:, model:].astype(F32)
    piece, encoded = lax.optimization_barrier((piece, encoded))
    with jax.named_scope("last_gather"):
        last = plane_gather(piece[None])
    last, spectrum_parts, wide_all = lax.optimization_barrier((last, spectrum_parts, wide_all))
    expand_sum, reduce_sum, project_sum, output_sum = finish_wide(wide_all, width)
    spectrogram_gradient = spectrum_sum(place, spectrum_parts).reshape(1, steps, bands)
    rows_of = (model, model, model, model, model, model, model, hidden)
    cuts = tuple((row, 0, size) for row, size in enumerate(rows_of))
    cuts += ((8, 0, 2 * width), (8, 2 * width, 3 * width))
    second_sum, first_sum, *sums = finish(last, bands, bands + 16, width, cuts)
    return (
        encoded.reshape(1, frames, model),
        spectrogram_gradient,
        first_sum.reshape(3, bands, width),
        sums[9],
        second_sum.reshape(3, width, model),
        sums[5],
        sums[0],
        sums[1],
        project_sum.T.reshape(model, 3, width),
        sums[8],
        output_sum,
        sums[4],
        sums[2],
        sums[3],
        expand_sum,
        sums[7],
        reduce_sum,
        sums[6],
    )


def solution(mesh):
    return jax.shard_map(
        on_device,
        mesh=mesh,
        in_specs=(
            P("dp", "seq", None),
            P(None, None, "mp"),
            P("mp"),
            P(None, "mp", None),
            P(),
            P(),
            P(),
            P(None, None, "mp"),
            P(None, "mp"),
            P("mp", None),
            P(),
            P(),
            P(),
            P(None, "mp"),
            P("mp"),
            P("mp", None),
            P(),
            P("dp", "seq", None),
        ),
        out_specs=(
            P("dp", "seq", None),
            P("dp", "seq", None),
            P(None, None, "mp"),
            P("mp"),
            P(None, "mp", None),
            P(),
            P(),
            P(),
            P(None, None, "mp"),
            P(None, "mp"),
            P("mp", None),
            P(),
            P(),
            P(),
            P(None, "mp"),
            P("mp"),
            P("mp", None),
            P(),
        ),
        check_vma=False,
    )
```

```python
import functools
import math

import jax
import jax.numpy as jnp
from jax import lax
from jax.experimental import pallas as pl
from jax.experimental.pallas import tpu as pltpu
from jax.sharding import PartitionSpec as P

HEAD_DIM = 64
BF = jnp.bfloat16
F32 = jnp.float32
VMEM_LIMIT = 60 * 1024 * 1024
SMALL = pl.CostEstimate(flops=1, bytes_accessed=1, transcendentals=0)


def product(left, right, left_dim=1, right_dim=0):
    dims = (((left_dim,), (right_dim,)), ((), ()))
    return lax.dot_general(left, right, dims, preferred_element_type=F32)


def after(value, *others):
    return lax.optimization_barrier((value, *others))[0]


def exact_gelu(value):
    return jax.nn.gelu(value, approximate=False)


def gelu_back(value, grad):
    return jax.vjp(exact_gelu, value)[1](grad)[0]


def layer_norm(value, gain, shift):
    centre = value - jnp.mean(value, axis=-1, keepdims=True)
    spread = jnp.mean(centre * centre, axis=-1, keepdims=True)
    return centre * lax.rsqrt(spread + 1e-05) * gain + shift


def norm_back(value, gain, grad):
    centre = value - jnp.mean(value, axis=-1, keepdims=True)
    spread = jnp.mean(centre * centre, axis=-1, keepdims=True)
    inverse = lax.rsqrt(spread + 1e-05)
    xhat = centre * inverse
    e = grad * gain
    back = (
        e - jnp.mean(e, axis=-1, keepdims=True) - xhat * jnp.mean(e * xhat, axis=-1, keepdims=True)
    ) * inverse
    return back, jnp.sum(grad * xhat, axis=0), jnp.sum(grad, axis=0)


def column_total(value):
    return jnp.sum(value.astype(F32), axis=0)


def sinusoid(start, count, width):
    half = width // 2
    rates = jnp.exp(jnp.arange(half, dtype=F32) * (-math.log(10000.0) / (half - 1)))
    times = (start + jnp.arange(count)).astype(F32)
    angles = times[:, None] * rates[None, :]
    return jnp.concatenate([jnp.sin(angles), jnp.cos(angles)], axis=1)


def turned(size, by):
    return [(i, (i + by) % size) for i in range(size)]


def gather_mp(block, name):
    size = lax.axis_size("mp")
    with jax.named_scope(name):
        return [block] + [lax.ppermute(block, "mp", turned(size, -j)) for j in range(1, size)]


def exchange_mp(blocks, name):
    size = lax.axis_size("mp")
    with jax.named_scope(name):
        got = [lax.ppermute(blocks[j], "mp", turned(size, j)) for j in range(1, size)]
    return [blocks[0]] + got


def row_blocks(value, count):
    rows = value.shape[0] // count
    return [value[j * rows : (j + 1) * rows] for j in range(count)]


def rolled_blocks(value):
    size, z = lax.axis_size("mp"), lax.axis_index("mp")
    rows = value.shape[0] // size
    return [
        lax.dynamic_slice_in_dim(value, lax.rem(z + j, size) * rows, rows, axis=0)
        for j in range(size)
    ]


def natural(blocks):
    size, z = lax.axis_size("mp"), lax.axis_index("mp")
    rows = blocks[0].shape[0]
    twice = jnp.concatenate(blocks + blocks, axis=0)
    return lax.dynamic_slice_in_dim(twice, lax.rem(size - z, size) * rows, rows * size, axis=0)


def total(parts):
    result = parts[0].astype(F32)
    for part in parts[1:]:
        result = result + part.astype(F32)
    return result


def scatter_sum(blocks, name):
    return total(exchange_mp([blocks[0]] + [block.astype(BF) for block in blocks[1:]], name))


def swapped(value, axis, bit, name):
    size = lax.axis_size(axis)
    with jax.named_scope(name):
        return lax.ppermute(value, axis, [(i, i ^ bit) for i in range(size)])


def passed_along(value, by):
    size = lax.axis_size("seq")
    pairs = [(i, i + by) for i in range(size) if 0 <= i + by < size]
    return lax.ppermute(value, "seq", pairs)


def plane_index():
    return lax.rem(lax.axis_index("dp"), 2) * 2 + lax.div(lax.axis_index("seq"), 2)


def plane_move(value, d, name):
    dps, seqs = lax.axis_size("dp"), lax.axis_size("seq")
    pairs = [
        (p * seqs + s, (p ^ (d >> 1)) * seqs + (s ^ (2 * (d & 1))))
        for p in range(dps)
        for s in range(seqs)
    ]
    with jax.named_scope(name):
        return lax.ppermute(value, ("dp", "seq"), pairs)


def rest_of_dp(value):
    dps = lax.axis_size("dp")
    if dps > 2:
        groups = [[i for i in range(dps) if i % 2 == bit] for bit in range(2)]
        value = lax.psum(value, "dp", axis_index_groups=groups)
    return value


def plane_scatter(quarters, name):
    index = plane_index()

    def piece(d):
        return lax.dynamic_index_in_dim(quarters, jnp.bitwise_xor(index, d), 0, keepdims=False)

    got = [plane_move(piece(d).astype(BF), d, name) for d in (1, 2, 3)]
    return rest_of_dp(total([piece(0)] + got).astype(BF))


def plane_gather(piece):
    dps = lax.axis_size("dp")
    if dps == 2:
        return lax.all_gather(piece, ("dp", "seq"), axis=0, tiled=True)
    pairs = [[i, i + 1] for i in range(0, dps, 2)]
    return lax.all_gather(
        lax.all_gather(piece, "seq", axis=0, tiled=True),
        "dp",
        axis=0,
        tiled=True,
        axis_index_groups=pairs,
    )


def core_rows(held, core, mine_out, other_out, start=0):
    rows = held.shape[0] // 8
    mine, others = [], []
    for quarter in range(4):
        here = pl.ds(pl.multiple_of((2 * quarter + core) * rows, rows), rows)
        there = pl.ds(pl.multiple_of((2 * quarter + 1 - core) * rows, rows), rows)
        mine.append(held[here, :])
        others.append(held[there, :])
    place = slice(start, start + 4 * rows)
    mine_out[place, :] = jnp.concatenate(mine, axis=0).astype(mine_out.dtype)
    other_out[place, :] = jnp.concatenate(others, axis=0).astype(BF)


def finish_wide_kernel(wide_ref, expand_out, reduce_out, project_out, output_out):
    part = expand_out.shape[0] // 8
    split = project_out.shape[0] // part
    for p in range(8):
        here = slice(p * part, (p + 1) * part)
        block = wide_ref[3 * p * part : 3 * (p + 1) * part, :].astype(F32)
        expand_out[here, :] = block[:part]
        reduce_out[here, :] = block[part : 2 * part]
        if p < split:
            project_out[here, :] = block[2 * part :]
        else:
            output_out[(p - split) * part : (p - split + 1) * part, :] = block[2 * part :]


def finish_kernel(bands, loose, vectors, gathered_ref, second_out, first_out, *refs):
    outs, (whole, small) = refs[:-2], refs[-2:]
    eighth = gathered_ref.shape[1]
    rows, few = eighth - loose // 8, loose // 8
    for p in range(8):
        whole[...] = gathered_ref[p].astype(F32)
        second_out[p * rows : (p + 1) * rows, :] = whole[:rows, :]
        small[p * few : (p + 1) * few, :] = whole[rows:, :]
    width = first_out.shape[1]
    for tap in range(3):
        first_out[tap * bands : (tap + 1) * bands, :] = small[
            :bands, tap * width : (tap + 1) * width
        ]
    for out, (row, start, stop) in zip(outs, vectors):
        if out.ndim == 1:
            out[...] = small[bands + row, start:stop]
        else:
            for k in range(out.shape[0]):
                place = start + k * width
                out[k : k + 1, :] = small[bands + row : bands + row + 1, place : place + width]


def spectrum_kernel(place_ref, *refs):
    parts, (out_ref, held) = refs[:-2], refs[-2:]
    for j, part in enumerate(parts):
        held[lax.rem(place_ref[0] + j, len(parts))] = part[...].astype(F32)
    result = held[0]
    for j in range(1, len(parts)):
        result = result + held[j]
    out_ref[...] = result


def end_kernel(bands, loose, vectors, mps, place_ref, wide_ref, gathered_ref, *refs):
    parts, refs = refs[:mps], refs[mps:]
    wide_outs, spectrum_out, refs = refs[:4], refs[4], refs[5:]
    outs, (whole, small, held) = refs[:-3], refs[-3:]
    finish_wide_kernel(wide_ref, *wide_outs)
    spectrum_kernel(place_ref, *parts, spectrum_out, held)
    finish_kernel(bands, loose, vectors, gathered_ref, *outs, whole, small)


def end(place, wide, gathered, parts, bands, loose, width, vectors):
    _, rows, model = gathered.shape
    vmem = pl.BlockSpec(memory_space=pltpu.VMEM)
    return pl.pallas_call(
        functools.partial(end_kernel, bands, loose, vectors, len(parts)),
        in_specs=[pl.BlockSpec(memory_space=pltpu.SMEM)] + [vmem] * (2 + len(parts)),
        out_shape=[
            jax.ShapeDtypeStruct((high, model), F32) for high in (model, model, 3 * width, width)
        ]
        + [
            jax.ShapeDtypeStruct(parts[0].shape, F32),
            jax.ShapeDtypeStruct((8 * rows - loose, model), F32),
            jax.ShapeDtypeStruct((3 * bands, width), F32),
        ]
        + [
            jax.ShapeDtypeStruct(
                (2, width) if stop - start == 2 * width else (stop - start,), F32
            )
            for _, start, stop in vectors
        ],
        scratch_shapes=[
            pltpu.VMEM((rows, model), F32),
            pltpu.VMEM((loose, model), F32),
            pltpu.VMEM((len(parts), *parts[0].shape), F32),
        ],
        compiler_params=pltpu.CompilerParams(vmem_limit_bytes=VMEM_LIMIT),
        cost_estimate=SMALL,
        name="end",
    )(place, wide, gathered, *parts)


def attend_kernel(heads, scale, place_ref, query_ref, *refs):
    pair_refs, (out_ref, turned_ref, level_ref), refs = refs[:4], refs[4:7], refs[7:]
    block_refs, held = refs[:-1], refs[-1]
    width = heads * HEAD_DIM
    count = pair_refs[0].shape[0]
    outs, levels = [], []
    for head in range(heads):
        cols = slice(head * HEAD_DIM, (head + 1) * HEAD_DIM)
        query = query_ref[:, cols] * jnp.asarray(scale, BF)
        top = None
        for index, pair in enumerate(pair_refs):
            scores = product(pair[:, cols], query, 1, 1)
            held[index * count : (index + 1) * count, :] = scores
            high = jnp.max(scores, axis=0, keepdims=True)
            top = high if top is None else jnp.maximum(top, high)
        weight, out = 0.0, 0.0
        vcols = slice(width + head * HEAD_DIM, width + (head + 1) * HEAD_DIM)
        for index, pair in enumerate(pair_refs):
            soft = jnp.exp(held[index * count : (index + 1) * count, :] - top)
            weight = weight + jnp.sum(soft, axis=0, keepdims=True)
            out = out + product(pair[:, vcols], soft.astype(BF), 0, 0)
        outs.append(out / weight)
        levels.append(top + jnp.log(weight))
    joined = jnp.concatenate(outs, axis=0)
    turned_ref[...] = joined
    out_ref[...] = joined.T.astype(BF)
    level_ref[...] = jnp.concatenate(levels, axis=0)
    rows = block_refs[0].shape[0]
    for j, block in enumerate(block_refs):
        start = pl.multiple_of(lax.rem(place_ref[0] + j, len(block_refs)) * rows, rows)
        block[...] = out_ref[pl.ds(start, rows), :]


def attend(place, query, pairs, mps):
    rows, width = query.shape
    heads = width // HEAD_DIM
    vmem = pl.BlockSpec(memory_space=pltpu.VMEM)
    return pl.pallas_call(
        functools.partial(attend_kernel, heads, HEAD_DIM ** (-0.5)),
        in_specs=[pl.BlockSpec(memory_space=pltpu.SMEM)] + [vmem] * 5,
        out_shape=[
            jax.ShapeDtypeStruct((rows, width), BF),
            jax.ShapeDtypeStruct((width, rows), F32),
            jax.ShapeDtypeStruct((heads, rows), F32),
        ]
        + [jax.ShapeDtypeStruct((rows // mps, width), BF)] * mps,
        scratch_shapes=[pltpu.VMEM((rows * len(pairs), rows), F32)],
        compiler_params=pltpu.CompilerParams(vmem_limit_bytes=VMEM_LIMIT),
        cost_estimate=SMALL,
        name="attend",
    )(place, query, *pairs)


def attend_back_kernel(heads, scale, place_ref, query_ref, turned_ref, level_ref, *refs):
    pair_refs, refs = refs[:4], refs[4:]
    block_refs, (query_out, near_out, far_out, core_out, grad_ref) = refs[:-5], refs[-5:]
    width = heads * HEAD_DIM
    rows = block_refs[0].shape[0]
    for j, block in enumerate(block_refs):
        start = pl.multiple_of(lax.rem(place_ref[0] + j, len(block_refs)) * rows, rows)
        grad_ref[pl.ds(start, rows), :] = block[...]
    grads_turned = grad_ref[...].astype(F32).T
    query_grads = []
    pair_grads = [([], []) for _ in range(4)]
    for head in range(heads):
        cols = slice(head * HEAD_DIM, (head + 1) * HEAD_DIM)
        vcols = slice(width + head * HEAD_DIM, width + (head + 1) * HEAD_DIM)
        query = query_ref[:, cols] * jnp.asarray(scale, BF)
        grad = grad_ref[:, cols]
        level = level_ref[head : head + 1, :]
        delta = jnp.sum(grads_turned[cols, :] * turned_ref[cols, :], axis=0, keepdims=True)
        query_grad = 0.0
        for index in range(4):
            pair = pair_refs[index]
            key = pair[:, cols]
            soft = jnp.exp(product(key, query, 1, 1) - level)
            grad_soft = product(pair[:, vcols], grad, 1, 1)
            low = (soft * (grad_soft - delta)).astype(BF)
            pair_grads[index][0].append(product(low, query))
            pair_grads[index][1].append(product(soft.astype(BF), grad))
            query_grad = query_grad + product(key, low, 0, 0)
        query_grads.append(query_grad * scale)
    query_out[...] = jnp.concatenate(query_grads, axis=0).T.astype(BF)
    near, near_core, far, far_core = [
        jnp.concatenate(keys + values, axis=1) for keys, values in pair_grads
    ]
    near_out[...] = near.astype(BF)
    far_out[...] = far.astype(BF)
    core_out[0] = near_core.astype(BF)
    core_out[1] = far_core.astype(BF)


def attend_back(place, query, turned_out, level, pairs, blocks):
    rows, width = query.shape
    heads = width // HEAD_DIM
    vmem = pl.BlockSpec(memory_space=pltpu.VMEM)
    return pl.pallas_call(
        functools.partial(attend_back_kernel, heads, HEAD_DIM ** (-0.5)),
        in_specs=[pl.BlockSpec(memory_space=pltpu.SMEM)] + [vmem] * (7 + len(blocks)),
        out_shape=[
            jax.ShapeDtypeStruct((rows, width), BF),
            jax.ShapeDtypeStruct((rows, 2 * width), BF),
            jax.ShapeDtypeStruct((rows, 2 * width), BF),
            jax.ShapeDtypeStruct((2, rows, 2 * width), BF),
        ],
        scratch_shapes=[pltpu.VMEM((rows, width), BF)],
        compiler_params=pltpu.CompilerParams(vmem_limit_bytes=VMEM_LIMIT),
        cost_estimate=SMALL,
        name="attend_back",
    )(place, query, turned_out, level, *pairs, *blocks)


def gelu_parts(value):
    share = 0.5 + 0.5 * lax.erf(value * math.sqrt(0.5))
    slope = share + value * jnp.exp(-0.5 * value * value) * (1.0 / math.sqrt(2.0 * math.pi))
    return value * share, slope


def hold_kernel(which_ref, expand_ref, reduce_ref, output_ref, bias_ref, out_ref, *turned):
    rows, columns = out_ref.shape
    model, width = expand_ref.shape[0], output_ref.shape[0]
    expand, output, bias = turned
    expand[...] = expand_ref[...].T
    output[...] = output_ref[...].T
    whole = bias_ref[...].reshape(1, -1)
    high = whole.astype(BF).astype(F32)
    both = [high, whole - high, jnp.zeros((126, whole.shape[1]), F32)]
    bias[...] = jnp.concatenate(both, axis=0).T
    here = pl.ds(pl.multiple_of(which_ref[0] * rows, rows), rows)
    out_ref[:, :model] = expand[here, :]
    out_ref[:, model : 2 * model] = reduce_ref[...]
    tail = columns - 2 * model - width
    out_ref[:, 2 * model :] = jnp.concatenate(
        [output[here, :], bias[here, :tail].astype(BF)], axis=1
    )


def hold(which, expand, reduce, output, bias, rows):
    model, hidden = expand.shape
    width = output.shape[0]
    columns = -(-(2 * model + width + 2) // 128) * 128
    return pl.pallas_call(
        hold_kernel,
        grid_spec=pltpu.PrefetchScalarGridSpec(
            num_scalar_prefetch=1,
            grid=(1,),
            in_specs=[
                pl.BlockSpec((model, hidden), lambda i, which: (0, 0)),
                pl.BlockSpec((rows, model), lambda i, which: (which[0], 0)),
                pl.BlockSpec((width, model), lambda i, which: (0, 0)),
                pl.BlockSpec((hidden,), lambda i, which: (0,)),
            ],
            out_specs=pl.BlockSpec((rows, columns), lambda i, which: (0, 0)),
            scratch_shapes=[
                pltpu.VMEM((hidden, model), BF),
                pltpu.VMEM((model, width), BF),
                pltpu.VMEM((hidden, 128), F32),
            ],
        ),
        out_shape=jax.ShapeDtypeStruct((rows, columns), BF),
        compiler_params=pltpu.CompilerParams(vmem_limit_bytes=VMEM_LIMIT),
        cost_estimate=SMALL,
        name="hold",
    )(which, expand, reduce, output, bias)


def across_of(weights_ref, j, mps, width):
    rows = weights_ref.shape[0] // (8 * mps)
    places = [(p * mps + j % mps) * rows for p in range(8)]
    return jnp.concatenate([weights_ref[place : place + rows, :width] for place in places], axis=0)


def norm_parts(value):
    centre = value - jnp.mean(value, axis=-1, keepdims=True)
    inverse = lax.rsqrt(jnp.mean(centre * centre, axis=-1, keepdims=True) + 1e-05)
    return centre * inverse, inverse


def norm_pull(grad, gain, xhat, inverse):
    e = grad * gain
    shared = jnp.mean(e, axis=-1, keepdims=True) + xhat * jnp.mean(e * xhat, axis=-1, keepdims=True)
    return (e - shared) * inverse


def join_kernel(weights_ref, resid_ref, vectors_ref, *refs):
    heads_refs, (resid_out, normed_out) = refs[:-2], refs[-2:]
    mps, width = len(heads_refs), heads_refs[0].shape[1]
    resid = resid_ref[...] + vectors_ref[0:1, :]
    for j in range(mps):
        part = across_of(weights_ref, -j, mps, width)
        resid = resid + product(heads_refs[j][...], part, 1, 1)
    resid_out[...] = resid
    xhat, _ = norm_parts(resid)
    normed_out[...] = (xhat * vectors_ref[2:3, :] + vectors_ref[3:4, :]).astype(BF)


def join(weights, heads, resid, vectors):
    rows, model = resid.shape
    wide = weights.shape[1] % 256 + 256 if weights.shape[1] % 256 else 256
    vmem = pl.BlockSpec(memory_space=pltpu.VMEM)
    return pl.pallas_call(
        join_kernel,
        grid=(1,),
        in_specs=[
            pl.BlockSpec((weights.shape[0], wide), lambda i: (0, weights.shape[1] // wide - 1)),
        ]
        + [vmem] * (2 + len(heads)),
        out_specs=[vmem, vmem],
        out_shape=[
            jax.ShapeDtypeStruct((rows, model), F32),
            jax.ShapeDtypeStruct((rows, model), BF),
        ],
        compiler_params=pltpu.CompilerParams(vmem_limit_bytes=VMEM_LIMIT),
        cost_estimate=SMALL,
        name="join",
    )(weights, resid, vectors, *heads)


def middle_kernel(
    mps,
    width,
    weights_ref,
    across_ref,
    resid_ref,
    normed_ref,
    cotangent_ref,
    vectors_ref,
    shown_ref,
    grad_ref,
    sums_ref,
    *refs,
):
    grad_heads_refs, (forward, backward) = refs[:mps], refs[mps:]
    rows, model = resid_ref.shape
    step = pl.program_id(0)

    @pl.when(step == 0)
    def _():
        forward[...] = jnp.zeros_like(forward)
        backward[...] = jnp.zeros_like(backward)

    expand = weights_ref[:, :model]
    reduce = weights_ref[:, model : 2 * model]
    tail = weights_ref[:, weights_ref.shape[1] - 128 :]
    lane = lax.broadcasted_iota(jnp.int32, (rows, 128), 1)
    bias_lane = 2 * model + width - (weights_ref.shape[1] - 128)
    ones = jnp.where(jnp.logical_or(lane == bias_lane, lane == bias_lane + 1), 1.0, 0.0).astype(BF)
    value = product(normed_ref[...], expand, 1, 1) + product(ones, tail, 1, 1)
    active, slope = gelu_parts(value)
    forward[...] += product(active.astype(BF), reduce)
    grad_mlp = cotangent_ref[...].astype(BF)
    grad = (product(grad_mlp, reduce, 1, 1) * slope).astype(BF)
    backward[...] += product(grad, expand)

    @pl.when(step == pl.num_programs(0) - 1)
    def _():
        resid = resid_ref[...]
        shown_ref[:, model:] = (resid + forward[...] + vectors_ref[1:2, :]).astype(BF)
        xhat, inverse = norm_parts(resid)
        grad = backward[...]
        grad_resid = cotangent_ref[...] + norm_pull(grad, vectors_ref[2:3, :], xhat, inverse)
        grad_ref[...] = grad_resid
        attn = grad_resid.astype(BF)
        shown_ref[:, :model] = attn
        sums_ref[...] = jnp.concatenate(
            [
                jnp.sum(grad * xhat, axis=0, keepdims=True),
                jnp.sum(grad, axis=0, keepdims=True),
                jnp.sum(attn.astype(F32), axis=0, keepdims=True),
                jnp.zeros((5, model), F32),
            ],
            axis=0,
        )
        for j in range(mps):
            part = across_of(across_ref, j, mps, width)
            grad_heads_refs[j][...] = product(attn, part).astype(BF)


def middle(weights, resid, normed, cotangent, vectors, mps, width):
    rows, model = resid.shape
    wide = weights.shape[1] % 256 + 256 if weights.shape[1] % 256 else 256
    chunk = 1024
    vmem = pl.BlockSpec(memory_space=pltpu.VMEM)
    return pl.pallas_call(
        functools.partial(middle_kernel, mps, width),
        grid=(weights.shape[0] // chunk,),
        in_specs=[
            pl.BlockSpec((chunk, weights.shape[1]), lambda i: (i, 0)),
            pl.BlockSpec((weights.shape[0], wide), lambda i: (0, weights.shape[1] // wide - 1)),
        ]
        + [vmem] * 4,
        out_specs=[vmem] * (3 + mps),
        out_shape=[
            jax.ShapeDtypeStruct((rows, 2 * model), BF),
            jax.ShapeDtypeStruct((rows, model), F32),
            jax.ShapeDtypeStruct((8, model), F32),
        ]
        + [jax.ShapeDtypeStruct((rows, width), BF)] * mps,
        scratch_shapes=[pltpu.VMEM((rows, model), F32)] * 2,
        compiler_params=pltpu.CompilerParams(vmem_limit_bytes=VMEM_LIMIT),
        cost_estimate=SMALL,
        name="middle",
    )(weights, weights, resid, normed, cotangent, vectors)


def feed_kernel(chunk, places_ref, expand_ref, reduce_ref, bias_ref, grad_ref, *refs):
    normed_refs, refs = refs[:-7], refs[-7:]
    mine_out, other_out, bias_out, normed, normed_turned, held, second_held = refs
    rows = normed_refs[0].shape[0]
    for j, ref in enumerate(normed_refs):
        normed[j * rows : (j + 1) * rows, :] = ref[...]
    normed_turned[...] = normed[...].T
    hidden = expand_ref.shape[1]
    for start in range(0, hidden, chunk):
        here = slice(start, start + chunk)
        value = product(normed[...], expand_ref[:, here]) + bias_ref[:, here]
        active, slope = gelu_parts(value)
        grad = product(grad_ref[...], reduce_ref[here, :], 1, 1) * slope
        low = grad.astype(BF)
        second_held[here, :] = product(active.astype(BF), grad_ref[...], 0, 0)
        held[:, here] = product(normed_turned[...], low)
        bias_out[:, here] = jnp.sum(low.astype(F32), axis=0, keepdims=True)
    core_rows(held, places_ref[1], mine_out, other_out)
    core_rows(second_held, places_ref[1], mine_out, other_out, held.shape[0] // 2)


def feed(places, expand, reduce, bias, grad, normed_blocks):
    model, hidden = expand.shape
    rows = grad.shape[0]
    vmem = pl.BlockSpec(memory_space=pltpu.VMEM)
    half = (model + hidden) // 2
    return pl.pallas_call(
        functools.partial(feed_kernel, 256),
        in_specs=[pl.BlockSpec(memory_space=pltpu.SMEM)] + [vmem] * (4 + len(normed_blocks)),
        out_shape=[
            jax.ShapeDtypeStruct((half, model), BF),
            jax.ShapeDtypeStruct((half, model), BF),
            jax.ShapeDtypeStruct((1, hidden), F32),
        ],
        scratch_shapes=[
            pltpu.VMEM((rows, model), BF),
            pltpu.VMEM((model, rows), BF),
            pltpu.VMEM((model, hidden), F32),
            pltpu.VMEM((hidden, model), F32),
        ],
        compiler_params=pltpu.CompilerParams(vmem_limit_bytes=VMEM_LIMIT),
        cost_estimate=SMALL,
        name="feed",
    )(places, expand, reduce, bias, grad, *normed_blocks)


def project_kernel(places_ref, packed_ref, normed_ref, attended_ref, attn_ref, *refs):
    mine_out, other_out, held = refs
    wide = packed_ref.shape[1]
    held[:wide, :] = product(packed_ref[...], normed_ref[...], 0, 0)
    held[wide:, :] = product(attended_ref[...], attn_ref[...], 0, 0)
    core_rows(held, places_ref[1], mine_out, other_out)


def project_weights(places, packed, normed, attended, shown):
    frames, wide = packed.shape
    width, model = attended.shape[1], normed.shape[1]
    vmem = pl.BlockSpec(memory_space=pltpu.VMEM)
    half = (wide + width) // 2
    return pl.pallas_call(
        project_kernel,
        grid=(1,),
        in_specs=[pl.BlockSpec(memory_space=pltpu.SMEM)]
        + [vmem] * 3
        + [pl.BlockSpec((frames, model), lambda i: (0, 0))],
        out_specs=[vmem, vmem],
        out_shape=[jax.ShapeDtypeStruct((half, model), BF)] * 2,
        scratch_shapes=[pltpu.VMEM((wide + width, model), F32)],
        compiler_params=pltpu.CompilerParams(vmem_limit_bytes=VMEM_LIMIT),
        cost_estimate=SMALL,
        name="project_weights",
    )(places, packed, normed, attended, shown)


def pieces_kernel(places_ref, feed_ref, feed_got_ref, project_ref, project_got_ref, *outs):
    part = project_ref.shape[0] // 4
    pairs = (
        (feed_ref, feed_got_ref, 0),
        (feed_ref, feed_got_ref, 4 * part),
        (project_ref, project_got_ref, 0),
    )
    for d, out in enumerate(outs):
        for which, (mine, got, start) in enumerate(pairs):
            place = start + jnp.bitwise_xor(places_ref[3], d) * part
            here = pl.ds(pl.multiple_of(place, part), part)
            value = mine[here, :].astype(F32) + got[here, :].astype(F32)
            out[which * part : (which + 1) * part, :] = value.astype(out.dtype)


def pieces(places, feed_mine, feed_got, project_mine, project_got):
    vmem = pl.BlockSpec(memory_space=pltpu.VMEM)
    model = feed_mine.shape[1]
    part = 3 * project_mine.shape[0] // 4
    return pl.pallas_call(
        pieces_kernel,
        in_specs=[pl.BlockSpec(memory_space=pltpu.SMEM)] + [vmem] * 4,
        out_shape=[jax.ShapeDtypeStruct((part, model), F32)]
        + [jax.ShapeDtypeStruct((part, model), BF)] * 3,
        compiler_params=pltpu.CompilerParams(vmem_limit_bytes=VMEM_LIMIT),
        cost_estimate=SMALL,
        name="pieces",
    )(places, feed_mine, feed_got, project_mine, project_got)


def pack_kernel(place_ref, query_ref, pair_ref, core_ref, other_ref, weight_ref, *outs):
    packed_out, sums_out, own_out, *others_out = outs
    pair = pair_ref[...].astype(F32) + core_ref[0].astype(F32) + other_ref[...].astype(F32)
    packed = jnp.concatenate([query_ref[...], pair.astype(BF)], axis=1)
    packed_out[...] = packed
    sums_out[...] = jnp.sum(packed.astype(F32), axis=0, keepdims=True)
    rows = own_out.shape[0]
    mps = len(others_out) + 1

    def part(j):
        start = pl.multiple_of(lax.rem(place_ref[0] + j, mps) * rows, rows)
        return product(packed_out[pl.ds(start, rows), :], weight_ref[...])

    own_out[...] = part(0)
    for j in range(1, mps):
        others_out[j - 1][...] = part(j).astype(BF)


def pack(place, query, pair, pair_core, pair_far, weight, mps):
    frames, width = query.shape
    model, rows = weight.shape[1], frames // mps
    vmem = pl.BlockSpec(memory_space=pltpu.VMEM)
    return pl.pallas_call(
        pack_kernel,
        grid=(1,),
        in_specs=[
            pl.BlockSpec(memory_space=pltpu.SMEM),
            vmem,
            vmem,
            pl.BlockSpec((1, frames, 2 * width), lambda i: (0, 0, 0)),
            vmem,
            vmem,
        ],
        out_specs=[vmem] * (2 + mps),
        out_shape=[
            jax.ShapeDtypeStruct((frames, 3 * width), BF),
            jax.ShapeDtypeStruct((1, 3 * width), F32),
            jax.ShapeDtypeStruct((rows, model), F32),
        ]
        + [jax.ShapeDtypeStruct((rows, model), BF)] * (mps - 1),
        compiler_params=pltpu.CompilerParams(vmem_limit_bytes=VMEM_LIMIT),
        cost_estimate=SMALL,
        name="pack",
    )(place, query, pair, pair_core, pair_far, weight)


def pull_kernel(resid_ref, grad_ref, stem_ref, gain_ref, sums_ref, *refs):
    got_refs, out_ref = refs[:-1], refs[-1]
    rows, model = resid_ref.shape
    grad = got_refs[0][...].astype(F32)
    for ref in got_refs[1:]:
        grad = grad + ref[...].astype(F32)
    xhat, inverse = norm_parts(resid_ref[...])
    grad_resid = grad_ref[...] + norm_pull(grad, gain_ref[...], xhat, inverse)
    _, slope = gelu_parts(stem_ref[...])
    low = (grad_resid * slope).astype(BF)
    out_ref[:rows, :] = low
    sums = jnp.concatenate(
        [
            jnp.sum(grad * xhat, axis=0, keepdims=True),
            jnp.sum(grad, axis=0, keepdims=True),
            sums_ref[0:3, :],
            jnp.sum(low.astype(F32), axis=0, keepdims=True),
            jnp.zeros((10, model), F32),
        ],
        axis=0,
    )
    out_ref[rows:, :] = sums.astype(BF)


def pull(resid, grad, stem, gain, sums, got):
    rows, model = resid.shape
    return pl.pallas_call(
        pull_kernel,
        out_shape=jax.ShapeDtypeStruct((rows + 16, model), BF),
        compiler_params=pltpu.CompilerParams(vmem_limit_bytes=VMEM_LIMIT),
        cost_estimate=SMALL,
        name="pull",
    )(resid, grad, stem, gain, sums, *got)


def second_kernel_body(mps, places_ref, taps_ref, gathered_ref, *refs):
    grad_out, sums_out, mine_out, other_out, held = refs
    rows = gathered_ref.shape[0] // mps
    own = rows - 16
    sums = 0.0
    for j in range(mps):
        grad_out[j * own : (j + 1) * own, :] = gathered_ref[j * rows : j * rows + own, :]
        sums = sums + gathered_ref[j * rows + own : (j + 1) * rows, :].astype(F32)
    sums_out[...] = sums
    held[...] = product(taps_ref[...], grad_out[...], 0, 0)
    core_rows(held, places_ref[1], mine_out, other_out)


def second_weight(places, taps, gathered, mps):
    frames, tall = taps.shape
    model = gathered.shape[1]
    vmem = pl.BlockSpec(memory_space=pltpu.VMEM)
    return pl.pallas_call(
        functools.partial(second_kernel_body, mps),
        in_specs=[pl.BlockSpec(memory_space=pltpu.SMEM)] + [vmem] * 2,
        out_shape=[
            jax.ShapeDtypeStruct((frames, model), BF),
            jax.ShapeDtypeStruct((16, model), F32),
            jax.ShapeDtypeStruct((tall // 2, model), F32),
            jax.ShapeDtypeStruct((tall // 2, model), BF),
        ],
        scratch_shapes=[pltpu.VMEM((tall, model), F32)],
        compiler_params=pltpu.CompilerParams(vmem_limit_bytes=VMEM_LIMIT),
        cost_estimate=SMALL,
        name="second_weight",
    )(places, taps, gathered)


def stem_back_kernel(
    bands,
    places_ref,
    grad_ref,
    edges_ref,
    matrix_ref,
    even_ref,
    odd_ref,
    rim_ref,
    window_ref,
    back_ref,
    sums_ref,
    reduce_ref,
    expand_ref,
    project_ref,
    loose_out,
    spectrum_out,
    held,
):
    frames = grad_ref.shape[0]
    width = even_ref.shape[1]
    row = lax.broadcasted_iota(jnp.int32, (frames, width), 0)

    def later(value, last):
        return jnp.where(row == frames - 1, last, pltpu.roll(value, frames - 1, 0))

    def earlier(value, start):
        return jnp.where(row == 0, start, pltpu.roll(value, 1, 0))

    def slope(value):
        return gelu_parts(value)[1]

    def rounded(value):
        return value.astype(BF).astype(F32)

    taps = product(grad_ref[...], matrix_ref[...], 1, 1)
    rims = product(edges_ref[...], matrix_ref[...], 1, 1)
    even = rounded(taps[:, width : 2 * width] * slope(even_ref[...]))
    odd = taps[:, 2 * width :] + later(taps[:, :width], rims[1:2, :width])
    odd = rounded(odd * slope(odd_ref[...]))
    rim_slope = slope(rim_ref[...])
    inside = (places_ref[2] > 0).astype(F32)
    odd_before = rounded((rims[0:1, 2 * width :] + taps[0:1, :width]) * rim_slope[0:1] * inside)
    even_after = rounded(rims[1:2, width : 2 * width] * rim_slope[1:2])
    bias = jnp.sum(even + odd, axis=0, keepdims=True)
    both = jnp.concatenate([even, odd], axis=1).astype(BF)
    weight = product(window_ref[...], both, 0, 0)
    weight = weight[: 3 * bands, :width] + weight[bands:, width:]
    spare = held.shape[1] - 3 * width
    held[:bands, :] = jnp.concatenate(
        [weight[k * bands : (k + 1) * bands] for k in range(3)] + [jnp.zeros((bands, spare), F32)],
        axis=1,
    )
    last = jnp.concatenate(
        [project_ref[:, :width], project_ref[:, 2 * width :], bias, jnp.zeros((1, spare), F32)],
        axis=1,
    )
    blank = jnp.zeros((held.shape[0] - bands - 9, held.shape[1]), F32)
    held[bands:, :] = jnp.concatenate(
        [sums_ref[0:6, :], reduce_ref[...], expand_ref[...], last, blank], axis=0
    )
    few = loose_out.shape[1]
    for p in range(8):
        loose_out[p] = held[p * few : (p + 1) * few, :]
    before = earlier(odd, odd_before).astype(BF)
    following = later(even, even_after).astype(BF)
    even, odd = even.astype(BF), odd.astype(BF)
    back = [back_ref[k * width : (k + 1) * width, :] for k in range(3)]
    spectrum = [
        product(before, back[0]) + product(even, back[1]) + product(odd, back[2]),
        product(even, back[0]) + product(odd, back[1]) + product(following, back[2]),
    ]
    spectrum_out[...] = jnp.concatenate(spectrum, axis=1).astype(BF)


def stem_back(places, grad, edges, matrix, even, odd, rim, window, back_matrix, *sums):
    frames, width = even.shape
    bands, model = back_matrix.shape[1], grad.shape[1]
    vmem = pl.BlockSpec(memory_space=pltpu.VMEM)
    return pl.pallas_call(
        functools.partial(stem_back_kernel, bands),
        in_specs=[pl.BlockSpec(memory_space=pltpu.SMEM)] + [vmem] * (8 + len(sums)),
        out_shape=[
            jax.ShapeDtypeStruct((8, (bands + 16) // 8, model), F32),
            jax.ShapeDtypeStruct((frames, 2 * bands), BF),
        ],
        scratch_shapes=[pltpu.VMEM((bands + 16, model), F32)],
        compiler_params=pltpu.CompilerParams(vmem_limit_bytes=VMEM_LIMIT),
        cost_estimate=SMALL,
        name="stem_back",
    )(places, grad, edges, matrix, even, odd, rim, window, back_matrix, *sums)


def on_device(
    spectrogram,
    first_kernel,
    first_bias,
    second_kernel,
    second_bias,
    attend_gain,
    attend_shift,
    project_weight,
    project_bias,
    output_weight,
    output_bias,
    mixer_gain,
    mixer_shift,
    expand_weight,
    expand_bias,
    reduce_weight,
    reduce_bias,
    cotangent,
):
    _, steps, bands = spectrogram.shape
    frames = steps // 2
    width = first_kernel.shape[2]
    model = second_kernel.shape[2]
    hidden = expand_weight.shape[1]
    mps, seqs = lax.axis_size("mp"), lax.axis_size("seq")
    z, seq = lax.axis_index("mp"), lax.axis_index("seq")
    core = lax.rem(seq, 2)
    rows = frames // mps

    held = hold(
        (2 * plane_index() + core).reshape(1),
        expand_weight,
        reduce_weight,
        output_weight,
        expand_bias,
        hidden // 8,
    )
    weights_got = gather_mp(held, "weights_mp")

    paired = spectrogram.reshape(frames, 2 * bands)
    before = passed_along(paired[-1:], 1)
    following = passed_along(paired[:1], -1)
    ahead = jnp.concatenate([before, paired, following], axis=0)
    window = jnp.concatenate(
        [ahead[:-2, bands:], ahead[1:-1], ahead[2:, :bands]], axis=1
    )
    prior = jnp.concatenate([before, paired[:1, :bands]], axis=1)
    latter = jnp.concatenate([paired[-1:, bands:], following], axis=1)
    first_matrix = first_kernel.reshape(3 * bands, width)
    even_in = jnp.concatenate([window[:, : 3 * bands], latter], axis=0)
    odd_in = jnp.concatenate([prior, window[:, bands:]], axis=0)
    pre_even = product(even_in, first_matrix) + first_bias
    pre_odd = product(odd_in, first_matrix) + first_bias
    inside = jnp.logical_or(jnp.arange(frames + 1) > 0, seq > 0)[:, None]
    hidden_even = exact_gelu(pre_even[:frames]).astype(BF)
    hidden_odd = jnp.where(inside, exact_gelu(pre_odd), 0.0).astype(BF)
    taps = jnp.concatenate([hidden_odd[:frames], hidden_even, hidden_odd[1:]], axis=1)
    second_matrix = second_kernel.reshape(3 * width, model)
    stem_part = product(taps, second_matrix)
    own_cotangent = rolled_blocks(cotangent.reshape(frames, model))
    early = (
        own_cotangent[0],
        jnp.concatenate(own_cotangent, axis=0).astype(BF),
        jnp.stack([output_bias, reduce_bias, mixer_gain, mixer_shift]),
        column_total(cotangent.reshape(frames, model).astype(BF))[None],
        jnp.transpose(first_kernel[::-1], (0, 2, 1)).reshape(3 * width, bands),
        jnp.concatenate([pre_odd[:1], pre_even[frames:], jnp.zeros((6, width), F32)], axis=0),
        pre_even[:frames],
        pre_odd[1:],
        window,
        taps,
        sinusoid(seq * frames + z * rows, rows, model),
        jnp.stack([z, core, seq, plane_index()]),
        z.reshape(1),
        attend_gain.reshape(1, model),
        expand_bias.reshape(1, hidden),
    )
    stem_part, weights_got, early = lax.optimization_barrier((stem_part, weights_got, early))
    own_cotangent, grad_mlp, vectors, reduce_bias_part, back_matrix = early[:5]
    rim, even_level, odd_level, window, taps, table = early[5:11]
    places, place, attend_gain_row, expand_bias_row = early[11:]
    with jax.named_scope("weights_plane"):
        weights_all = plane_gather(jnp.concatenate(weights_got, axis=0))
    stem_pre = scatter_sum(rolled_blocks(stem_part), "stem_sum") + second_bias
    resid_zero = exact_gelu(stem_pre) + table
    normed_one = lax.all_gather(
        layer_norm(resid_zero, attend_gain, attend_shift).astype(BF), "mp", axis=0, tiled=True
    )

    project_matrix = project_weight.transpose(1, 2, 0).reshape(3 * width, model)
    offsets = jnp.concatenate([project_bias[0], jnp.zeros_like(project_bias[0]), project_bias[1]])
    packed = (product(normed_one, project_matrix, 1, 1) + offsets).astype(BF)
    query, pair = packed[:, :width], packed[:, width:]
    pair_far = swapped(pair, "seq", 2, "pair_far")
    pair_core = swapped(pair, "seq", 1, "pair_core")
    pair_far_core = swapped(pair_far, "seq", 1, "pair_far_core")
    pairs = [pair, pair_core, pair_far, pair_far_core]
    attended, attended_turned, level, *attended_blocks = attend(place, query, pairs, mps)
    heads_got = exchange_mp(attended_blocks, "attended")
    resid_one, normed_two_own = join(weights_all, heads_got, resid_zero, vectors)
    normed_two_all = gather_mp(normed_two_own, "normed_two")
    shown_own, grad_resid_one, middle_sums, *grad_heads = middle(
        weights_all,
        resid_one,
        normed_two_own,
        own_cotangent,
        vectors,
        mps,
        width,
    )
    shown = lax.all_gather(shown_own, "mp", axis=0, tiled=True)
    rows_got = exchange_mp(grad_heads, "grad_heads")
    grad_attended = natural([rows_got[-j % mps] for j in range(mps)])
    grad_attended, normed_two_all = lax.optimization_barrier((grad_attended, normed_two_all))

    query_grad, near, far, cores = attend_back(
        place,
        query,
        attended_turned,
        level,
        pairs,
        [grad_attended],
    )
    cores_got = swapped(cores, "seq", 1, "grad_core")
    far = (far.astype(F32) + cores_got[1].astype(F32)).astype(BF)
    far_got = swapped(far, "seq", 2, "grad_far")
    feed_mine, feed_other, expand_bias_part = feed(
        places,
        expand_weight,
        reduce_weight,
        expand_bias_row,
        after(grad_mlp, far),
        normed_two_all,
    )
    far_got, feed_other = lax.optimization_barrier((far_got, feed_other))
    feed_got = swapped(feed_other, "seq", 1, "feed_core")
    grad_packed, project_columns, *normed_parts = pack(
        place, query_grad, near, cores_got, far_got, project_matrix, mps
    )
    normed_got = exchange_mp(normed_parts, "grad_normed_one")

    project_mine, project_other = project_weights(places, grad_packed, normed_one, attended, shown)
    project_got = swapped(project_other, "seq", 1, "project_core")
    wide_pieces = pieces(places, feed_mine, feed_got, project_mine, project_got)
    normed_got, wide_pieces = lax.optimization_barrier((normed_got, wide_pieces))
    wide_parts = [
        plane_move(piece, d, "wide_scatter") for d, piece in zip((1, 2, 3), wide_pieces[1:])
    ]

    grad_stem_own = pull(
        resid_zero, grad_resid_one, stem_pre, attend_gain_row, middle_sums, normed_got
    )
    with jax.named_scope("grad_stem"):
        gathered = lax.all_gather(grad_stem_own, "mp", axis=0, tiled=True)
    gathered, wide_parts = lax.optimization_barrier((gathered, wide_parts))
    with jax.named_scope("wide_gather"):
        wide_all = plane_gather(rest_of_dp(total([wide_pieces[0]] + wide_parts).astype(BF)))
    last_row = (mps - 1) * (rows + 16) + rows - 1
    stem_before = passed_along(gathered[last_row : last_row + 1], 1)
    stem_following = passed_along(gathered[:1], -1)
    grad_stem, small, second_mine, second_other = second_weight(places, taps, gathered, mps)
    second_got = swapped(second_other, "seq", 1, "second_core")
    edges = jnp.concatenate([stem_before, stem_following, jnp.zeros((14, model), BF)], axis=0)
    loose, spectrum_part = stem_back(
        places,
        grad_stem,
        edges,
        second_matrix,
        even_level,
        odd_level,
        rim,
        window,
        back_matrix,
        small,
        reduce_bias_part,
        expand_bias_part,
        project_columns,
    )
    halves = loose.reshape(4, 2, -1, model)
    loose_mine = lax.dynamic_index_in_dim(halves, core, 1, keepdims=False)
    loose_other = lax.dynamic_index_in_dim(halves, 1 - core, 1, keepdims=False)
    loose_got = swapped(loose_other.astype(BF), "seq", 1, "small_core")

    joined = jnp.concatenate(
        [
            (second_mine + second_got.astype(F32)).reshape(4, -1, model),
            loose_mine + loose_got.astype(F32),
        ],
        axis=1,
    )
    spectrum_parts = gather_mp(spectrum_part, "spectrum")
    joined, shown = lax.optimization_barrier((joined, shown))
    piece = plane_scatter(joined, "last_scatter")
    encoded = shown[:, model:].astype(F32)
    piece, encoded = lax.optimization_barrier((piece, encoded))
    with jax.named_scope("last_gather"):
        last = plane_gather(piece[None])
    last, spectrum_parts, wide_all = lax.optimization_barrier((last, spectrum_parts, wide_all))
    rows_of = (model, model, model, model, model, model, model, hidden)
    cuts = tuple((row, 0, size) for row, size in enumerate(rows_of))
    cuts += ((8, 0, 2 * width), (8, 2 * width, 3 * width))
    expand_sum, reduce_sum, project_sum, output_sum, spectrum, second_sum, first_sum, *sums = end(
        place, wide_all, last, spectrum_parts, bands, bands + 16, width, cuts
    )
    spectrogram_gradient = spectrum.reshape(1, steps, bands)
    return (
        encoded.reshape(1, frames, model),
        spectrogram_gradient,
        first_sum.reshape(3, bands, width),
        sums[9],
        second_sum.reshape(3, width, model),
        sums[5],
        sums[0],
        sums[1],
        project_sum.T.reshape(model, 3, width),
        sums[8],
        output_sum,
        sums[4],
        sums[2],
        sums[3],
        expand_sum,
        sums[7],
        reduce_sum,
        sums[6],
    )


def solution(mesh):
    return jax.shard_map(
        on_device,
        mesh=mesh,
        in_specs=(
            P("dp", "seq", None),
            P(None, None, "mp"),
            P("mp"),
            P(None, "mp", None),
            P(),
            P(),
            P(),
            P(None, None, "mp"),
            P(None, "mp"),
            P("mp", None),
            P(),
            P(),
            P(),
            P(None, "mp"),
            P("mp"),
            P("mp", None),
            P(),
            P("dp", "seq", None),
        ),
        out_specs=(
            P("dp", "seq", None),
            P("dp", "seq", None),
            P(None, None, "mp"),
            P("mp"),
            P(None, "mp", None),
            P(),
            P(),
            P(),
            P(None, None, "mp"),
            P(None, "mp"),
            P("mp", None),
            P(),
            P(),
            P(),
            P(None, "mp"),
            P("mp"),
            P("mp", None),
            P(),
        ),
        check_vma=False,
    )
```

```python
import functools
import math

import jax
import jax.numpy as jnp
from jax import lax
from jax.experimental import pallas as pl
from jax.experimental.pallas import tpu as pltpu
from jax.sharding import PartitionSpec as P

HEAD_DIM = 64
BF = jnp.bfloat16
F32 = jnp.float32
VMEM_LIMIT = 60 * 1024 * 1024
SMALL = pl.CostEstimate(flops=1, bytes_accessed=1, transcendentals=0)


def product(left, right, left_dim=1, right_dim=0):
    dims = (((left_dim,), (right_dim,)), ((), ()))
    return lax.dot_general(left, right, dims, preferred_element_type=F32)


def after(value, *others):
    return lax.optimization_barrier((value, *others))[0]


def exact_gelu(value):
    return jax.nn.gelu(value, approximate=False)


def gelu_back(value, grad):
    return jax.vjp(exact_gelu, value)[1](grad)[0]


def layer_norm(value, gain, shift):
    centre = value - jnp.mean(value, axis=-1, keepdims=True)
    spread = jnp.mean(centre * centre, axis=-1, keepdims=True)
    return centre * lax.rsqrt(spread + 1e-05) * gain + shift


def norm_back(value, gain, grad):
    centre = value - jnp.mean(value, axis=-1, keepdims=True)
    spread = jnp.mean(centre * centre, axis=-1, keepdims=True)
    inverse = lax.rsqrt(spread + 1e-05)
    xhat = centre * inverse
    e = grad * gain
    back = (
        e - jnp.mean(e, axis=-1, keepdims=True) - xhat * jnp.mean(e * xhat, axis=-1, keepdims=True)
    ) * inverse
    return back, jnp.sum(grad * xhat, axis=0), jnp.sum(grad, axis=0)


def column_total(value):
    return jnp.sum(value.astype(F32), axis=0)


def sinusoid(start, count, width):
    half = width // 2
    rates = jnp.exp(jnp.arange(half, dtype=F32) * (-math.log(10000.0) / (half - 1)))
    times = (start + jnp.arange(count)).astype(F32)
    angles = times[:, None] * rates[None, :]
    return jnp.concatenate([jnp.sin(angles), jnp.cos(angles)], axis=1)


def turned(size, by):
    return [(i, (i + by) % size) for i in range(size)]


def gather_mp(block, name):
    size = lax.axis_size("mp")
    with jax.named_scope(name):
        return [block] + [lax.ppermute(block, "mp", turned(size, -j)) for j in range(1, size)]


def exchange_mp(blocks, name):
    size = lax.axis_size("mp")
    with jax.named_scope(name):
        got = [lax.ppermute(blocks[j], "mp", turned(size, j)) for j in range(1, size)]
    return [blocks[0]] + got


def row_blocks(value, count):
    rows = value.shape[0] // count
    return [value[j * rows : (j + 1) * rows] for j in range(count)]


def rolled_blocks(value):
    size, z = lax.axis_size("mp"), lax.axis_index("mp")
    rows = value.shape[0] // size
    return [
        lax.dynamic_slice_in_dim(value, lax.rem(z + j, size) * rows, rows, axis=0)
        for j in range(size)
    ]


def natural(blocks):
    size, z = lax.axis_size("mp"), lax.axis_index("mp")
    rows = blocks[0].shape[0]
    twice = jnp.concatenate(blocks + blocks, axis=0)
    return lax.dynamic_slice_in_dim(twice, lax.rem(size - z, size) * rows, rows * size, axis=0)


def total(parts):
    result = parts[0].astype(F32)
    for part in parts[1:]:
        result = result + part.astype(F32)
    return result


def scatter_sum(blocks, name):
    return total(exchange_mp([blocks[0]] + [block.astype(BF) for block in blocks[1:]], name))


def swapped(value, axis, bit, name):
    size = lax.axis_size(axis)
    with jax.named_scope(name):
        return lax.ppermute(value, axis, [(i, i ^ bit) for i in range(size)])


def passed_along(value, by):
    size = lax.axis_size("seq")
    pairs = [(i, i + by) for i in range(size) if 0 <= i + by < size]
    return lax.ppermute(value, "seq", pairs)


def plane_index():
    return lax.rem(lax.axis_index("dp"), 2) * 2 + lax.div(lax.axis_index("seq"), 2)


def plane_move(value, d, name):
    dps, seqs = lax.axis_size("dp"), lax.axis_size("seq")
    pairs = [
        (p * seqs + s, (p ^ (d >> 1)) * seqs + (s ^ (2 * (d & 1))))
        for p in range(dps)
        for s in range(seqs)
    ]
    with jax.named_scope(name):
        return lax.ppermute(value, ("dp", "seq"), pairs)


def rest_of_dp(value):
    dps = lax.axis_size("dp")
    if dps > 2:
        groups = [[i for i in range(dps) if i % 2 == bit] for bit in range(2)]
        value = lax.psum(value, "dp", axis_index_groups=groups)
    return value


def plane_scatter(quarters, name):
    index = plane_index()

    def piece(d):
        return lax.dynamic_index_in_dim(quarters, jnp.bitwise_xor(index, d), 0, keepdims=False)

    got = [plane_move(piece(d).astype(BF), d, name) for d in (1, 2, 3)]
    return rest_of_dp(total([piece(0)] + got).astype(BF))


def plane_gather(piece):
    dps = lax.axis_size("dp")
    if dps == 2:
        return lax.all_gather(piece, ("dp", "seq"), axis=0, tiled=True)
    pairs = [[i, i + 1] for i in range(0, dps, 2)]
    return lax.all_gather(
        lax.all_gather(piece, "seq", axis=0, tiled=True),
        "dp",
        axis=0,
        tiled=True,
        axis_index_groups=pairs,
    )


def core_rows(held, core, mine_out, other_out, start=0):
    rows = held.shape[0] // 8
    mine, others = [], []
    for quarter in range(4):
        here = pl.ds(pl.multiple_of((2 * quarter + core) * rows, rows), rows)
        there = pl.ds(pl.multiple_of((2 * quarter + 1 - core) * rows, rows), rows)
        mine.append(held[here, :])
        others.append(held[there, :])
    place = slice(start, start + 4 * rows)
    mine_out[place, :] = jnp.concatenate(mine, axis=0).astype(mine_out.dtype)
    other_out[place, :] = jnp.concatenate(others, axis=0).astype(BF)


def finish_wide_kernel(wide_ref, expand_out, reduce_out, project_out, output_out):
    part = expand_out.shape[0] // 8
    split = project_out.shape[0] // part
    for p in range(8):
        here = slice(p * part, (p + 1) * part)
        block = wide_ref[3 * p * part : 3 * (p + 1) * part, :].astype(F32)
        expand_out[here, :] = block[:part]
        reduce_out[here, :] = block[part : 2 * part]
        if p < split:
            project_out[here, :] = block[2 * part :]
        else:
            output_out[(p - split) * part : (p - split + 1) * part, :] = block[2 * part :]


def finish_kernel(bands, loose, vectors, gathered_ref, second_out, first_out, *refs):
    outs, (whole, small) = refs[:-2], refs[-2:]
    eighth = gathered_ref.shape[1]
    rows, few = eighth - loose // 8, loose // 8
    for p in range(8):
        whole[...] = gathered_ref[p].astype(F32)
        second_out[p * rows : (p + 1) * rows, :] = whole[:rows, :]
        small[p * few : (p + 1) * few, :] = whole[rows:, :]
    width = first_out.shape[1]
    for tap in range(3):
        first_out[tap * bands : (tap + 1) * bands, :] = small[
            :bands, tap * width : (tap + 1) * width
        ]
    for out, (row, start, stop) in zip(outs, vectors):
        if out.ndim == 1:
            out[...] = small[bands + row, start:stop]
        else:
            for k in range(out.shape[0]):
                place = start + k * width
                out[k : k + 1, :] = small[bands + row : bands + row + 1, place : place + width]


def spectrum_kernel(place_ref, *refs):
    parts, (out_ref, held) = refs[:-2], refs[-2:]
    for j, part in enumerate(parts):
        held[lax.rem(place_ref[0] + j, len(parts))] = part[...].astype(F32)
    result = held[0]
    for j in range(1, len(parts)):
        result = result + held[j]
    out_ref[...] = result


def end_kernel(bands, loose, vectors, mps, place_ref, wide_ref, gathered_ref, *refs):
    parts, refs = refs[:mps], refs[mps:]
    wide_outs, spectrum_out, refs = refs[:4], refs[4], refs[5:]
    outs, (whole, small, held) = refs[:-3], refs[-3:]
    finish_wide_kernel(wide_ref, *wide_outs)
    spectrum_kernel(place_ref, *parts, spectrum_out, held)
    finish_kernel(bands, loose, vectors, gathered_ref, *outs, whole, small)


def end(place, wide, gathered, parts, bands, loose, width, vectors):
    _, rows, model = gathered.shape
    vmem = pl.BlockSpec(memory_space=pltpu.VMEM)
    return pl.pallas_call(
        functools.partial(end_kernel, bands, loose, vectors, len(parts)),
        in_specs=[pl.BlockSpec(memory_space=pltpu.SMEM)] + [vmem] * (2 + len(parts)),
        out_shape=[
            jax.ShapeDtypeStruct((high, model), F32) for high in (model, model, 3 * width, width)
        ]
        + [
            jax.ShapeDtypeStruct(parts[0].shape, F32),
            jax.ShapeDtypeStruct((8 * rows - loose, model), F32),
            jax.ShapeDtypeStruct((3 * bands, width), F32),
        ]
        + [
            jax.ShapeDtypeStruct(
                (2, width) if stop - start == 2 * width else (stop - start,), F32
            )
            for _, start, stop in vectors
        ],
        scratch_shapes=[
            pltpu.VMEM((rows, model), F32),
            pltpu.VMEM((loose, model), F32),
            pltpu.VMEM((len(parts), *parts[0].shape), F32),
        ],
        compiler_params=pltpu.CompilerParams(vmem_limit_bytes=VMEM_LIMIT),
        cost_estimate=SMALL,
        name="end",
    )(place, wide, gathered, *parts)


def attend_kernel(heads, scale, place_ref, query_ref, *refs):
    pair_refs, (out_ref, turned_ref, level_ref), refs = refs[:4], refs[4:7], refs[7:]
    block_refs, held = refs[:-1], refs[-1]
    width = heads * HEAD_DIM
    count = pair_refs[0].shape[0]
    outs, levels = [], []
    for head in range(heads):
        cols = slice(head * HEAD_DIM, (head + 1) * HEAD_DIM)
        query = query_ref[:, cols] * jnp.asarray(scale, BF)
        top = None
        for index, pair in enumerate(pair_refs):
            scores = product(pair[:, cols], query, 1, 1)
            held[index * count : (index + 1) * count, :] = scores
            high = jnp.max(scores, axis=0, keepdims=True)
            top = high if top is None else jnp.maximum(top, high)
        weight, out = 0.0, 0.0
        vcols = slice(width + head * HEAD_DIM, width + (head + 1) * HEAD_DIM)
        for index, pair in enumerate(pair_refs):
            soft = jnp.exp(held[index * count : (index + 1) * count, :] - top)
            weight = weight + jnp.sum(soft, axis=0, keepdims=True)
            out = out + product(pair[:, vcols], soft.astype(BF), 0, 0)
        outs.append(out / weight)
        levels.append(top + jnp.log(weight))
    joined = jnp.concatenate(outs, axis=0)
    turned_ref[...] = joined
    out_ref[...] = joined.T.astype(BF)
    level_ref[...] = jnp.concatenate(levels, axis=0)
    rows = block_refs[0].shape[0]
    for j, block in enumerate(block_refs):
        start = pl.multiple_of(lax.rem(place_ref[0] + j, len(block_refs)) * rows, rows)
        block[...] = out_ref[pl.ds(start, rows), :]


def attend(place, query, pairs, mps):
    rows, width = query.shape
    heads = width // HEAD_DIM
    vmem = pl.BlockSpec(memory_space=pltpu.VMEM)
    return pl.pallas_call(
        functools.partial(attend_kernel, heads, HEAD_DIM ** (-0.5)),
        in_specs=[pl.BlockSpec(memory_space=pltpu.SMEM)] + [vmem] * 5,
        out_shape=[
            jax.ShapeDtypeStruct((rows, width), BF),
            jax.ShapeDtypeStruct((width, rows), F32),
            jax.ShapeDtypeStruct((heads, rows), F32),
        ]
        + [jax.ShapeDtypeStruct((rows // mps, width), BF)] * mps,
        scratch_shapes=[pltpu.VMEM((rows * len(pairs), rows), F32)],
        compiler_params=pltpu.CompilerParams(vmem_limit_bytes=VMEM_LIMIT),
        cost_estimate=SMALL,
        name="attend",
    )(place, query, *pairs)


def attend_back_kernel(heads, scale, place_ref, query_ref, turned_ref, level_ref, *refs):
    pair_refs, refs = refs[:4], refs[4:]
    block_refs, (query_out, near_out, far_out, core_out, grad_ref) = refs[:-5], refs[-5:]
    width = heads * HEAD_DIM
    rows = block_refs[0].shape[0]
    for j, block in enumerate(block_refs):
        start = pl.multiple_of(lax.rem(place_ref[0] + j, len(block_refs)) * rows, rows)
        grad_ref[pl.ds(start, rows), :] = block[...]
    grads_turned = grad_ref[...].astype(F32).T
    query_grads = []
    pair_grads = [([], []) for _ in range(4)]
    for head in range(heads):
        cols = slice(head * HEAD_DIM, (head + 1) * HEAD_DIM)
        vcols = slice(width + head * HEAD_DIM, width + (head + 1) * HEAD_DIM)
        query = query_ref[:, cols] * jnp.asarray(scale, BF)
        grad = grad_ref[:, cols]
        level = level_ref[head : head + 1, :]
        delta = jnp.sum(grads_turned[cols, :] * turned_ref[cols, :], axis=0, keepdims=True)
        query_grad = 0.0
        for index in range(4):
            pair = pair_refs[index]
            key = pair[:, cols]
            soft = jnp.exp(product(key, query, 1, 1) - level)
            grad_soft = product(pair[:, vcols], grad, 1, 1)
            low = (soft * (grad_soft - delta)).astype(BF)
            pair_grads[index][0].append(product(low, query))
            pair_grads[index][1].append(product(soft.astype(BF), grad))
            query_grad = query_grad + product(key, low, 0, 0)
        query_grads.append(query_grad * scale)
    query_out[...] = jnp.concatenate(query_grads, axis=0).T.astype(BF)
    near, near_core, far, far_core = [
        jnp.concatenate(keys + values, axis=1) for keys, values in pair_grads
    ]
    near_out[...] = near.astype(BF)
    far_out[...] = far.astype(BF)
    core_out[0] = near_core.astype(BF)
    core_out[1] = far_core.astype(BF)


def attend_back(place, query, turned_out, level, pairs, blocks):
    rows, width = query.shape
    heads = width // HEAD_DIM
    vmem = pl.BlockSpec(memory_space=pltpu.VMEM)
    return pl.pallas_call(
        functools.partial(attend_back_kernel, heads, HEAD_DIM ** (-0.5)),
        in_specs=[pl.BlockSpec(memory_space=pltpu.SMEM)] + [vmem] * (7 + len(blocks)),
        out_shape=[
            jax.ShapeDtypeStruct((rows, width), BF),
            jax.ShapeDtypeStruct((rows, 2 * width), BF),
            jax.ShapeDtypeStruct((rows, 2 * width), BF),
            jax.ShapeDtypeStruct((2, rows, 2 * width), BF),
        ],
        scratch_shapes=[pltpu.VMEM((rows, width), BF)],
        compiler_params=pltpu.CompilerParams(vmem_limit_bytes=VMEM_LIMIT),
        cost_estimate=SMALL,
        name="attend_back",
    )(place, query, turned_out, level, *pairs, *blocks)


def gelu_parts(value):
    share = 0.5 + 0.5 * lax.erf(value * math.sqrt(0.5))
    slope = share + value * jnp.exp(-0.5 * value * value) * (1.0 / math.sqrt(2.0 * math.pi))
    return value * share, slope


def hold_kernel(which_ref, expand_ref, reduce_ref, output_ref, bias_ref, out_ref, *turned):
    rows, columns = out_ref.shape
    model, width = expand_ref.shape[0], output_ref.shape[0]
    expand, output, bias = turned
    expand[...] = expand_ref[...].T
    output[...] = output_ref[...].T
    whole = bias_ref[...].reshape(1, -1)
    high = whole.astype(BF).astype(F32)
    both = [high, whole - high, jnp.zeros((126, whole.shape[1]), F32)]
    bias[...] = jnp.concatenate(both, axis=0).T
    here = pl.ds(pl.multiple_of(which_ref[0] * rows, rows), rows)
    out_ref[:, :model] = expand[here, :]
    out_ref[:, model : 2 * model] = reduce_ref[...]
    tail = columns - 2 * model - width
    out_ref[:, 2 * model :] = jnp.concatenate(
        [output[here, :], bias[here, :tail].astype(BF)], axis=1
    )


def hold(which, expand, reduce, output, bias, rows):
    model, hidden = expand.shape
    width = output.shape[0]
    columns = -(-(2 * model + width + 2) // 128) * 128
    return pl.pallas_call(
        hold_kernel,
        grid_spec=pltpu.PrefetchScalarGridSpec(
            num_scalar_prefetch=1,
            grid=(1,),
            in_specs=[
                pl.BlockSpec((model, hidden), lambda i, which: (0, 0)),
                pl.BlockSpec((rows, model), lambda i, which: (which[0], 0)),
                pl.BlockSpec((width, model), lambda i, which: (0, 0)),
                pl.BlockSpec((hidden,), lambda i, which: (0,)),
            ],
            out_specs=pl.BlockSpec((rows, columns), lambda i, which: (0, 0)),
            scratch_shapes=[
                pltpu.VMEM((hidden, model), BF),
                pltpu.VMEM((model, width), BF),
                pltpu.VMEM((hidden, 128), F32),
            ],
        ),
        out_shape=jax.ShapeDtypeStruct((rows, columns), BF),
        compiler_params=pltpu.CompilerParams(vmem_limit_bytes=VMEM_LIMIT),
        cost_estimate=SMALL,
        name="hold",
    )(which, expand, reduce, output, bias)


def across_of(weights_ref, j, mps, width):
    rows = weights_ref.shape[0] // (8 * mps)
    places = [(p * mps + j % mps) * rows for p in range(8)]
    return jnp.concatenate([weights_ref[place : place + rows, :width] for place in places], axis=0)


def norm_parts(value):
    centre = value - jnp.mean(value, axis=-1, keepdims=True)
    inverse = lax.rsqrt(jnp.mean(centre * centre, axis=-1, keepdims=True) + 1e-05)
    return centre * inverse, inverse


def norm_pull(grad, gain, xhat, inverse):
    e = grad * gain
    shared = jnp.mean(e, axis=-1, keepdims=True) + xhat * jnp.mean(e * xhat, axis=-1, keepdims=True)
    return (e - shared) * inverse


def join_kernel(weights_ref, resid_ref, vectors_ref, *refs):
    heads_refs, (resid_out, normed_out) = refs[:-2], refs[-2:]
    mps, width = len(heads_refs), heads_refs[0].shape[1]
    resid = resid_ref[...] + vectors_ref[0:1, :]
    for j in range(mps):
        part = across_of(weights_ref, -j, mps, width)
        resid = resid + product(heads_refs[j][...], part, 1, 1)
    resid_out[...] = resid
    xhat, _ = norm_parts(resid)
    normed_out[...] = (xhat * vectors_ref[2:3, :] + vectors_ref[3:4, :]).astype(BF)


def join(weights, heads, resid, vectors):
    rows, model = resid.shape
    wide = weights.shape[1] % 256 + 256 if weights.shape[1] % 256 else 256
    vmem = pl.BlockSpec(memory_space=pltpu.VMEM)
    return pl.pallas_call(
        join_kernel,
        grid=(1,),
        in_specs=[
            pl.BlockSpec((weights.shape[0], wide), lambda i: (0, weights.shape[1] // wide - 1)),
        ]
        + [vmem] * (2 + len(heads)),
        out_specs=[vmem, vmem],
        out_shape=[
            jax.ShapeDtypeStruct((rows, model), F32),
            jax.ShapeDtypeStruct((rows, model), BF),
        ],
        compiler_params=pltpu.CompilerParams(vmem_limit_bytes=VMEM_LIMIT),
        cost_estimate=SMALL,
        name="join",
    )(weights, resid, vectors, *heads)


def middle_kernel(
    mps,
    width,
    weights_ref,
    across_ref,
    resid_ref,
    normed_ref,
    cotangent_ref,
    vectors_ref,
    shown_ref,
    grad_ref,
    sums_ref,
    *refs,
):
    grad_heads_refs, (forward, backward) = refs[:mps], refs[mps:]
    rows, model = resid_ref.shape
    step = pl.program_id(0)

    @pl.when(step == 0)
    def _():
        forward[...] = jnp.zeros_like(forward)
        backward[...] = jnp.zeros_like(backward)

    expand = weights_ref[:, :model]
    reduce = weights_ref[:, model : 2 * model]
    tail = weights_ref[:, weights_ref.shape[1] - 128 :]
    lane = lax.broadcasted_iota(jnp.int32, (rows, 128), 1)
    bias_lane = 2 * model + width - (weights_ref.shape[1] - 128)
    ones = jnp.where(jnp.logical_or(lane == bias_lane, lane == bias_lane + 1), 1.0, 0.0).astype(BF)
    value = product(normed_ref[...], expand, 1, 1) + product(ones, tail, 1, 1)
    active, slope = gelu_parts(value)
    forward[...] += product(active.astype(BF), reduce)
    grad_mlp = cotangent_ref[...].astype(BF)
    grad = (product(grad_mlp, reduce, 1, 1) * slope).astype(BF)
    backward[...] += product(grad, expand)

    @pl.when(step == pl.num_programs(0) - 1)
    def _():
        resid = resid_ref[...]
        shown_ref[:, model:] = (resid + forward[...] + vectors_ref[1:2, :]).astype(BF)
        xhat, inverse = norm_parts(resid)
        grad = backward[...]
        grad_resid = cotangent_ref[...] + norm_pull(grad, vectors_ref[2:3, :], xhat, inverse)
        grad_ref[...] = grad_resid
        attn = grad_resid.astype(BF)
        shown_ref[:, :model] = attn
        sums_ref[...] = jnp.concatenate(
            [
                jnp.sum(grad * xhat, axis=0, keepdims=True),
                jnp.sum(grad, axis=0, keepdims=True),
                jnp.sum(attn.astype(F32), axis=0, keepdims=True),
                jnp.zeros((5, model), F32),
            ],
            axis=0,
        )
        for j in range(mps):
            part = across_of(across_ref, j, mps, width)
            grad_heads_refs[j][...] = product(attn, part).astype(BF)


def middle(weights, resid, normed, cotangent, vectors, mps, width):
    rows, model = resid.shape
    wide = weights.shape[1] % 256 + 256 if weights.shape[1] % 256 else 256
    chunk = 1024
    vmem = pl.BlockSpec(memory_space=pltpu.VMEM)
    return pl.pallas_call(
        functools.partial(middle_kernel, mps, width),
        grid=(weights.shape[0] // chunk,),
        in_specs=[
            pl.BlockSpec((chunk, weights.shape[1]), lambda i: (i, 0)),
            pl.BlockSpec((weights.shape[0], wide), lambda i: (0, weights.shape[1] // wide - 1)),
        ]
        + [vmem] * 4,
        out_specs=[vmem] * (3 + mps),
        out_shape=[
            jax.ShapeDtypeStruct((rows, 2 * model), BF),
            jax.ShapeDtypeStruct((rows, model), F32),
            jax.ShapeDtypeStruct((8, model), F32),
        ]
        + [jax.ShapeDtypeStruct((rows, width), BF)] * mps,
        scratch_shapes=[pltpu.VMEM((rows, model), F32)] * 2,
        compiler_params=pltpu.CompilerParams(vmem_limit_bytes=VMEM_LIMIT),
        cost_estimate=SMALL,
        name="middle",
    )(weights, weights, resid, normed, cotangent, vectors)


def feed_kernel(chunk, places_ref, expand_ref, reduce_ref, bias_ref, grad_ref, *refs):
    normed_refs, refs = refs[:-7], refs[-7:]
    mine_out, other_out, bias_out, normed, normed_turned, held, second_held = refs
    rows = normed_refs[0].shape[0]
    for j, ref in enumerate(normed_refs):
        normed[j * rows : (j + 1) * rows, :] = ref[...]
    normed_turned[...] = normed[...].T
    hidden = expand_ref.shape[1]
    for start in range(0, hidden, chunk):
        here = slice(start, start + chunk)
        value = product(normed[...], expand_ref[:, here]) + bias_ref[:, here]
        active, slope = gelu_parts(value)
        grad = product(grad_ref[...], reduce_ref[here, :], 1, 1) * slope
        low = grad.astype(BF)
        second_held[here, :] = product(active.astype(BF), grad_ref[...], 0, 0)
        held[:, here] = product(normed_turned[...], low)
        bias_out[:, here] = jnp.sum(low.astype(F32), axis=0, keepdims=True)
    core_rows(held, places_ref[1], mine_out, other_out)
    core_rows(second_held, places_ref[1], mine_out, other_out, held.shape[0] // 2)


def feed(places, expand, reduce, bias, grad, normed_blocks):
    model, hidden = expand.shape
    rows = grad.shape[0]
    vmem = pl.BlockSpec(memory_space=pltpu.VMEM)
    half = (model + hidden) // 2
    return pl.pallas_call(
        functools.partial(feed_kernel, 256),
        in_specs=[pl.BlockSpec(memory_space=pltpu.SMEM)] + [vmem] * (4 + len(normed_blocks)),
        out_shape=[
            jax.ShapeDtypeStruct((half, model), BF),
            jax.ShapeDtypeStruct((half, model), BF),
            jax.ShapeDtypeStruct((1, hidden), F32),
        ],
        scratch_shapes=[
            pltpu.VMEM((rows, model), BF),
            pltpu.VMEM((model, rows), BF),
            pltpu.VMEM((model, hidden), F32),
            pltpu.VMEM((hidden, model), F32),
        ],
        compiler_params=pltpu.CompilerParams(vmem_limit_bytes=VMEM_LIMIT),
        cost_estimate=SMALL,
        name="feed",
    )(places, expand, reduce, bias, grad, *normed_blocks)


def project_kernel(places_ref, packed_ref, normed_ref, attended_ref, attn_ref, *refs):
    mine_out, other_out, held = refs
    wide = packed_ref.shape[1]
    held[:wide, :] = product(packed_ref[...], normed_ref[...], 0, 0)
    held[wide:, :] = product(attended_ref[...], attn_ref[...], 0, 0)
    core_rows(held, places_ref[1], mine_out, other_out)


def project_weights(places, packed, normed, attended, shown):
    frames, wide = packed.shape
    width, model = attended.shape[1], normed.shape[1]
    vmem = pl.BlockSpec(memory_space=pltpu.VMEM)
    half = (wide + width) // 2
    return pl.pallas_call(
        project_kernel,
        grid=(1,),
        in_specs=[pl.BlockSpec(memory_space=pltpu.SMEM)]
        + [vmem] * 3
        + [pl.BlockSpec((frames, model), lambda i: (0, 0))],
        out_specs=[vmem, vmem],
        out_shape=[jax.ShapeDtypeStruct((half, model), BF)] * 2,
        scratch_shapes=[pltpu.VMEM((wide + width, model), F32)],
        compiler_params=pltpu.CompilerParams(vmem_limit_bytes=VMEM_LIMIT),
        cost_estimate=SMALL,
        name="project_weights",
    )(places, packed, normed, attended, shown)


def pieces_kernel(places_ref, feed_ref, feed_got_ref, project_ref, project_got_ref, *outs):
    part = project_ref.shape[0] // 4
    pairs = (
        (feed_ref, feed_got_ref, 0),
        (feed_ref, feed_got_ref, 4 * part),
        (project_ref, project_got_ref, 0),
    )
    for d, out in enumerate(outs):
        for which, (mine, got, start) in enumerate(pairs):
            place = start + jnp.bitwise_xor(places_ref[3], d) * part
            here = pl.ds(pl.multiple_of(place, part), part)
            value = mine[here, :].astype(F32) + got[here, :].astype(F32)
            out[which * part : (which + 1) * part, :] = value.astype(out.dtype)


def pieces(places, feed_mine, feed_got, project_mine, project_got):
    vmem = pl.BlockSpec(memory_space=pltpu.VMEM)
    model = feed_mine.shape[1]
    part = 3 * project_mine.shape[0] // 4
    return pl.pallas_call(
        pieces_kernel,
        in_specs=[pl.BlockSpec(memory_space=pltpu.SMEM)] + [vmem] * 4,
        out_shape=[jax.ShapeDtypeStruct((part, model), F32)]
        + [jax.ShapeDtypeStruct((part, model), BF)] * 3,
        compiler_params=pltpu.CompilerParams(vmem_limit_bytes=VMEM_LIMIT),
        cost_estimate=SMALL,
        name="pieces",
    )(places, feed_mine, feed_got, project_mine, project_got)


def pack_kernel(place_ref, query_ref, pair_ref, core_ref, other_ref, weight_ref, *outs):
    packed_out, sums_out, own_out, *others_out = outs
    pair = pair_ref[...].astype(F32) + core_ref[0].astype(F32) + other_ref[...].astype(F32)
    packed = jnp.concatenate([query_ref[...], pair.astype(BF)], axis=1)
    packed_out[...] = packed
    sums_out[...] = jnp.sum(packed.astype(F32), axis=0, keepdims=True)
    rows = own_out.shape[0]
    mps = len(others_out) + 1

    def part(j):
        start = pl.multiple_of(lax.rem(place_ref[0] + j, mps) * rows, rows)
        return product(packed_out[pl.ds(start, rows), :], weight_ref[...])

    own_out[...] = part(0)
    for j in range(1, mps):
        others_out[j - 1][...] = part(j).astype(BF)


def pack(place, query, pair, pair_core, pair_far, weight, mps):
    frames, width = query.shape
    model, rows = weight.shape[1], frames // mps
    vmem = pl.BlockSpec(memory_space=pltpu.VMEM)
    return pl.pallas_call(
        pack_kernel,
        grid=(1,),
        in_specs=[
            pl.BlockSpec(memory_space=pltpu.SMEM),
            vmem,
            vmem,
            pl.BlockSpec((1, frames, 2 * width), lambda i: (0, 0, 0)),
            vmem,
            vmem,
        ],
        out_specs=[vmem] * (2 + mps),
        out_shape=[
            jax.ShapeDtypeStruct((frames, 3 * width), BF),
            jax.ShapeDtypeStruct((1, 3 * width), F32),
            jax.ShapeDtypeStruct((rows, model), F32),
        ]
        + [jax.ShapeDtypeStruct((rows, model), BF)] * (mps - 1),
        compiler_params=pltpu.CompilerParams(vmem_limit_bytes=VMEM_LIMIT),
        cost_estimate=SMALL,
        name="pack",
    )(place, query, pair, pair_core, pair_far, weight)


def pull_kernel(resid_ref, grad_ref, stem_ref, gain_ref, sums_ref, *refs):
    got_refs, out_ref = refs[:-1], refs[-1]
    rows, model = resid_ref.shape
    grad = got_refs[0][...].astype(F32)
    for ref in got_refs[1:]:
        grad = grad + ref[...].astype(F32)
    xhat, inverse = norm_parts(resid_ref[...])
    grad_resid = grad_ref[...] + norm_pull(grad, gain_ref[...], xhat, inverse)
    _, slope = gelu_parts(stem_ref[...])
    low = (grad_resid * slope).astype(BF)
    out_ref[:rows, :] = low
    sums = jnp.concatenate(
        [
            jnp.sum(grad * xhat, axis=0, keepdims=True),
            jnp.sum(grad, axis=0, keepdims=True),
            sums_ref[0:3, :],
            jnp.sum(low.astype(F32), axis=0, keepdims=True),
            jnp.zeros((10, model), F32),
        ],
        axis=0,
    )
    out_ref[rows:, :] = sums.astype(BF)


def pull(resid, grad, stem, gain, sums, got):
    rows, model = resid.shape
    return pl.pallas_call(
        pull_kernel,
        out_shape=jax.ShapeDtypeStruct((rows + 16, model), BF),
        compiler_params=pltpu.CompilerParams(vmem_limit_bytes=VMEM_LIMIT),
        cost_estimate=SMALL,
        name="pull",
    )(resid, grad, stem, gain, sums, *got)


def second_kernel_body(mps, places_ref, taps_ref, gathered_ref, *refs):
    grad_out, sums_out, mine_out, other_out, held = refs
    rows = gathered_ref.shape[0] // mps
    own = rows - 16
    sums = 0.0
    for j in range(mps):
        grad_out[j * own : (j + 1) * own, :] = gathered_ref[j * rows : j * rows + own, :]
        sums = sums + gathered_ref[j * rows + own : (j + 1) * rows, :].astype(F32)
    sums_out[...] = sums
    held[...] = product(taps_ref[...], grad_out[...], 0, 0)
    core_rows(held, places_ref[1], mine_out, other_out)


def second_weight(places, taps, gathered, mps):
    frames, tall = taps.shape
    model = gathered.shape[1]
    vmem = pl.BlockSpec(memory_space=pltpu.VMEM)
    return pl.pallas_call(
        functools.partial(second_kernel_body, mps),
        in_specs=[pl.BlockSpec(memory_space=pltpu.SMEM)] + [vmem] * 2,
        out_shape=[
            jax.ShapeDtypeStruct((frames, model), BF),
            jax.ShapeDtypeStruct((16, model), F32),
            jax.ShapeDtypeStruct((tall // 2, model), F32),
            jax.ShapeDtypeStruct((tall // 2, model), BF),
        ],
        scratch_shapes=[pltpu.VMEM((tall, model), F32)],
        compiler_params=pltpu.CompilerParams(vmem_limit_bytes=VMEM_LIMIT),
        cost_estimate=SMALL,
        name="second_weight",
    )(places, taps, gathered)


def stem_back_kernel(
    bands,
    places_ref,
    grad_ref,
    edges_ref,
    matrix_ref,
    even_ref,
    odd_ref,
    rim_ref,
    window_ref,
    back_ref,
    sums_ref,
    reduce_ref,
    expand_ref,
    project_ref,
    mine_out,
    other_out,
    spectrum_out,
    held,
    small,
):
    frames = grad_ref.shape[0]
    width = even_ref.shape[1]
    row = lax.broadcasted_iota(jnp.int32, (frames, width), 0)

    def later(value, last):
        return jnp.where(row == frames - 1, last, pltpu.roll(value, frames - 1, 0))

    def earlier(value, start):
        return jnp.where(row == 0, start, pltpu.roll(value, 1, 0))

    def slope(value):
        return gelu_parts(value)[1]

    def rounded(value):
        return value.astype(BF).astype(F32)

    taps = product(grad_ref[...], matrix_ref[...], 1, 1)
    rims = product(edges_ref[...], matrix_ref[...], 1, 1)
    even = rounded(taps[:, width : 2 * width] * slope(even_ref[...]))
    odd = taps[:, 2 * width :] + later(taps[:, :width], rims[1:2, :width])
    odd = rounded(odd * slope(odd_ref[...]))
    rim_slope = slope(rim_ref[...])
    inside = (places_ref[2] > 0).astype(F32)
    odd_before = rounded((rims[0:1, 2 * width :] + taps[0:1, :width]) * rim_slope[0:1] * inside)
    even_after = rounded(rims[1:2, width : 2 * width] * rim_slope[1:2])
    bias = jnp.sum(even + odd, axis=0, keepdims=True)
    both = jnp.concatenate([even, odd], axis=1).astype(BF)
    weight = product(window_ref[...], both, 0, 0)
    weight = weight[: 3 * bands, :width] + weight[bands:, width:]
    spare = held.shape[1] - 3 * width
    held[:bands, :] = jnp.concatenate(
        [weight[k * bands : (k + 1) * bands] for k in range(3)] + [jnp.zeros((bands, spare), F32)],
        axis=1,
    )
    last = jnp.concatenate(
        [project_ref[:, :width], project_ref[:, 2 * width :], bias, jnp.zeros((1, spare), F32)],
        axis=1,
    )
    blank = jnp.zeros((held.shape[0] - bands - 9, held.shape[1]), F32)
    held[bands:, :] = jnp.concatenate(
        [sums_ref[0:6, :], reduce_ref[...], expand_ref[...], last, blank], axis=0
    )
    few = small.shape[1]
    for p in range(8):
        small[p] = held[p * few : (p + 1) * few, :]
    filled = jnp.zeros((other_out.shape[1] - few, held.shape[1]), F32)
    for quarter in range(4):
        mine_out[quarter] = small[2 * quarter + places_ref[1]]
        other = small[2 * quarter + 1 - places_ref[1]]
        other_out[quarter] = jnp.concatenate([other, filled], axis=0).astype(BF)
    before = earlier(odd, odd_before).astype(BF)
    following = later(even, even_after).astype(BF)
    even, odd = even.astype(BF), odd.astype(BF)
    back = [back_ref[k * width : (k + 1) * width, :] for k in range(3)]
    spectrum = [
        product(before, back[0]) + product(even, back[1]) + product(odd, back[2]),
        product(even, back[0]) + product(odd, back[1]) + product(following, back[2]),
    ]
    spectrum_out[...] = jnp.concatenate(spectrum, axis=1).astype(BF)


def stem_back(places, grad, edges, matrix, even, odd, rim, window, back_matrix, *sums):
    frames, width = even.shape
    bands, model = back_matrix.shape[1], grad.shape[1]
    vmem = pl.BlockSpec(memory_space=pltpu.VMEM)
    return pl.pallas_call(
        functools.partial(stem_back_kernel, bands),
        in_specs=[pl.BlockSpec(memory_space=pltpu.SMEM)] + [vmem] * (8 + len(sums)),
        out_shape=[
            jax.ShapeDtypeStruct((4, (bands + 16) // 8, model), F32),
            jax.ShapeDtypeStruct((4, 16, model), BF),
            jax.ShapeDtypeStruct((frames, 2 * bands), BF),
        ],
        scratch_shapes=[
            pltpu.VMEM((bands + 16, model), F32),
            pltpu.VMEM((8, (bands + 16) // 8, model), F32),
        ],
        compiler_params=pltpu.CompilerParams(vmem_limit_bytes=VMEM_LIMIT),
        cost_estimate=SMALL,
        name="stem_back",
    )(places, grad, edges, matrix, even, odd, rim, window, back_matrix, *sums)


def on_device(
    spectrogram,
    first_kernel,
    first_bias,
    second_kernel,
    second_bias,
    attend_gain,
    attend_shift,
    project_weight,
    project_bias,
    output_weight,
    output_bias,
    mixer_gain,
    mixer_shift,
    expand_weight,
    expand_bias,
    reduce_weight,
    reduce_bias,
    cotangent,
):
    _, steps, bands = spectrogram.shape
    frames = steps // 2
    width = first_kernel.shape[2]
    model = second_kernel.shape[2]
    hidden = expand_weight.shape[1]
    mps, seqs = lax.axis_size("mp"), lax.axis_size("seq")
    z, seq = lax.axis_index("mp"), lax.axis_index("seq")
    core = lax.rem(seq, 2)
    rows = frames // mps

    held = hold(
        (2 * plane_index() + core).reshape(1),
        expand_weight,
        reduce_weight,
        output_weight,
        expand_bias,
        hidden // 8,
    )
    weights_got = gather_mp(held, "weights_mp")

    paired = spectrogram.reshape(frames, 2 * bands)
    before = passed_along(paired[-1:], 1)
    following = passed_along(paired[:1], -1)
    ahead = jnp.concatenate([before, paired, following], axis=0)
    window = jnp.concatenate(
        [ahead[:-2, bands:], ahead[1:-1], ahead[2:, :bands]], axis=1
    )
    prior = jnp.concatenate([before, paired[:1, :bands]], axis=1)
    latter = jnp.concatenate([paired[-1:, bands:], following], axis=1)
    first_matrix = first_kernel.reshape(3 * bands, width)
    even_in = jnp.concatenate([window[:, : 3 * bands], latter], axis=0)
    odd_in = jnp.concatenate([prior, window[:, bands:]], axis=0)
    pre_even = product(even_in, first_matrix) + first_bias
    pre_odd = product(odd_in, first_matrix) + first_bias
    inside = jnp.logical_or(jnp.arange(frames + 1) > 0, seq > 0)[:, None]
    hidden_even = exact_gelu(pre_even[:frames]).astype(BF)
    hidden_odd = jnp.where(inside, exact_gelu(pre_odd), 0.0).astype(BF)
    taps = jnp.concatenate([hidden_odd[:frames], hidden_even, hidden_odd[1:]], axis=1)
    second_matrix = second_kernel.reshape(3 * width, model)
    stem_part = product(taps, second_matrix)
    own_cotangent = rolled_blocks(cotangent.reshape(frames, model))
    early = (
        own_cotangent[0],
        jnp.concatenate(own_cotangent, axis=0).astype(BF),
        jnp.stack([output_bias, reduce_bias, mixer_gain, mixer_shift]),
        column_total(cotangent.reshape(frames, model).astype(BF))[None],
        jnp.transpose(first_kernel[::-1], (0, 2, 1)).reshape(3 * width, bands),
        jnp.concatenate([pre_odd[:1], pre_even[frames:], jnp.zeros((6, width), F32)], axis=0),
        pre_even[:frames],
        pre_odd[1:],
        window,
        taps,
        sinusoid(seq * frames + z * rows, rows, model),
        jnp.stack([z, core, seq, plane_index()]),
        z.reshape(1),
        attend_gain.reshape(1, model),
        expand_bias.reshape(1, hidden),
    )
    stem_part, weights_got, early = lax.optimization_barrier((stem_part, weights_got, early))
    own_cotangent, grad_mlp, vectors, reduce_bias_part, back_matrix = early[:5]
    rim, even_level, odd_level, window, taps, table = early[5:11]
    places, place, attend_gain_row, expand_bias_row = early[11:]
    with jax.named_scope("weights_plane"):
        weights_all = plane_gather(jnp.concatenate(weights_got, axis=0))
    stem_pre = scatter_sum(rolled_blocks(stem_part), "stem_sum") + second_bias
    resid_zero = exact_gelu(stem_pre) + table
    normed_one = lax.all_gather(
        layer_norm(resid_zero, attend_gain, attend_shift).astype(BF), "mp", axis=0, tiled=True
    )

    project_matrix = project_weight.transpose(1, 2, 0).reshape(3 * width, model)
    offsets = jnp.concatenate([project_bias[0], jnp.zeros_like(project_bias[0]), project_bias[1]])
    packed = (product(normed_one, project_matrix, 1, 1) + offsets).astype(BF)
    query, pair = packed[:, :width], packed[:, width:]
    pair_far = swapped(pair, "seq", 2, "pair_far")
    pair_core = swapped(pair, "seq", 1, "pair_core")
    pair_far, query = lax.optimization_barrier((pair_far, query))
    pair_far_core = swapped(pair_far, "seq", 1, "pair_far_core")
    pairs = [pair, pair_core, pair_far, pair_far_core]
    attended, attended_turned, level, *attended_blocks = attend(place, query, pairs, mps)
    heads_got = exchange_mp(attended_blocks, "attended")
    resid_one, normed_two_own = join(weights_all, heads_got, resid_zero, vectors)
    normed_two_all = gather_mp(normed_two_own, "normed_two")
    shown_own, grad_resid_one, middle_sums, *grad_heads = middle(
        weights_all,
        resid_one,
        normed_two_own,
        own_cotangent,
        vectors,
        mps,
        width,
    )
    shown = lax.all_gather(shown_own, "mp", axis=0, tiled=True)
    rows_got = exchange_mp(grad_heads, "grad_heads")
    grad_attended = natural([rows_got[-j % mps] for j in range(mps)])
    grad_attended, normed_two_all = lax.optimization_barrier((grad_attended, normed_two_all))

    query_grad, near, far, cores = attend_back(
        place,
        query,
        attended_turned,
        level,
        pairs,
        [grad_attended],
    )
    cores_got = swapped(cores, "seq", 1, "grad_core")
    far = (far.astype(F32) + cores_got[1].astype(F32)).astype(BF)
    far_got = swapped(far, "seq", 2, "grad_far")
    feed_mine, feed_other, expand_bias_part = feed(
        places,
        expand_weight,
        reduce_weight,
        expand_bias_row,
        after(grad_mlp, far),
        normed_two_all,
    )
    far_got, feed_other = lax.optimization_barrier((far_got, feed_other))
    feed_got = swapped(feed_other, "seq", 1, "feed_core")
    grad_packed, project_columns, *normed_parts = pack(
        place, query_grad, near, cores_got, far_got, project_matrix, mps
    )
    normed_got = exchange_mp(normed_parts, "grad_normed_one")

    project_mine, project_other = project_weights(places, grad_packed, normed_one, attended, shown)
    project_got = swapped(project_other, "seq", 1, "project_core")
    wide_pieces = pieces(places, feed_mine, feed_got, project_mine, project_got)
    normed_got, wide_pieces = lax.optimization_barrier((normed_got, wide_pieces))
    wide_parts = [
        plane_move(piece, d, "wide_scatter") for d, piece in zip((1, 2, 3), wide_pieces[1:])
    ]

    grad_stem_own = pull(
        resid_zero, grad_resid_one, stem_pre, attend_gain_row, middle_sums, normed_got
    )
    with jax.named_scope("grad_stem"):
        gathered = lax.all_gather(grad_stem_own, "mp", axis=0, tiled=True)
    gathered, wide_parts = lax.optimization_barrier((gathered, wide_parts))
    with jax.named_scope("wide_gather"):
        wide_all = plane_gather(rest_of_dp(total([wide_pieces[0]] + wide_parts).astype(BF)))
    last_row = (mps - 1) * (rows + 16) + rows - 1
    stem_before = passed_along(gathered[last_row : last_row + 1], 1)
    stem_following = passed_along(gathered[:1], -1)
    grad_stem, small, second_mine, second_other = second_weight(places, taps, gathered, mps)
    second_got = swapped(second_other, "seq", 1, "second_core")
    edges = jnp.concatenate([stem_before, stem_following, jnp.zeros((14, model), BF)], axis=0)
    loose_mine, loose_other, spectrum_part = stem_back(
        places,
        grad_stem,
        edges,
        second_matrix,
        even_level,
        odd_level,
        rim,
        window,
        back_matrix,
        small,
        reduce_bias_part,
        expand_bias_part,
        project_columns,
    )
    loose_got = swapped(loose_other, "seq", 1, "small_core")[:, : (bands + 16) // 8]

    joined = jnp.concatenate(
        [
            (second_mine + second_got.astype(F32)).reshape(4, -1, model),
            loose_mine + loose_got.astype(F32),
        ],
        axis=1,
    )
    spectrum_parts = gather_mp(spectrum_part, "spectrum")
    joined, shown = lax.optimization_barrier((joined, shown))
    piece = plane_scatter(joined, "last_scatter")
    encoded = shown[:, model:].astype(F32)
    piece, encoded = lax.optimization_barrier((piece, encoded))
    with jax.named_scope("last_gather"):
        last = plane_gather(piece[None])
    last, spectrum_parts, wide_all = lax.optimization_barrier((last, spectrum_parts, wide_all))
    rows_of = (model, model, model, model, model, model, model, hidden)
    cuts = tuple((row, 0, size) for row, size in enumerate(rows_of))
    cuts += ((8, 0, 2 * width), (8, 2 * width, 3 * width))
    expand_sum, reduce_sum, project_sum, output_sum, spectrum, second_sum, first_sum, *sums = end(
        place, wide_all, last, spectrum_parts, bands, bands + 16, width, cuts
    )
    spectrogram_gradient = spectrum.reshape(1, steps, bands)
    return (
        encoded.reshape(1, frames, model),
        spectrogram_gradient,
        first_sum.reshape(3, bands, width),
        sums[9],
        second_sum.reshape(3, width, model),
        sums[5],
        sums[0],
        sums[1],
        project_sum.T.reshape(model, 3, width),
        sums[8],
        output_sum,
        sums[4],
        sums[2],
        sums[3],
        expand_sum,
        sums[7],
        reduce_sum,
        sums[6],
    )


def solution(mesh):
    return jax.shard_map(
        on_device,
        mesh=mesh,
        in_specs=(
            P("dp", "seq", None),
            P(None, None, "mp"),
            P("mp"),
            P(None, "mp", None),
            P(),
            P(),
            P(),
            P(None, None, "mp"),
            P(None, "mp"),
            P("mp", None),
            P(),
            P(),
            P(),
            P(None, "mp"),
            P("mp"),
            P("mp", None),
            P(),
            P("dp", "seq", None),
        ),
        out_specs=(
            P("dp", "seq", None),
            P("dp", "seq", None),
            P(None, None, "mp"),
            P("mp"),
            P(None, "mp", None),
            P(),
            P(),
            P(),
            P(None, None, "mp"),
            P(None, "mp"),
            P("mp", None),
            P(),
            P(),
            P(),
            P(None, "mp"),
            P("mp"),
            P("mp", None),
            P(),
        ),
        check_vma=False,
    )
```

```python
import functools
import math

import jax
import jax.numpy as jnp
from jax import lax
from jax.experimental import pallas as pl
from jax.experimental.pallas import tpu as pltpu
from jax.sharding import PartitionSpec as P

HEAD_DIM = 64
BF = jnp.bfloat16
F32 = jnp.float32
VMEM_LIMIT = 60 * 1024 * 1024
SMALL = pl.CostEstimate(flops=1, bytes_accessed=1, transcendentals=0)


def product(left, right, left_dim=1, right_dim=0):
    dims = (((left_dim,), (right_dim,)), ((), ()))
    return lax.dot_general(left, right, dims, preferred_element_type=F32)


def after(value, *others):
    return lax.optimization_barrier((value, *others))[0]


def exact_gelu(value):
    return jax.nn.gelu(value, approximate=False)


def gelu_back(value, grad):
    return jax.vjp(exact_gelu, value)[1](grad)[0]


def layer_norm(value, gain, shift):
    centre = value - jnp.mean(value, axis=-1, keepdims=True)
    spread = jnp.mean(centre * centre, axis=-1, keepdims=True)
    return centre * lax.rsqrt(spread + 1e-05) * gain + shift


def norm_back(value, gain, grad):
    centre = value - jnp.mean(value, axis=-1, keepdims=True)
    spread = jnp.mean(centre * centre, axis=-1, keepdims=True)
    inverse = lax.rsqrt(spread + 1e-05)
    xhat = centre * inverse
    e = grad * gain
    back = (
        e - jnp.mean(e, axis=-1, keepdims=True) - xhat * jnp.mean(e * xhat, axis=-1, keepdims=True)
    ) * inverse
    return back, jnp.sum(grad * xhat, axis=0), jnp.sum(grad, axis=0)


def column_total(value):
    return jnp.sum(value.astype(F32), axis=0)


def sinusoid(start, count, width):
    half = width // 2
    rates = jnp.exp(jnp.arange(half, dtype=F32) * (-math.log(10000.0) / (half - 1)))
    times = (start + jnp.arange(count)).astype(F32)
    angles = times[:, None] * rates[None, :]
    return jnp.concatenate([jnp.sin(angles), jnp.cos(angles)], axis=1)


def turned(size, by):
    return [(i, (i + by) % size) for i in range(size)]


def gather_mp(block, name):
    size = lax.axis_size("mp")
    with jax.named_scope(name):
        return [block] + [lax.ppermute(block, "mp", turned(size, -j)) for j in range(1, size)]


def exchange_mp(blocks, name):
    size = lax.axis_size("mp")
    with jax.named_scope(name):
        got = [lax.ppermute(blocks[j], "mp", turned(size, j)) for j in range(1, size)]
    return [blocks[0]] + got


def row_blocks(value, count):
    rows = value.shape[0] // count
    return [value[j * rows : (j + 1) * rows] for j in range(count)]


def rolled_blocks(value):
    size, z = lax.axis_size("mp"), lax.axis_index("mp")
    rows = value.shape[0] // size
    return [
        lax.dynamic_slice_in_dim(value, lax.rem(z + j, size) * rows, rows, axis=0)
        for j in range(size)
    ]


def natural(blocks):
    size, z = lax.axis_size("mp"), lax.axis_index("mp")
    rows = blocks[0].shape[0]
    twice = jnp.concatenate(blocks + blocks, axis=0)
    return lax.dynamic_slice_in_dim(twice, lax.rem(size - z, size) * rows, rows * size, axis=0)


def total(parts):
    result = parts[0].astype(F32)
    for part in parts[1:]:
        result = result + part.astype(F32)
    return result


def scatter_sum(blocks, name):
    return total(exchange_mp([blocks[0]] + [block.astype(BF) for block in blocks[1:]], name))


def swapped(value, axis, bit, name):
    size = lax.axis_size(axis)
    with jax.named_scope(name):
        return lax.ppermute(value, axis, [(i, i ^ bit) for i in range(size)])


def passed_along(value, by):
    size = lax.axis_size("seq")
    pairs = [(i, i + by) for i in range(size) if 0 <= i + by < size]
    return lax.ppermute(value, "seq", pairs)


def plane_index():
    return lax.rem(lax.axis_index("dp"), 2) * 2 + lax.div(lax.axis_index("seq"), 2)


def plane_move(value, d, name):
    dps, seqs = lax.axis_size("dp"), lax.axis_size("seq")
    pairs = [
        (p * seqs + s, (p ^ (d >> 1)) * seqs + (s ^ (2 * (d & 1))))
        for p in range(dps)
        for s in range(seqs)
    ]
    with jax.named_scope(name):
        return lax.ppermute(value, ("dp", "seq"), pairs)


def rest_of_dp(value):
    dps = lax.axis_size("dp")
    if dps > 2:
        groups = [[i for i in range(dps) if i % 2 == bit] for bit in range(2)]
        value = lax.psum(value, "dp", axis_index_groups=groups)
    return value


def plane_scatter(quarters, name):
    index = plane_index()

    def piece(d):
        return lax.dynamic_index_in_dim(quarters, jnp.bitwise_xor(index, d), 0, keepdims=False)

    got = [plane_move(piece(d).astype(BF), d, name) for d in (1, 2, 3)]
    return rest_of_dp(total([piece(0)] + got).astype(BF))


def plane_gather(piece):
    dps = lax.axis_size("dp")
    if dps == 2:
        return lax.all_gather(piece, ("dp", "seq"), axis=0, tiled=True)
    pairs = [[i, i + 1] for i in range(0, dps, 2)]
    return lax.all_gather(
        lax.all_gather(piece, "seq", axis=0, tiled=True),
        "dp",
        axis=0,
        tiled=True,
        axis_index_groups=pairs,
    )


def core_rows(held, core, mine_out, other_out, start=0):
    rows = held.shape[0] // 8
    mine, others = [], []
    for quarter in range(4):
        here = pl.ds(pl.multiple_of((2 * quarter + core) * rows, rows), rows)
        there = pl.ds(pl.multiple_of((2 * quarter + 1 - core) * rows, rows), rows)
        mine.append(held[here, :])
        others.append(held[there, :])
    place = slice(start, start + 4 * rows)
    mine_out[place, :] = jnp.concatenate(mine, axis=0).astype(mine_out.dtype)
    other_out[place, :] = jnp.concatenate(others, axis=0).astype(BF)


def finish_wide_kernel(wide_ref, expand_out, reduce_out, project_out, output_out):
    part = expand_out.shape[0] // 8
    split = project_out.shape[0] // part
    for p in range(8):
        here = slice(p * part, (p + 1) * part)
        block = wide_ref[3 * p * part : 3 * (p + 1) * part, :].astype(F32)
        expand_out[here, :] = block[:part]
        reduce_out[here, :] = block[part : 2 * part]
        if p < split:
            project_out[here, :] = block[2 * part :]
        else:
            output_out[(p - split) * part : (p - split + 1) * part, :] = block[2 * part :]


def finish_kernel(bands, loose, vectors, gathered_ref, second_out, first_out, *refs):
    outs, (whole, small) = refs[:-2], refs[-2:]
    eighth = gathered_ref.shape[1]
    rows, few = eighth - loose // 8, loose // 8
    for p in range(8):
        whole[...] = gathered_ref[p].astype(F32)
        second_out[p * rows : (p + 1) * rows, :] = whole[:rows, :]
        small[p * few : (p + 1) * few, :] = whole[rows:, :]
    width = first_out.shape[1]
    for tap in range(3):
        first_out[tap * bands : (tap + 1) * bands, :] = small[
            :bands, tap * width : (tap + 1) * width
        ]
    for out, (row, start, stop) in zip(outs, vectors):
        if out.ndim == 1:
            out[...] = small[bands + row, start:stop]
        else:
            for k in range(out.shape[0]):
                place = start + k * width
                out[k : k + 1, :] = small[bands + row : bands + row + 1, place : place + width]


def spectrum_kernel(place_ref, *refs):
    parts, (out_ref, held) = refs[:-2], refs[-2:]
    for j, part in enumerate(parts):
        held[lax.rem(place_ref[0] + j, len(parts))] = part[...].astype(F32)
    result = held[0]
    for j in range(1, len(parts)):
        result = result + held[j]
    out_ref[...] = result


def end_kernel(bands, loose, vectors, mps, place_ref, wide_ref, gathered_ref, *refs):
    parts, refs = refs[:mps], refs[mps:]
    wide_outs, spectrum_out, refs = refs[:4], refs[4], refs[5:]
    outs, (whole, small, held) = refs[:-3], refs[-3:]
    finish_wide_kernel(wide_ref, *wide_outs)
    spectrum_kernel(place_ref, *parts, spectrum_out, held)
    finish_kernel(bands, loose, vectors, gathered_ref, *outs, whole, small)


def end(place, wide, gathered, parts, bands, loose, width, vectors):
    _, rows, model = gathered.shape
    vmem = pl.BlockSpec(memory_space=pltpu.VMEM)
    return pl.pallas_call(
        functools.partial(end_kernel, bands, loose, vectors, len(parts)),
        in_specs=[pl.BlockSpec(memory_space=pltpu.SMEM)] + [vmem] * (2 + len(parts)),
        out_shape=[
            jax.ShapeDtypeStruct((high, model), F32) for high in (model, model, 3 * width, width)
        ]
        + [
            jax.ShapeDtypeStruct(parts[0].shape, F32),
            jax.ShapeDtypeStruct((8 * rows - loose, model), F32),
            jax.ShapeDtypeStruct((3 * bands, width), F32),
        ]
        + [
            jax.ShapeDtypeStruct(
                (2, width) if stop - start == 2 * width else (stop - start,), F32
            )
            for _, start, stop in vectors
        ],
        scratch_shapes=[
            pltpu.VMEM((rows, model), F32),
            pltpu.VMEM((loose, model), F32),
            pltpu.VMEM((len(parts), *parts[0].shape), F32),
        ],
        compiler_params=pltpu.CompilerParams(vmem_limit_bytes=VMEM_LIMIT),
        cost_estimate=SMALL,
        name="end",
    )(place, wide, gathered, *parts)


def attend_kernel(heads, scale, place_ref, query_ref, *refs):
    pair_refs, (out_ref, turned_ref, level_ref), refs = refs[:4], refs[4:7], refs[7:]
    block_refs, held = refs[:-1], refs[-1]
    width = heads * HEAD_DIM
    count = pair_refs[0].shape[0]
    outs, levels = [], []
    for head in range(heads):
        cols = slice(head * HEAD_DIM, (head + 1) * HEAD_DIM)
        query = query_ref[:, cols] * jnp.asarray(scale, BF)
        top = None
        for index, pair in enumerate(pair_refs):
            scores = product(pair[:, cols], query, 1, 1)
            held[index * count : (index + 1) * count, :] = scores
            high = jnp.max(scores, axis=0, keepdims=True)
            top = high if top is None else jnp.maximum(top, high)
        weight, out = 0.0, 0.0
        vcols = slice(width + head * HEAD_DIM, width + (head + 1) * HEAD_DIM)
        for index, pair in enumerate(pair_refs):
            soft = jnp.exp(held[index * count : (index + 1) * count, :] - top)
            weight = weight + jnp.sum(soft, axis=0, keepdims=True)
            out = out + product(pair[:, vcols], soft.astype(BF), 0, 0)
        outs.append(out / weight)
        levels.append(top + jnp.log(weight))
    joined = jnp.concatenate(outs, axis=0)
    turned_ref[...] = joined
    out_ref[...] = joined.T.astype(BF)
    level_ref[...] = jnp.concatenate(levels, axis=0)
    rows = block_refs[0].shape[0]
    for j, block in enumerate(block_refs):
        start = pl.multiple_of(lax.rem(place_ref[0] + j, len(block_refs)) * rows, rows)
        block[...] = out_ref[pl.ds(start, rows), :]


def attend(place, query, pairs, mps):
    rows, width = query.shape
    heads = width // HEAD_DIM
    vmem = pl.BlockSpec(memory_space=pltpu.VMEM)
    return pl.pallas_call(
        functools.partial(attend_kernel, heads, HEAD_DIM ** (-0.5)),
        in_specs=[pl.BlockSpec(memory_space=pltpu.SMEM)] + [vmem] * 5,
        out_shape=[
            jax.ShapeDtypeStruct((rows, width), BF),
            jax.ShapeDtypeStruct((width, rows), F32),
            jax.ShapeDtypeStruct((heads, rows), F32),
        ]
        + [jax.ShapeDtypeStruct((rows // mps, width), BF)] * mps,
        scratch_shapes=[pltpu.VMEM((rows * len(pairs), rows), F32)],
        compiler_params=pltpu.CompilerParams(vmem_limit_bytes=VMEM_LIMIT),
        cost_estimate=SMALL,
        name="attend",
    )(place, query, *pairs)


def attend_back_kernel(heads, scale, place_ref, query_ref, turned_ref, level_ref, *refs):
    pair_refs, refs = refs[:4], refs[4:]
    block_refs, (query_out, near_out, far_out, core_out, grad_ref) = refs[:-5], refs[-5:]
    width = heads * HEAD_DIM
    rows = block_refs[0].shape[0]
    for j, block in enumerate(block_refs):
        start = pl.multiple_of(lax.rem(place_ref[0] + j, len(block_refs)) * rows, rows)
        grad_ref[pl.ds(start, rows), :] = block[...]
    grads_turned = grad_ref[...].astype(F32).T
    query_grads = []
    pair_grads = [([], []) for _ in range(4)]
    for head in range(heads):
        cols = slice(head * HEAD_DIM, (head + 1) * HEAD_DIM)
        vcols = slice(width + head * HEAD_DIM, width + (head + 1) * HEAD_DIM)
        query = query_ref[:, cols] * jnp.asarray(scale, BF)
        grad = grad_ref[:, cols]
        level = level_ref[head : head + 1, :]
        delta = jnp.sum(grads_turned[cols, :] * turned_ref[cols, :], axis=0, keepdims=True)
        query_grad = 0.0
        for index in range(4):
            pair = pair_refs[index]
            key = pair[:, cols]
            soft = jnp.exp(product(key, query, 1, 1) - level)
            grad_soft = product(pair[:, vcols], grad, 1, 1)
            low = (soft * (grad_soft - delta)).astype(BF)
            pair_grads[index][0].append(product(low, query))
            pair_grads[index][1].append(product(soft.astype(BF), grad))
            query_grad = query_grad + product(key, low, 0, 0)
        query_grads.append(query_grad * scale)
    query_out[...] = jnp.concatenate(query_grads, axis=0).T.astype(BF)
    near, near_core, far, far_core = [
        jnp.concatenate(keys + values, axis=1) for keys, values in pair_grads
    ]
    near_out[...] = near.astype(BF)
    far_out[...] = far.astype(BF)
    core_out[0] = near_core.astype(BF)
    core_out[1] = far_core.astype(BF)


def attend_back(place, query, turned_out, level, pairs, blocks):
    rows, width = query.shape
    heads = width // HEAD_DIM
    vmem = pl.BlockSpec(memory_space=pltpu.VMEM)
    return pl.pallas_call(
        functools.partial(attend_back_kernel, heads, HEAD_DIM ** (-0.5)),
        in_specs=[pl.BlockSpec(memory_space=pltpu.SMEM)] + [vmem] * (7 + len(blocks)),
        out_shape=[
            jax.ShapeDtypeStruct((rows, width), BF),
            jax.ShapeDtypeStruct((rows, 2 * width), BF),
            jax.ShapeDtypeStruct((rows, 2 * width), BF),
            jax.ShapeDtypeStruct((2, rows, 2 * width), BF),
        ],
        scratch_shapes=[pltpu.VMEM((rows, width), BF)],
        compiler_params=pltpu.CompilerParams(vmem_limit_bytes=VMEM_LIMIT),
        cost_estimate=SMALL,
        name="attend_back",
    )(place, query, turned_out, level, *pairs, *blocks)


def gelu_parts(value):
    share = 0.5 + 0.5 * lax.erf(value * math.sqrt(0.5))
    slope = share + value * jnp.exp(-0.5 * value * value) * (1.0 / math.sqrt(2.0 * math.pi))
    return value * share, slope


def hold_kernel(which_ref, expand_ref, reduce_ref, output_ref, bias_ref, out_ref, *turned):
    rows, columns = out_ref.shape
    model, width = expand_ref.shape[0], output_ref.shape[0]
    expand, output, bias = turned
    expand[...] = expand_ref[...].T
    output[...] = output_ref[...].T
    whole = bias_ref[...].reshape(1, -1)
    high = whole.astype(BF).astype(F32)
    both = [high, whole - high, jnp.zeros((126, whole.shape[1]), F32)]
    bias[...] = jnp.concatenate(both, axis=0).T
    here = pl.ds(pl.multiple_of(which_ref[0] * rows, rows), rows)
    out_ref[:, :model] = expand[here, :]
    out_ref[:, model : 2 * model] = reduce_ref[...]
    tail = columns - 2 * model - width
    out_ref[:, 2 * model :] = jnp.concatenate(
        [output[here, :], bias[here, :tail].astype(BF)], axis=1
    )


def hold(which, expand, reduce, output, bias, rows):
    model, hidden = expand.shape
    width = output.shape[0]
    columns = -(-(2 * model + width + 2) // 128) * 128
    return pl.pallas_call(
        hold_kernel,
        grid_spec=pltpu.PrefetchScalarGridSpec(
            num_scalar_prefetch=1,
            grid=(1,),
            in_specs=[
                pl.BlockSpec((model, hidden), lambda i, which: (0, 0)),
                pl.BlockSpec((rows, model), lambda i, which: (which[0], 0)),
                pl.BlockSpec((width, model), lambda i, which: (0, 0)),
                pl.BlockSpec((hidden,), lambda i, which: (0,)),
            ],
            out_specs=pl.BlockSpec((rows, columns), lambda i, which: (0, 0)),
            scratch_shapes=[
                pltpu.VMEM((hidden, model), BF),
                pltpu.VMEM((model, width), BF),
                pltpu.VMEM((hidden, 128), F32),
            ],
        ),
        out_shape=jax.ShapeDtypeStruct((rows, columns), BF),
        compiler_params=pltpu.CompilerParams(vmem_limit_bytes=VMEM_LIMIT),
        cost_estimate=SMALL,
        name="hold",
    )(which, expand, reduce, output, bias)


def across_of(weights_ref, j, mps, width):
    rows = weights_ref.shape[0] // (8 * mps)
    places = [(p * mps + j % mps) * rows for p in range(8)]
    return jnp.concatenate([weights_ref[place : place + rows, :width] for place in places], axis=0)


def norm_parts(value):
    centre = value - jnp.mean(value, axis=-1, keepdims=True)
    inverse = lax.rsqrt(jnp.mean(centre * centre, axis=-1, keepdims=True) + 1e-05)
    return centre * inverse, inverse


def norm_pull(grad, gain, xhat, inverse):
    e = grad * gain
    shared = jnp.mean(e, axis=-1, keepdims=True) + xhat * jnp.mean(e * xhat, axis=-1, keepdims=True)
    return (e - shared) * inverse


def join_kernel(weights_ref, resid_ref, vectors_ref, *refs):
    heads_refs, (resid_out, normed_out) = refs[:-2], refs[-2:]
    mps, width = len(heads_refs), heads_refs[0].shape[1]
    resid = resid_ref[...] + vectors_ref[0:1, :]
    for j in range(mps):
        part = across_of(weights_ref, -j, mps, width)
        resid = resid + product(heads_refs[j][...], part, 1, 1)
    resid_out[...] = resid
    xhat, _ = norm_parts(resid)
    normed_out[...] = (xhat * vectors_ref[2:3, :] + vectors_ref[3:4, :]).astype(BF)


def join(weights, heads, resid, vectors):
    rows, model = resid.shape
    wide = weights.shape[1] % 256 + 256 if weights.shape[1] % 256 else 256
    vmem = pl.BlockSpec(memory_space=pltpu.VMEM)
    return pl.pallas_call(
        join_kernel,
        grid=(1,),
        in_specs=[
            pl.BlockSpec((weights.shape[0], wide), lambda i: (0, weights.shape[1] // wide - 1)),
        ]
        + [vmem] * (2 + len(heads)),
        out_specs=[vmem, vmem],
        out_shape=[
            jax.ShapeDtypeStruct((rows, model), F32),
            jax.ShapeDtypeStruct((rows, model), BF),
        ],
        compiler_params=pltpu.CompilerParams(vmem_limit_bytes=VMEM_LIMIT),
        cost_estimate=SMALL,
        name="join",
    )(weights, resid, vectors, *heads)


def middle_kernel(
    mps,
    width,
    weights_ref,
    across_ref,
    resid_ref,
    normed_ref,
    cotangent_ref,
    vectors_ref,
    shown_ref,
    grad_ref,
    sums_ref,
    *refs,
):
    grad_heads_refs, (forward, backward) = refs[:mps], refs[mps:]
    rows, model = resid_ref.shape
    step = pl.program_id(0)

    @pl.when(step == 0)
    def _():
        forward[...] = jnp.zeros_like(forward)
        backward[...] = jnp.zeros_like(backward)

    expand = weights_ref[:, :model]
    reduce = weights_ref[:, model : 2 * model]
    tail = weights_ref[:, weights_ref.shape[1] - 128 :]
    lane = lax.broadcasted_iota(jnp.int32, (rows, 128), 1)
    bias_lane = 2 * model + width - (weights_ref.shape[1] - 128)
    ones = jnp.where(jnp.logical_or(lane == bias_lane, lane == bias_lane + 1), 1.0, 0.0).astype(BF)
    value = product(normed_ref[...], expand, 1, 1) + product(ones, tail, 1, 1)
    active, slope = gelu_parts(value)
    forward[...] += product(active.astype(BF), reduce)
    grad_mlp = cotangent_ref[...].astype(BF)
    grad = (product(grad_mlp, reduce, 1, 1) * slope).astype(BF)
    backward[...] += product(grad, expand)

    @pl.when(step == pl.num_programs(0) - 1)
    def _():
        resid = resid_ref[...]
        shown_ref[:, model:] = (resid + forward[...] + vectors_ref[1:2, :]).astype(BF)
        xhat, inverse = norm_parts(resid)
        grad = backward[...]
        grad_resid = cotangent_ref[...] + norm_pull(grad, vectors_ref[2:3, :], xhat, inverse)
        grad_ref[...] = grad_resid
        attn = grad_resid.astype(BF)
        shown_ref[:, :model] = attn
        sums_ref[...] = jnp.concatenate(
            [
                jnp.sum(grad * xhat, axis=0, keepdims=True),
                jnp.sum(grad, axis=0, keepdims=True),
                jnp.sum(attn.astype(F32), axis=0, keepdims=True),
                jnp.zeros((5, model), F32),
            ],
            axis=0,
        )
        for j in range(mps):
            part = across_of(across_ref, j, mps, width)
            grad_heads_refs[j][...] = product(attn, part).astype(BF)


def middle(weights, resid, normed, cotangent, vectors, mps, width):
    rows, model = resid.shape
    wide = weights.shape[1] % 256 + 256 if weights.shape[1] % 256 else 256
    chunk = 1024
    vmem = pl.BlockSpec(memory_space=pltpu.VMEM)
    return pl.pallas_call(
        functools.partial(middle_kernel, mps, width),
        grid=(weights.shape[0] // chunk,),
        in_specs=[
            pl.BlockSpec((chunk, weights.shape[1]), lambda i: (i, 0)),
            pl.BlockSpec((weights.shape[0], wide), lambda i: (0, weights.shape[1] // wide - 1)),
        ]
        + [vmem] * 4,
        out_specs=[vmem] * (3 + mps),
        out_shape=[
            jax.ShapeDtypeStruct((rows, 2 * model), BF),
            jax.ShapeDtypeStruct((rows, model), F32),
            jax.ShapeDtypeStruct((8, model), F32),
        ]
        + [jax.ShapeDtypeStruct((rows, width), BF)] * mps,
        scratch_shapes=[pltpu.VMEM((rows, model), F32)] * 2,
        compiler_params=pltpu.CompilerParams(vmem_limit_bytes=VMEM_LIMIT),
        cost_estimate=SMALL,
        name="middle",
    )(weights, weights, resid, normed, cotangent, vectors)


def feed_kernel(chunk, places_ref, expand_ref, reduce_ref, bias_ref, grad_ref, *refs):
    normed_refs, refs = refs[:-7], refs[-7:]
    mine_out, other_out, bias_out, normed, normed_turned, held, second_held = refs
    rows = normed_refs[0].shape[0]
    for j, ref in enumerate(normed_refs):
        normed[j * rows : (j + 1) * rows, :] = ref[...]
    normed_turned[...] = normed[...].T
    hidden = expand_ref.shape[1]
    for start in range(0, hidden, chunk):
        here = slice(start, start + chunk)
        value = product(normed[...], expand_ref[:, here]) + bias_ref[:, here]
        active, slope = gelu_parts(value)
        grad = product(grad_ref[...], reduce_ref[here, :], 1, 1) * slope
        low = grad.astype(BF)
        second_held[here, :] = product(active.astype(BF), grad_ref[...], 0, 0)
        held[:, here] = product(normed_turned[...], low)
        bias_out[:, here] = jnp.sum(low.astype(F32), axis=0, keepdims=True)
    core_rows(held, places_ref[1], mine_out, other_out)
    core_rows(second_held, places_ref[1], mine_out, other_out, held.shape[0] // 2)


def feed(places, expand, reduce, bias, grad, normed_blocks):
    model, hidden = expand.shape
    rows = grad.shape[0]
    vmem = pl.BlockSpec(memory_space=pltpu.VMEM)
    half = (model + hidden) // 2
    return pl.pallas_call(
        functools.partial(feed_kernel, 256),
        in_specs=[pl.BlockSpec(memory_space=pltpu.SMEM)] + [vmem] * (4 + len(normed_blocks)),
        out_shape=[
            jax.ShapeDtypeStruct((half, model), BF),
            jax.ShapeDtypeStruct((half, model), BF),
            jax.ShapeDtypeStruct((1, hidden), F32),
        ],
        scratch_shapes=[
            pltpu.VMEM((rows, model), BF),
            pltpu.VMEM((model, rows), BF),
            pltpu.VMEM((model, hidden), F32),
            pltpu.VMEM((hidden, model), F32),
        ],
        compiler_params=pltpu.CompilerParams(vmem_limit_bytes=VMEM_LIMIT),
        cost_estimate=SMALL,
        name="feed",
    )(places, expand, reduce, bias, grad, *normed_blocks)


def project_kernel(places_ref, packed_ref, normed_ref, attended_ref, attn_ref, *refs):
    mine_out, other_out, held = refs
    wide = packed_ref.shape[1]
    held[:wide, :] = product(packed_ref[...], normed_ref[...], 0, 0)
    held[wide:, :] = product(attended_ref[...], attn_ref[...], 0, 0)
    core_rows(held, places_ref[1], mine_out, other_out)


def project_weights(places, packed, normed, attended, shown):
    frames, wide = packed.shape
    width, model = attended.shape[1], normed.shape[1]
    vmem = pl.BlockSpec(memory_space=pltpu.VMEM)
    half = (wide + width) // 2
    return pl.pallas_call(
        project_kernel,
        grid=(1,),
        in_specs=[pl.BlockSpec(memory_space=pltpu.SMEM)]
        + [vmem] * 3
        + [pl.BlockSpec((frames, model), lambda i: (0, 0))],
        out_specs=[vmem, vmem],
        out_shape=[jax.ShapeDtypeStruct((half, model), BF)] * 2,
        scratch_shapes=[pltpu.VMEM((wide + width, model), F32)],
        compiler_params=pltpu.CompilerParams(vmem_limit_bytes=VMEM_LIMIT),
        cost_estimate=SMALL,
        name="project_weights",
    )(places, packed, normed, attended, shown)


def pieces_kernel(places_ref, feed_ref, feed_got_ref, project_ref, project_got_ref, *outs):
    part = project_ref.shape[0] // 4
    pairs = (
        (feed_ref, feed_got_ref, 0),
        (feed_ref, feed_got_ref, 4 * part),
        (project_ref, project_got_ref, 0),
    )
    for d, out in enumerate(outs):
        for which, (mine, got, start) in enumerate(pairs):
            place = start + jnp.bitwise_xor(places_ref[3], d) * part
            here = pl.ds(pl.multiple_of(place, part), part)
            value = mine[here, :].astype(F32) + got[here, :].astype(F32)
            out[which * part : (which + 1) * part, :] = value.astype(out.dtype)


def pieces(places, feed_mine, feed_got, project_mine, project_got):
    vmem = pl.BlockSpec(memory_space=pltpu.VMEM)
    model = feed_mine.shape[1]
    part = 3 * project_mine.shape[0] // 4
    return pl.pallas_call(
        pieces_kernel,
        in_specs=[pl.BlockSpec(memory_space=pltpu.SMEM)] + [vmem] * 4,
        out_shape=[jax.ShapeDtypeStruct((part, model), BF)]
        + [jax.ShapeDtypeStruct((part, model), BF)] * 3,
        compiler_params=pltpu.CompilerParams(vmem_limit_bytes=VMEM_LIMIT),
        cost_estimate=SMALL,
        name="pieces",
    )(places, feed_mine, feed_got, project_mine, project_got)


def pack_kernel(place_ref, query_ref, pair_ref, core_ref, other_ref, weight_ref, *outs):
    packed_out, sums_out, own_out, *others_out = outs
    pair = pair_ref[...].astype(F32) + core_ref[0].astype(F32) + other_ref[...].astype(F32)
    packed = jnp.concatenate([query_ref[...], pair.astype(BF)], axis=1)
    packed_out[...] = packed
    sums_out[...] = jnp.sum(packed.astype(F32), axis=0, keepdims=True)
    rows = own_out.shape[0]
    mps = len(others_out) + 1

    def part(j):
        start = pl.multiple_of(lax.rem(place_ref[0] + j, mps) * rows, rows)
        return product(packed_out[pl.ds(start, rows), :], weight_ref[...])

    own_out[...] = part(0)
    for j in range(1, mps):
        others_out[j - 1][...] = part(j).astype(BF)


def pack(place, query, pair, pair_core, pair_far, weight, mps):
    frames, width = query.shape
    model, rows = weight.shape[1], frames // mps
    vmem = pl.BlockSpec(memory_space=pltpu.VMEM)
    return pl.pallas_call(
        pack_kernel,
        grid=(1,),
        in_specs=[
            pl.BlockSpec(memory_space=pltpu.SMEM),
            vmem,
            vmem,
            pl.BlockSpec((1, frames, 2 * width), lambda i: (0, 0, 0)),
            vmem,
            vmem,
        ],
        out_specs=[vmem] * (2 + mps),
        out_shape=[
            jax.ShapeDtypeStruct((frames, 3 * width), BF),
            jax.ShapeDtypeStruct((1, 3 * width), F32),
            jax.ShapeDtypeStruct((rows, model), F32),
        ]
        + [jax.ShapeDtypeStruct((rows, model), BF)] * (mps - 1),
        compiler_params=pltpu.CompilerParams(vmem_limit_bytes=VMEM_LIMIT),
        cost_estimate=SMALL,
        name="pack",
    )(place, query, pair, pair_core, pair_far, weight)


def pull_kernel(resid_ref, grad_ref, stem_ref, gain_ref, sums_ref, *refs):
    got_refs, out_ref = refs[:-1], refs[-1]
    rows, model = resid_ref.shape
    grad = got_refs[0][...].astype(F32)
    for ref in got_refs[1:]:
        grad = grad + ref[...].astype(F32)
    xhat, inverse = norm_parts(resid_ref[...])
    grad_resid = grad_ref[...] + norm_pull(grad, gain_ref[...], xhat, inverse)
    _, slope = gelu_parts(stem_ref[...])
    low = (grad_resid * slope).astype(BF)
    out_ref[:rows, :] = low
    sums = jnp.concatenate(
        [
            jnp.sum(grad * xhat, axis=0, keepdims=True),
            jnp.sum(grad, axis=0, keepdims=True),
            sums_ref[0:3, :],
            jnp.sum(low.astype(F32), axis=0, keepdims=True),
            jnp.zeros((10, model), F32),
        ],
        axis=0,
    )
    out_ref[rows:, :] = sums.astype(BF)


def pull(resid, grad, stem, gain, sums, got):
    rows, model = resid.shape
    return pl.pallas_call(
        pull_kernel,
        out_shape=jax.ShapeDtypeStruct((rows + 16, model), BF),
        compiler_params=pltpu.CompilerParams(vmem_limit_bytes=VMEM_LIMIT),
        cost_estimate=SMALL,
        name="pull",
    )(resid, grad, stem, gain, sums, *got)


def second_kernel_body(mps, places_ref, taps_ref, gathered_ref, *refs):
    grad_out, sums_out, mine_out, other_out, held = refs
    rows = gathered_ref.shape[0] // mps
    own = rows - 16
    sums = 0.0
    for j in range(mps):
        grad_out[j * own : (j + 1) * own, :] = gathered_ref[j * rows : j * rows + own, :]
        sums = sums + gathered_ref[j * rows + own : (j + 1) * rows, :].astype(F32)
    sums_out[...] = sums
    held[...] = product(taps_ref[...], grad_out[...], 0, 0)
    core_rows(held, places_ref[1], mine_out, other_out)


def second_weight(places, taps, gathered, mps):
    frames, tall = taps.shape
    model = gathered.shape[1]
    vmem = pl.BlockSpec(memory_space=pltpu.VMEM)
    return pl.pallas_call(
        functools.partial(second_kernel_body, mps),
        in_specs=[pl.BlockSpec(memory_space=pltpu.SMEM)] + [vmem] * 2,
        out_shape=[
            jax.ShapeDtypeStruct((frames, model), BF),
            jax.ShapeDtypeStruct((16, model), F32),
            jax.ShapeDtypeStruct((tall // 2, model), F32),
            jax.ShapeDtypeStruct((tall // 2, model), BF),
        ],
        scratch_shapes=[pltpu.VMEM((tall, model), F32)],
        compiler_params=pltpu.CompilerParams(vmem_limit_bytes=VMEM_LIMIT),
        cost_estimate=SMALL,
        name="second_weight",
    )(places, taps, gathered)


def stem_back_kernel(
    bands,
    places_ref,
    grad_ref,
    edges_ref,
    matrix_ref,
    even_ref,
    odd_ref,
    rim_ref,
    window_ref,
    back_ref,
    sums_ref,
    reduce_ref,
    expand_ref,
    project_ref,
    mine_out,
    other_out,
    spectrum_out,
    held,
    small,
):
    frames = grad_ref.shape[0]
    width = even_ref.shape[1]
    row = lax.broadcasted_iota(jnp.int32, (frames, width), 0)

    def later(value, last):
        return jnp.where(row == frames - 1, last, pltpu.roll(value, frames - 1, 0))

    def earlier(value, start):
        return jnp.where(row == 0, start, pltpu.roll(value, 1, 0))

    def slope(value):
        return gelu_parts(value)[1]

    def rounded(value):
        return value.astype(BF).astype(F32)

    taps = product(grad_ref[...], matrix_ref[...], 1, 1)
    rims = product(edges_ref[...], matrix_ref[...], 1, 1)
    even = rounded(taps[:, width : 2 * width] * slope(even_ref[...]))
    odd = taps[:, 2 * width :] + later(taps[:, :width], rims[1:2, :width])
    odd = rounded(odd * slope(odd_ref[...]))
    rim_slope = slope(rim_ref[...])
    inside = (places_ref[2] > 0).astype(F32)
    odd_before = rounded((rims[0:1, 2 * width :] + taps[0:1, :width]) * rim_slope[0:1] * inside)
    even_after = rounded(rims[1:2, width : 2 * width] * rim_slope[1:2])
    bias = jnp.sum(even + odd, axis=0, keepdims=True)
    both = jnp.concatenate([even, odd], axis=1).astype(BF)
    weight = product(window_ref[...], both, 0, 0)
    weight = weight[: 3 * bands, :width] + weight[bands:, width:]
    spare = held.shape[1] - 3 * width
    held[:bands, :] = jnp.concatenate(
        [weight[k * bands : (k + 1) * bands] for k in range(3)] + [jnp.zeros((bands, spare), F32)],
        axis=1,
    )
    last = jnp.concatenate(
        [project_ref[:, :width], project_ref[:, 2 * width :], bias, jnp.zeros((1, spare), F32)],
        axis=1,
    )
    blank = jnp.zeros((held.shape[0] - bands - 9, held.shape[1]), F32)
    held[bands:, :] = jnp.concatenate(
        [sums_ref[0:6, :], reduce_ref[...], expand_ref[...], last, blank], axis=0
    )
    few = small.shape[1]
    for p in range(8):
        small[p] = held[p * few : (p + 1) * few, :]
    filled = jnp.zeros((other_out.shape[1] - few, held.shape[1]), F32)
    for quarter in range(4):
        mine_out[quarter] = small[2 * quarter + places_ref[1]]
        other = small[2 * quarter + 1 - places_ref[1]]
        other_out[quarter] = jnp.concatenate([other, filled], axis=0).astype(BF)
    before = earlier(odd, odd_before).astype(BF)
    following = later(even, even_after).astype(BF)
    even, odd = even.astype(BF), odd.astype(BF)
    back = [back_ref[k * width : (k + 1) * width, :] for k in range(3)]
    spectrum = [
        product(before, back[0]) + product(even, back[1]) + product(odd, back[2]),
        product(even, back[0]) + product(odd, back[1]) + product(following, back[2]),
    ]
    spectrum_out[...] = jnp.concatenate(spectrum, axis=1).astype(BF)


def stem_back(places, grad, edges, matrix, even, odd, rim, window, back_matrix, *sums):
    frames, width = even.shape
    bands, model = back_matrix.shape[1], grad.shape[1]
    vmem = pl.BlockSpec(memory_space=pltpu.VMEM)
    return pl.pallas_call(
        functools.partial(stem_back_kernel, bands),
        in_specs=[pl.BlockSpec(memory_space=pltpu.SMEM)] + [vmem] * (8 + len(sums)),
        out_shape=[
            jax.ShapeDtypeStruct((4, (bands + 16) // 8, model), F32),
            jax.ShapeDtypeStruct((4, 16, model), BF),
            jax.ShapeDtypeStruct((frames, 2 * bands), BF),
        ],
        scratch_shapes=[
            pltpu.VMEM((bands + 16, model), F32),
            pltpu.VMEM((8, (bands + 16) // 8, model), F32),
        ],
        compiler_params=pltpu.CompilerParams(vmem_limit_bytes=VMEM_LIMIT),
        cost_estimate=SMALL,
        name="stem_back",
    )(places, grad, edges, matrix, even, odd, rim, window, back_matrix, *sums)


def on_device(
    spectrogram,
    first_kernel,
    first_bias,
    second_kernel,
    second_bias,
    attend_gain,
    attend_shift,
    project_weight,
    project_bias,
    output_weight,
    output_bias,
    mixer_gain,
    mixer_shift,
    expand_weight,
    expand_bias,
    reduce_weight,
    reduce_bias,
    cotangent,
):
    _, steps, bands = spectrogram.shape
    frames = steps // 2
    width = first_kernel.shape[2]
    model = second_kernel.shape[2]
    hidden = expand_weight.shape[1]
    mps, seqs = lax.axis_size("mp"), lax.axis_size("seq")
    z, seq = lax.axis_index("mp"), lax.axis_index("seq")
    core = lax.rem(seq, 2)
    rows = frames // mps

    held = hold(
        (2 * plane_index() + core).reshape(1),
        expand_weight,
        reduce_weight,
        output_weight,
        expand_bias,
        hidden // 8,
    )
    weights_got = gather_mp(held, "weights_mp")

    paired = spectrogram.reshape(frames, 2 * bands)
    before = passed_along(paired[-1:], 1)
    following = passed_along(paired[:1], -1)
    ahead = jnp.concatenate([before, paired, following], axis=0)
    window = jnp.concatenate(
        [ahead[:-2, bands:], ahead[1:-1], ahead[2:, :bands]], axis=1
    )
    prior = jnp.concatenate([before, paired[:1, :bands]], axis=1)
    latter = jnp.concatenate([paired[-1:, bands:], following], axis=1)
    first_matrix = first_kernel.reshape(3 * bands, width)
    even_in = jnp.concatenate([window[:, : 3 * bands], latter], axis=0)
    odd_in = jnp.concatenate([prior, window[:, bands:]], axis=0)
    pre_even = product(even_in, first_matrix) + first_bias
    pre_odd = product(odd_in, first_matrix) + first_bias
    inside = jnp.logical_or(jnp.arange(frames + 1) > 0, seq > 0)[:, None]
    hidden_even = exact_gelu(pre_even[:frames]).astype(BF)
    hidden_odd = jnp.where(inside, exact_gelu(pre_odd), 0.0).astype(BF)
    taps = jnp.concatenate([hidden_odd[:frames], hidden_even, hidden_odd[1:]], axis=1)
    second_matrix = second_kernel.reshape(3 * width, model)
    stem_part = product(taps, second_matrix)
    own_cotangent = rolled_blocks(cotangent.reshape(frames, model))
    early = (
        own_cotangent[0],
        jnp.concatenate(own_cotangent, axis=0).astype(BF),
        jnp.stack([output_bias, reduce_bias, mixer_gain, mixer_shift]),
        column_total(cotangent.reshape(frames, model).astype(BF))[None],
        jnp.transpose(first_kernel[::-1], (0, 2, 1)).reshape(3 * width, bands),
        jnp.concatenate([pre_odd[:1], pre_even[frames:], jnp.zeros((6, width), F32)], axis=0),
        pre_even[:frames],
        pre_odd[1:],
        window,
        taps,
        sinusoid(seq * frames + z * rows, rows, model),
        jnp.stack([z, core, seq, plane_index()]),
        z.reshape(1),
        attend_gain.reshape(1, model),
        expand_bias.reshape(1, hidden),
    )
    stem_part, weights_got, early = lax.optimization_barrier((stem_part, weights_got, early))
    own_cotangent, grad_mlp, vectors, reduce_bias_part, back_matrix = early[:5]
    rim, even_level, odd_level, window, taps, table = early[5:11]
    places, place, attend_gain_row, expand_bias_row = early[11:]
    with jax.named_scope("weights_plane"):
        weights_all = plane_gather(jnp.concatenate(weights_got, axis=0))
    stem_pre = scatter_sum(rolled_blocks(stem_part), "stem_sum") + second_bias
    resid_zero = exact_gelu(stem_pre) + table
    normed_one = lax.all_gather(
        layer_norm(resid_zero, attend_gain, attend_shift).astype(BF), "mp", axis=0, tiled=True
    )

    project_matrix = project_weight.transpose(1, 2, 0).reshape(3 * width, model)
    offsets = jnp.concatenate([project_bias[0], jnp.zeros_like(project_bias[0]), project_bias[1]])
    packed = (product(normed_one, project_matrix, 1, 1) + offsets).astype(BF)
    query, pair = packed[:, :width], packed[:, width:]
    pair_far = swapped(pair, "seq", 2, "pair_far")
    pair_core = swapped(pair, "seq", 1, "pair_core")
    pair_far, query = lax.optimization_barrier((pair_far, query))
    pair_far_core = swapped(pair_far, "seq", 1, "pair_far_core")
    pairs = [pair, pair_core, pair_far, pair_far_core]
    attended, attended_turned, level, *attended_blocks = attend(place, query, pairs, mps)
    heads_got = exchange_mp(attended_blocks, "attended")
    resid_one, normed_two_own = join(weights_all, heads_got, resid_zero, vectors)
    normed_two_all = gather_mp(normed_two_own, "normed_two")
    shown_own, grad_resid_one, middle_sums, *grad_heads = middle(
        weights_all,
        resid_one,
        normed_two_own,
        own_cotangent,
        vectors,
        mps,
        width,
    )
    shown = lax.all_gather(shown_own, "mp", axis=0, tiled=True)
    rows_got = exchange_mp(grad_heads, "grad_heads")
    grad_attended = natural([rows_got[-j % mps] for j in range(mps)])
    grad_attended, normed_two_all = lax.optimization_barrier((grad_attended, normed_two_all))

    query_grad, near, far, cores = attend_back(
        place,
        query,
        attended_turned,
        level,
        pairs,
        [grad_attended],
    )
    cores_got = swapped(cores, "seq", 1, "grad_core")
    far = (far.astype(F32) + cores_got[1].astype(F32)).astype(BF)
    far_got = swapped(far, "seq", 2, "grad_far")
    feed_mine, feed_other, expand_bias_part = feed(
        places,
        expand_weight,
        reduce_weight,
        expand_bias_row,
        after(grad_mlp, far),
        normed_two_all,
    )
    far_got, feed_other = lax.optimization_barrier((far_got, feed_other))
    feed_got = swapped(feed_other, "seq", 1, "feed_core")
    grad_packed, project_columns, *normed_parts = pack(
        place, query_grad, near, cores_got, far_got, project_matrix, mps
    )
    normed_got = exchange_mp(normed_parts, "grad_normed_one")

    project_mine, project_other = project_weights(places, grad_packed, normed_one, attended, shown)
    project_got = swapped(project_other, "seq", 1, "project_core")
    wide_pieces = pieces(places, feed_mine, feed_got, project_mine, project_got)
    normed_got, wide_pieces = lax.optimization_barrier((normed_got, wide_pieces))
    wide_parts = [
        plane_move(piece, d, "wide_scatter") for d, piece in zip((1, 2, 3), wide_pieces[1:])
    ]

    grad_stem_own = pull(
        resid_zero, grad_resid_one, stem_pre, attend_gain_row, middle_sums, normed_got
    )
    with jax.named_scope("grad_stem"):
        gathered = lax.all_gather(grad_stem_own, "mp", axis=0, tiled=True)
    gathered, wide_parts = lax.optimization_barrier((gathered, wide_parts))
    with jax.named_scope("wide_gather"):
        wide_all = plane_gather(rest_of_dp(total([wide_pieces[0]] + wide_parts).astype(BF)))
    last_row = (mps - 1) * (rows + 16) + rows - 1
    stem_before = passed_along(gathered[last_row : last_row + 1], 1)
    stem_following = passed_along(gathered[:1], -1)
    grad_stem, small, second_mine, second_other = second_weight(places, taps, gathered, mps)
    second_got = swapped(second_other, "seq", 1, "second_core")
    edges = jnp.concatenate([stem_before, stem_following, jnp.zeros((14, model), BF)], axis=0)
    loose_mine, loose_other, spectrum_part = stem_back(
        places,
        grad_stem,
        edges,
        second_matrix,
        even_level,
        odd_level,
        rim,
        window,
        back_matrix,
        small,
        reduce_bias_part,
        expand_bias_part,
        project_columns,
    )
    loose_got = swapped(loose_other, "seq", 1, "small_core")[:, : (bands + 16) // 8]

    joined = jnp.concatenate(
        [
            (second_mine + second_got.astype(F32)).reshape(4, -1, model),
            loose_mine + loose_got.astype(F32),
        ],
        axis=1,
    )
    spectrum_parts = gather_mp(spectrum_part, "spectrum")
    joined, shown = lax.optimization_barrier((joined, shown))
    piece = plane_scatter(joined, "last_scatter")
    encoded = shown[:, model:].astype(F32)
    piece, encoded = lax.optimization_barrier((piece, encoded))
    with jax.named_scope("last_gather"):
        last = plane_gather(piece[None])
    last, spectrum_parts, wide_all = lax.optimization_barrier((last, spectrum_parts, wide_all))
    rows_of = (model, model, model, model, model, model, model, hidden)
    cuts = tuple((row, 0, size) for row, size in enumerate(rows_of))
    cuts += ((8, 0, 2 * width), (8, 2 * width, 3 * width))
    expand_sum, reduce_sum, project_sum, output_sum, spectrum, second_sum, first_sum, *sums = end(
        place, wide_all, last, spectrum_parts, bands, bands + 16, width, cuts
    )
    spectrogram_gradient = spectrum.reshape(1, steps, bands)
    return (
        encoded.reshape(1, frames, model),
        spectrogram_gradient,
        first_sum.reshape(3, bands, width),
        sums[9],
        second_sum.reshape(3, width, model),
        sums[5],
        sums[0],
        sums[1],
        project_sum.T.reshape(model, 3, width),
        sums[8],
        output_sum,
        sums[4],
        sums[2],
        sums[3],
        expand_sum,
        sums[7],
        reduce_sum,
        sums[6],
    )


def solution(mesh):
    return jax.shard_map(
        on_device,
        mesh=mesh,
        in_specs=(
            P("dp", "seq", None),
            P(None, None, "mp"),
            P("mp"),
            P(None, "mp", None),
            P(),
            P(),
            P(),
            P(None, None, "mp"),
            P(None, "mp"),
            P("mp", None),
            P(),
            P(),
            P(),
            P(None, "mp"),
            P("mp"),
            P("mp", None),
            P(),
            P("dp", "seq", None),
        ),
        out_specs=(
            P("dp", "seq", None),
            P("dp", "seq", None),
            P(None, None, "mp"),
            P("mp"),
            P(None, "mp", None),
            P(),
            P(),
            P(),
            P(None, None, "mp"),
            P(None, "mp"),
            P("mp", None),
            P(),
            P(),
            P(),
            P(None, "mp"),
            P("mp"),
            P("mp", None),
            P(),
        ),
        check_vma=False,
    )
```
